256 devices in a mesh: dp: 32 (over z, y_hi, core), tensor: 8 (over y_lo, x).
Axes of the slice: x: 4, y: 4 (y_hi: 2, y_lo: 2; y = y_hi * 2 + y_lo), z: 8, core: 2. Of those that a mesh axis runs over, the one named last changes fastest.
Arguments:
- glu_input: bfloat16 [4096, 2, 3, 1024], P('dp', None, None, 'tensor'), may hold values from -6 to 6
- conv_kernel: bfloat16 [32, 3, 1024], P(None, None, 'tensor'), may hold values from -1 to 1
- norm_gain: float32 [3, 1024], P(None, 'tensor'), may hold values from 0.5 to 2
- norm_shift: float32 [3, 1024], P(None, 'tensor'), may hold values from -3 to 3
- out_weight: bfloat16 [3, 1024, 3, 1024], P(None, 'tensor'), may hold values from -0.109375 to 0.109375
- out_cotangent: bfloat16 [4096, 3, 1024], P('dp'), may hold values from -6 to 6
- root_stack: bfloat16 [16, 2, 1024, 1024], P('tensor', None, 'dp'), as said below
- home: int32 [9], replicated, may hold values from 0 to 15, as said below
Outputs:
- glu_grad: bfloat16 [4096, 2, 3, 1024], P('dp', None, None, 'tensor')
- kernel_grad: float32 [32, 3, 1024], P(None, None, 'tensor')
- update: bfloat16 [3, 1024, 3, 1024], P(None, 'tensor')
The draws below stay inside these ranges and needn't reach their ends.
Inputs may be any that keep to these rules, and one draw needn't show every extreme that they name: Distinct entries; tensor index home // 2 owns block b. An owner holds at most 2 blocks, and in every draw one owner holds exactly 2. `root_stack`: each of the two matrices in a slot is symmetric.
All inputs are finite; a program needn't handle non-finite values.
Results may differ from the reference program's by a relative error of at most 0.0057.
Values may be sent and summed in bfloat16 or wider, within the bound.
A program may use at most 128 MiB of HBM per device.

```python
import math
import jax
import jax.numpy as jnp
from jax import lax

C = 3072
KERNEL = 32
BLOCK = 1024
LEN = 2048
NB = 3
NBLK = 9
OWNERS = 8
SLOTS = 2
TOKENS = 4096
UTTS = 2


def draw_root_stack(key, part):
    key = jax.random.fold_in(key, 11)
    key_off, key_diag = jax.random.split(key)
    shape = (OWNERS * SLOTS, 2, BLOCK, BLOCK)
    raw = jax.random.normal(key_off, shape, jnp.float32)
    diag_vals = jnp.exp(jax.random.uniform(key_diag, shape[:-1], jnp.float32, -0.6931, 0.6931))
    symmetric = (raw + jnp.swapaxes(raw, -1, -2)) * 0.5 ** 0.5 * 0.02
    identity = (jnp.arange(BLOCK)[:, None] == jnp.arange(BLOCK)[None, :]).astype(jnp.float32)
    matrix = 0.4 * (symmetric * (1.0 - identity) + identity * diag_vals[..., None, :])
    return matrix.astype(jnp.bfloat16)


def draw_home(key, part):
    key = jax.random.fold_in(key, 7)
    key_owner, key_mid, key_order = jax.random.split(key, 3)
    full_owner = jax.random.randint(key_owner, (), 0, OWNERS)
    full_slots = full_owner * SLOTS + jnp.arange(SLOTS, dtype=jnp.int32)
    indices = jnp.arange((OWNERS - 1) * SLOTS, dtype=jnp.int32)
    others = indices + SLOTS * (indices >= full_owner * SLOTS).astype(jnp.int32)
    middle = jax.random.permutation(key_mid, others[1:-1])
    picked = jnp.concatenate([others[:1], others[-1:], middle[:NBLK - SLOTS - 2]])
    placed = jnp.concatenate([full_slots, picked])
    return jax.random.permutation(key_order, placed).astype(jnp.int32)


def with_spikes(array, own_key, source, target, blocks, factor):
    def block_of(axis_at):
        return (jnp.arange(array.shape[axis_at]) // (array.shape[axis_at] // blocks)).reshape((-1,) + (1,) * (array.ndim - 1 - axis_at))

    near = jax.random.permutation(own_key, blocks)[block_of(target)]
    second = (block_of(target) + blocks // 2) % blocks
    return jnp.where((block_of(source) == near) | (block_of(source) == second), factor * array, array)


def level_of(stream_key, extent, shards, least, high):
    def one(axis_at, parts):
        steps = jax.random.uniform(jax.random.fold_in(jax.random.fold_in(stream_key, 6), axis_at), (parts,), jnp.float32, least / len(shards), high / len(shards))
        return jnp.repeat(jnp.exp(steps), extent[axis_at] // parts).reshape((-1,) + (1,) * (len(extent) - axis_at - 1))

    level = one(*shards[0])
    for cut in shards[1:]:
        level = level * one(*cut)
    return level


def gaussian(key, dims, spread, limit, pieces=(), held_as=jnp.bfloat16):
    array = jax.random.normal(key, dims, jnp.float32) * spread
    if len(pieces) > 0:
        array = level_of(key, dims, pieces, -0.22, 0.18) * array
    return jnp.clip(array, min=-limit, max=limit).astype(held_as)


def heavy_noise(stream_key, shape, deviation, most, cuts, heavy, kind=jnp.bfloat16):
    entries = deviation * jax.random.normal(stream_key, shape, jnp.float32)
    if cuts:
        entries = entries * level_of(stream_key, shape, cuts, -0.22, 0.18)
    return jnp.clip(with_spikes(entries, jax.random.fold_in(stream_key, 3), *heavy), -most, most).astype(kind)


def setup_inputs(seed: int = 0) -> dict:
    key_of = jax.random.split(jax.random.key(seed), 9)
    glu_input = gaussian(key_of[0], (TOKENS, 2, NB, BLOCK), 1.0, 6.0, ((0, 32), (3, 8)))
    conv_kernel = gaussian(key_of[1], (KERNEL, NB, BLOCK), KERNEL ** -0.5, 1.0, ((2, 8),))
    norm_gain = jnp.clip(jnp.exp(math.log(2.0) - 1.3862944 * jax.random.uniform(key_of[2], (NB, BLOCK), jnp.float32) ** level_of(key_of[2], (NB, BLOCK), ((1, 8),), -0.2, 0.2)), 0.5, 2.0)
    norm_shift = gaussian(key_of[3], (NB, BLOCK), 0.5, 3.0, ((1, 8),), jnp.float32)
    out_weight = gaussian(key_of[4], (NB, BLOCK, NB, BLOCK), C ** -0.5, 0.109375, ((1, 8),))
    out_cotangent = heavy_noise(key_of[5], (TOKENS, NB, BLOCK), 1.0, 6.0, ((0, 32),), (0, 2, 32, 2.75))
    root_stack = draw_root_stack(jax.random.fold_in(key_of[8], 71), 0)
    home = draw_home(jax.random.fold_in(key_of[8], 71), 0)
    return {"glu_input": glu_input, "conv_kernel": conv_kernel, "norm_gain": norm_gain, "norm_shift": norm_shift, "out_weight": out_weight, "out_cotangent": out_cotangent, "root_stack": root_stack, "home": home}


def reference(glu_input, conv_kernel, norm_gain, norm_shift, out_weight, out_cotangent, root_stack, home):
    half_kernel = KERNEL // 2
    lin_half = glu_input[:, 0].astype(jnp.float32)
    gate_half = glu_input[:, 1].astype(jnp.float32)
    gate_sig = jax.nn.sigmoid(gate_half)
    glu_out = (lin_half * gate_sig).astype(jnp.bfloat16)
    own_utt = (jnp.arange(TOKENS, dtype=jnp.int32) + LEN // 2) // LEN
    ext_utt = (jnp.arange(TOKENS + KERNEL, dtype=jnp.int32) - half_kernel + LEN // 2) // LEN
    padded = jnp.pad(glu_out.astype(jnp.float32), ((half_kernel, half_kernel), (0, 0), (0, 0)))
    kernel_f = conv_kernel.astype(jnp.float32)
    conv_out = jnp.zeros((TOKENS, NB, BLOCK), jnp.float32)
    for tap_index in range(KERNEL):
        same_utt = (ext_utt[tap_index:tap_index + TOKENS] == own_utt).astype(jnp.float32)
        conv_out = conv_out + kernel_f[tap_index] * padded[tap_index:tap_index + TOKENS] * same_utt[:, None, None]
    normed = conv_out * norm_gain + norm_shift
    norm_sig = jax.nn.sigmoid(normed)
    activated = (normed * norm_sig).astype(jnp.bfloat16)
    act_grad = jnp.dot(out_cotangent.reshape(TOKENS, C), out_weight.reshape(C, C).T, preferred_element_type=jnp.float32)
    act_grad = act_grad.reshape(TOKENS, NB, BLOCK)
    conv_grad = (act_grad * norm_sig * (1.0 + normed * (1.0 - norm_sig)) * norm_gain).astype(jnp.bfloat16)
    grad_f = conv_grad.astype(jnp.float32)
    grad_pad = jnp.pad(grad_f, ((half_kernel, half_kernel), (0, 0), (0, 0)))
    kernel_terms = []
    input_grad = jnp.zeros((TOKENS, NB, BLOCK), jnp.float32)
    for tap_index in range(KERNEL):
        same_utt = (ext_utt[tap_index:tap_index + TOKENS] == own_utt).astype(jnp.float32)
        kernel_terms.append(jnp.sum(padded[tap_index:tap_index + TOKENS] * same_utt[:, None, None] * grad_f, axis=0))
        back_index = KERNEL - tap_index
        same_back = (ext_utt[back_index:back_index + TOKENS] == own_utt).astype(jnp.float32)
        input_grad = input_grad + kernel_f[tap_index] * grad_pad[back_index:back_index + TOKENS] * same_back[:, None, None]
    kernel_grad = jnp.stack(kernel_terms) / UTTS
    glu_grad = jnp.stack([input_grad * gate_sig, input_grad * lin_half * gate_sig * (1.0 - gate_sig)], axis=1).astype(jnp.bfloat16)
    weight_grad = jnp.dot(activated.reshape(TOKENS, C).T, out_cotangent.reshape(TOKENS, C), preferred_element_type=jnp.float32) / UTTS
    grid = weight_grad.reshape(NB, BLOCK, NB, BLOCK).transpose(0, 2, 1, 3)
    chosen = root_stack[home].astype(jnp.float32).reshape(NB, NB, 2, BLOCK, BLOCK)
    left_product = jnp.einsum("ijab,ijbc->ijac", chosen[:, :, 0], grid, precision=lax.Precision.HIGHEST)
    update = jnp.einsum("ijab,ijbc->ijac", left_product, chosen[:, :, 1], precision=lax.Precision.HIGHEST)
    update = update.transpose(0, 2, 1, 3).astype(jnp.bfloat16)
    return glu_grad, kernel_grad, update
```

```python
import functools

import jax
import jax.numpy as jnp
from jax import lax
from jax.experimental import pallas as pl
from jax.experimental.pallas import tpu as pltpu
from jax.sharding import PartitionSpec as P

LEN = 2048
MESH = pl.DeviceIdType.MESH
BF = jnp.bfloat16
F32 = jnp.float32

Z = 8
QUADS = 4
TENSOR = 8
TAPS = 32
HALF = TAPS // 2
ROWS = 128
BLOCK = 1024
NB = 3
NBLK = 9
COLS = BLOCK // 2
QUART = BLOCK // 4
SHARE = LEN / (ROWS * Z * QUADS)

ORDER = (4, 3, 5, 2, 6, 1, 7, 0)
SPOT = {off: k for k, off in enumerate(ORDER)}
HOPS = ((4, 3), (3, 4))


def dot(a, b, dims):
    return lax.dot_general(a, b, (dims, ((), ())), preferred_element_type=F32)


def keep(dst, at, src, m):
    dst[at] = src[m]


def kernel(
    home, glu, weight_hbm, cot, roots, taps, gain, shift,
    upd, kgrad, igrad,
    tapf, cand, rpick, lpick, rrows, rfull, lfull, lturn,
    halo, cg_halo, gext, normed_s, at_s, cg_b, cgext, weight,
    gsend, gsib, gown, rs_send, rs_recv, e_send, e_recv,
    ysend, yrecv, gfull, wall,
    kpart, kin1, ksend2, kin2, ksum, kz, khalf,
    w_sem, halo_s, halo_r, s1_s, s1_r, r2_s, r2_r, l2_s, l2_r,
    r3_s, r3_r, l3_s, l3_r, gs_s, gs_r, rs_s, rs_r, es_s, es_r,
    y_s, y_r, c_s, c_r, wt_s, wt_r, uy_s, uy_r, uz_s, uz_r, us_s, us_r,
    ez_s, ez_r, ch_s, ch_r, k_s, k_r,
):
    d = lax.axis_index("dp")
    t = lax.axis_index("tensor")
    z = lax.div(d, 4)
    a = lax.rem(d, 4)
    yh = lax.div(a, 2)
    c = lax.rem(a, 2)
    sib = d + 1 - 2 * c
    par = d + 2 - 4 * yh

    def at_z(zz):
        return lax.rem(zz + 2 * Z, Z) * 4 + a

    z_dn, z_up = at_z(z - 1), at_z(z + 1)
    sends = []

    def send(src, dst, ss, rs, dev, when=None, start=True):
        copy = pltpu.make_async_remote_copy(
            src_ref=src, dst_ref=dst, send_sem=ss, recv_sem=rs,
            device_id=dev, device_id_type=MESH,
        )
        if when is None:
            copy.start()
        else:
            pl.when(when)(copy.start)
        sends.append((copy, when))

    def got(dst, rs):
        pltpu.make_async_remote_copy(
            src_ref=dst, dst_ref=dst, send_sem=s1_s.at[0], recv_sem=rs,
            device_id=(sib, t), device_id_type=MESH,
        ).wait_recv()

    barrier = pltpu.get_barrier_semaphore()

    def hello(dev):
        pl.semaphore_signal(barrier, inc=1, device_id=dev, device_id_type=MESH)

    hello((lax.rem(d + 31, 32), t))
    hello((lax.rem(d + 1, 32), t))
    for m in range(1, 4):
        hello((z * 4 + lax.rem(a + m, 4), t))
    for m in range(1, Z):
        hello((at_z(z + m), t))
    for m in range(1, TENSOR):
        hello((d, lax.rem(t + m, TENSOR)))

    r_to = lax.div(z, 2)
    r_slot = lax.rem(z, 2) * 4 + a

    for n in range(Z):
        pl.when(8 * a + n != d)(functools.partial(hello, (8 * a + n, t)))

    w_copy = pltpu.make_async_copy(weight_hbm, weight, w_sem)
    w_copy.start()

    left_ok = (d != 0) & (lax.rem(d * ROWS + LEN // 2, LEN) != 0)
    right_ok = (d != 31) & (lax.rem((d + 1) * ROWS + LEN // 2, LEN) != 0)
    for i in range(NB):
        gext[i, HALF:HALF + ROWS, :] = glu[i].astype(F32)
        tapf[i] = taps[i].astype(F32)

    pl.semaphore_wait(barrier, 2 + 3 + Z - 1 + TENSOR - 1 + Z - jnp.where(r_to == a, 1, 0))

    dn, up = (lax.rem(d + 31, 32), t), (lax.rem(d + 1, 32), t)
    send(glu.at[:, 0:HALF], halo.at[1], halo_s.at[0], halo_r.at[1], dn, left_ok)
    send(glu.at[:, ROWS - HALF:ROWS], halo.at[0], halo_s.at[1], halo_r.at[0], up, right_ok)
    for m in range(1, TENSOR):
        tt = lax.rem(t + m, TENSOR)
        share_cols = pl.ds(pl.multiple_of(tt * ROWS, ROWS), ROWS)
        send(roots.at[:, :, :, share_cols], cand.at[t], s1_s.at[m], s1_r.at[m], (d, tt))
    cand[t] = roots[:, :, :, pl.ds(pl.multiple_of(t * ROWS, ROWS), ROWS)]

    def rim(side, ok, sem, src, dst, rows):
        @pl.when(ok)
        def _():
            got(src.at[side], sem.at[side])
            for i in range(NB):
                dst[i, rows, :] = src[side, i].astype(F32)

        @pl.when(jnp.logical_not(ok))
        def _():
            for i in range(NB):
                dst[i, rows, :] = jnp.zeros((HALF, ROWS), F32)

    low, high = pl.ds(0, HALF), pl.ds(HALF + ROWS, HALF)
    rim(0, left_ok, halo_r, halo, gext, low)
    rim(1, right_ok, halo_r, halo, gext, high)

    def conv(i, carry):
        total = jnp.zeros((ROWS, ROWS), F32)
        for j in range(TAPS):
            total = total + tapf[i, j:j + 1, :] * gext[i, j:j + ROWS, :]
        normed = total * gain[i] + shift[i]
        normed_s[i] = normed
        at_s[i] = (normed * jax.nn.sigmoid(normed)).T.astype(BF)
        return carry

    lax.fori_loop(0, NB, conv, 0)

    own_cols = pl.ds(pl.multiple_of(c * COLS, COLS), COLS)
    sib_cols = pl.ds(pl.multiple_of((1 - c) * COLS, COLS), COLS)
    sequence = (0, 1, 2, 8, 3, 4, 5, 6, 7)
    for k in sequence:
        block = jnp.int32(8) if k == 8 else lax.rem(z + ORDER[k], Z)
        row = lax.div(block, NB)
        col = lax.rem(block, NB)
        left = at_s[row]
        gsend[k] = dot(left, cot[col, :, sib_cols], ((1,), (0,))).astype(BF)
        send(gsend.at[k], gsib.at[k], gs_s.at[k], gs_r.at[k], (sib, t))
        gown[k] = dot(left, cot[col, :, own_cols], ((1,), (0,)))

    home_z = z == 0
    for m in range(1, TENSOR):
        got(cand.at[lax.rem(t + m, TENSOR)], s1_r.at[TENSOR - m])
    r_rows = pl.ds(pl.multiple_of(r_slot * 32, 32), 32)
    for m in range(NBLK):
        x = m // Z
        zz = 0 if x else lax.rem(z + m, Z)
        slot = home[8 if x else zz]
        own, which = lax.shift_right_logical(slot, 1), slot & 1
        lpick[m] = cand[own, which, 0]
        rpick[m] = cand[own, which, 1]
        r_dev = zz * 4 + r_to
        l_dev = zz * 4 + a
        send(rpick.at[m], rrows.at[x, r_rows], r2_s.at[m], r2_r.at[x, r_slot], (r_dev, t), r_dev != d)
        pl.when(r_dev == d)(functools.partial(keep, rrows, (x, r_rows), rpick, m))
        send(lpick.at[m], lfull.at[x, z, a], l2_s.at[m], l2_r.at[x, z], (l_dev, t), l_dev != d)
        pl.when(l_dev == d)(functools.partial(keep, lfull, (x, z, a), lpick, m))

    def pair_sum(k):
        got(gsib.at[k], gs_r.at[k])
        gown[k] = gown[k] + gsib[k].astype(F32)

    def ring_step(s):
        for h, hops in enumerate(HOPS):
            for way in (0, 1):
                if s >= hops[way]:
                    continue
                off = (Z - hops[0] + s) % Z if way == 0 else hops[1] - s
                rows = slice(64 * h, 64 * h + 64)
                total = gown[SPOT[off], rows, :]
                if s > 0:
                    got(rs_recv.at[h, way, s - 1], rs_r.at[h, way, s - 1])
                    total = total + rs_recv[h, way, s - 1].astype(F32)
                rs_send[h, way, s] = total.astype(BF)
                send(
                    rs_send.at[h, way, s], rs_recv.at[h, way, s],
                    rs_s.at[h, way, s], rs_r.at[h, way, s],
                    (z_dn if way == 0 else z_up, t),
                )

    def extra_step_5():
        @pl.when(z == 5)
        def _():
            e_send[...] = gown[8].astype(BF)

        send(e_send, e_recv.at[0], es_s.at[0], es_r.at[0], (6 * 4 + a, t), z == 5)

    def extra_turn(s):
        zz = 5 + s

        @pl.when(z == zz)
        def _():
            got(e_recv.at[0], es_r.at[0])
            e_send[...] = (gown[8] + e_recv[0].astype(F32)).astype(BF)

        land = 1 if zz == 7 else 0
        send(e_send, e_recv.at[land], es_s.at[0], es_r.at[land], (((zz + 1) % Z) * 4 + a, t), z == zz)

    def extra_down(s):
        zz = 4 - s

        @pl.when(z == zz)
        def _():
            total = gown[8]
            if s > 0:
                got(e_recv.at[0], es_r.at[0])
                total = total + e_recv[0].astype(F32)
            e_send[...] = total.astype(BF)

        send(e_send, e_recv.at[0], es_s.at[0], es_r.at[0], ((zz - 1) * 4 + a, t), z == zz)

    for k in (0, 1, 2):
        pair_sum(k)
    ring_step(0)
    pair_sum(8)
    extra_down(0)
    extra_step_5()

    w_copy.wait()
    for i in range(NB):
        grad = jnp.zeros((ROWS, ROWS), F32)
        for j in range(NB):
            grad = grad + dot(cot[j], weight[i, j], ((1,), (1,)))
        normed = normed_s[i]
        sg = jax.nn.sigmoid(normed)
        cg = (grad * sg * (1.0 + normed * (1.0 - sg)) * gain[i]).astype(BF)
        cg_b[i] = cg
        cgext[i, HALF:HALF + ROWS, :] = cg.astype(F32)
    send(cg_b.at[:, 0:HALF], cg_halo.at[1], ch_s.at[0], ch_r.at[1], dn, left_ok)
    send(cg_b.at[:, ROWS - HALF:ROWS], cg_halo.at[0], ch_s.at[1], ch_r.at[0], up, right_ok)

    for k in (3, 4):
        pair_sum(k)
    ring_step(1)
    extra_down(1)
    extra_turn(1)

    def tap_grad(i, carry):
        cg = cgext[i, HALF:HALF + ROWS, :]
        for j in range(TAPS):
            terms = (cg * gext[i, j:j + ROWS, :]).reshape(ROWS // 8, 8, ROWS)
            row = jnp.sum(jnp.sum(terms, axis=0), axis=0, keepdims=True)
            kpart[j // HALF, i, j % HALF:j % HALF + 1, :] = row
        return carry

    lax.fori_loop(0, NB, tap_grad, 0)
    send(kpart.at[1 - c], kin1, k_s.at[0], k_r.at[0], (sib, t))

    for k in (5, 6):
        pair_sum(k)
    ring_step(2)
    extra_down(2)
    extra_turn(2)

    my_cols = pl.ds(pl.multiple_of(t * ROWS, ROWS), ROWS)

    def roots_in(x):
        for n in range(Z):
            source = 8 * a + n
            rows = pl.ds(32 * n, 32)
            pl.when(source != d)(functools.partial(got, rrows.at[x, rows], r2_r.at[x, n]))
            pl.when(z != n)(functools.partial(got, lfull.at[x, n, a], l2_r.at[x, n]))
        rfull[x, :, my_cols] = rrows[x]

    def roots_out(x, when):
        for m in range(1, TENSOR):
            dev = (d, lax.rem(t + m, TENSOR))
            send(rrows.at[x], rfull.at[x, :, my_cols], r3_s.at[x, m], r3_r.at[x, m], dev, when)
        for m in range(1, QUADS):
            dev = (z * 4 + lax.rem(a + m, QUADS), t)
            send(lfull.at[x, :, a], lfull.at[x, :, a], l3_s.at[x, m], l3_r.at[x, m], dev, when)

    roots_in(0)
    roots_out(0, None)
    pl.when(home_z)(functools.partial(roots_in, 1))
    roots_out(1, home_z)

    got(kin1, k_r.at[0])
    ksend2[...] = kpart[c] + kin1[...]
    send(ksend2, kin2, k_s.at[1], k_r.at[1], (par, t))

    pair_sum(7)
    ring_step(3)
    extra_down(3)

    def shares():
        for h, hops in enumerate(HOPS):
            rows = slice(64 * h, 64 * h + 64)
            total = gown[7, rows, :]
            for way in (0, 1):
                last = hops[way] - 1
                got(rs_recv.at[h, way, last], rs_r.at[h, way, last])
                total = total + rs_recv[h, way, last].astype(F32)
            gown[7, rows, :] = total
            ysend[0, rows, :] = total.astype(BF)

    shares()
    send(ysend.at[0], yrecv.at[0], y_s.at[0], y_r.at[0], (par, t))

    @pl.when(home_z)
    def _():
        total = gown[8]
        for way in (0, 1):
            got(e_recv.at[way], es_r.at[way])
            total = total + e_recv[way].astype(F32)
        gown[8] = total
        ysend[1] = total.astype(BF)

    send(ysend.at[1], yrecv.at[1], y_s.at[1], y_r.at[1], (par, t), home_z)

    got(kin2, k_r.at[1])
    ksum[...] = ksend2[...] + kin2[...]
    for m in range(1, Z):
        send(ksum, kz.at[z], k_s.at[1 + m], k_r.at[1 + m], (at_z(z + m), t))
    kz[z] = ksum[...]

    def join(x):
        got(yrecv.at[x], y_r.at[x])
        gfull[x, c] = (gown[7 + x] + yrecv[x].astype(F32)).astype(BF)

    join(0)
    send(gfull.at[0, c], gfull.at[0, c], c_s.at[0], c_r.at[0], (sib, t))

    @pl.when(home_z)
    def _():
        join(1)

    send(gfull.at[1, c], gfull.at[1, c], c_s.at[1], c_r.at[1], (sib, t), home_z)

    def roots_all(x):
        for m in range(1, TENSOR):
            tt = lax.rem(t + m, TENSOR)
            cols = pl.ds(pl.multiple_of(tt * ROWS, ROWS), ROWS)
            got(rfull.at[x, :, cols], r3_r.at[x, TENSOR - m])
        for m in range(1, QUADS):
            got(lfull.at[x, :, lax.rem(a + m, QUADS)], l3_r.at[x, QUADS - m])
        for zz in range(Z):
            part = lfull[x, zz].reshape(ROWS, ROWS).astype(F32)
            lturn[x, :, ROWS * zz:ROWS * zz + ROWS] = part.T.astype(BF)

    roots_all(0)
    got(gfull.at[0, 1 - c], c_r.at[0])

    def right(x):
        part = dot(gfull[x, 0], rfull[x, :, :COLS], ((1,), (1,)))
        part = part + dot(gfull[x, 1], rfull[x, :, COLS:], ((1,), (1,)))
        wall[x, t] = (part * SHARE).astype(BF)

    right(0)
    for m in range(1, TENSOR):
        dev = (d, lax.rem(t + m, TENSOR))
        send(wall.at[0, t], wall.at[0, t], wt_s.at[0, m], wt_r.at[0, m], dev)

    @pl.when(home_z)
    def _():
        roots_all(1)
        got(gfull.at[1, 1 - c], c_r.at[1])
        right(1)

    for m in range(1, TENSOR):
        dev = (d, lax.rem(t + m, TENSOR))
        send(wall.at[1, t], wall.at[1, t], wt_s.at[1, m], wt_r.at[1, m], dev, home_z)

    rim(0, left_ok, ch_r, cg_halo, cgext, low)
    rim(1, right_ok, ch_r, cg_halo, cgext, high)

    def back(i, carry):
        total = jnp.zeros((ROWS, ROWS), F32)
        for j in range(TAPS):
            total = total + tapf[i, j:j + 1, :] * cgext[i, TAPS - j:TAPS - j + ROWS, :]
        igrad[i] = total
        return carry

    lax.fori_loop(0, NB, back, 0)

    def quarter(block, q):
        cols = pl.ds(pl.multiple_of(q * QUART, QUART), QUART)
        return upd.at[lax.div(block, NB), lax.rem(block, NB), :, cols]

    def left_mult(x, block):
        for m in range(1, TENSOR):
            got(wall.at[x, lax.rem(t + m, TENSOR)], wt_r.at[x, TENSOR - m])
        part = dot(lturn[x], wall[x].reshape(BLOCK, QUART), ((1,), (0,)))
        quarter(block, a)[...] = part.astype(BF)

    ap = a + 2 - 4 * yh
    second = jnp.int32(Z)

    left_mult(0, z)
    send(quarter(z, a), quarter(z, a), uy_s.at[0], uy_r.at[0], (par, t))

    quarters = (c, 2 + c)

    def piece(off, h):
        return quarter(lax.rem(z + off, Z), quarters[h])

    def share(off, h):
        send(piece(off, h), piece(off, h), us_s.at[off, h], us_r.at[off, h], (sib, t))

    def spread(s):
        for h, hops in enumerate(HOPS):
            for way in (0, 1):
                if s >= hops[way]:
                    continue
                off = s if way == 0 else (Z - s) % Z
                land = off + 1 if way == 0 else (off - 1) % Z
                send(
                    piece(off, h), piece(off, h), uz_s.at[h, way, s], uz_r.at[h, land],
                    (z_dn if way == 0 else z_up, t),
                )

    @pl.when(home_z)
    def _():
        left_mult(1, second)

    send(quarter(second, a), quarter(second, a), uy_s.at[1], uy_r.at[1], (par, t), home_z)
    got(quarter(z, ap), uy_r.at[0])
    spread(0)

    def extra_spread(s):
        for h in range(2):
            src = quarter(second, quarters[h])
            send(src, src, ez_s.at[h, 0], ez_r.at[h], ((s + 1) * 4 + a, t), z == s)
            if s < 3:
                far = (Z - s) % Z
                send(src, src, ez_s.at[h, 1], ez_r.at[h], ((7 - s) * 4 + a, t), z == far)

    @pl.when(home_z)
    def _():
        got(quarter(second, ap), uy_r.at[1])

    extra_spread(0)
    for h in range(2):
        share(0, h)
        src = quarter(second, quarters[h])
        send(src, src, us_s.at[8, h], us_r.at[8, h], (sib, t), home_z)

    for s in range(1, 5):
        for h, hops in enumerate(HOPS):
            if s <= hops[0]:
                got(piece(s, h), uz_r.at[h, s])
            if s <= hops[1]:
                got(piece(Z - s, h), uz_r.at[h, Z - s])
        if s < 4:
            spread(s)
        at = (z == s) | (z == Z - s)

        @pl.when(at)
        def _():
            for h in range(2):
                got(quarter(second, quarters[h]), ez_r.at[h])

        if s < 4:
            extra_spread(s)
        for h, hops in enumerate(HOPS):
            if s <= hops[0]:
                share(s, h)
            if s <= hops[1]:
                share(Z - s, h)
            src = quarter(second, quarters[h])
            send(src, src, us_s.at[8, h], us_r.at[8, h], (sib, t), at)
        if s == 2:
            for m in range(1, Z):
                got(kz.at[lax.rem(z + m, Z)], k_r.at[1 + Z - m])
            total = kz[0]
            for zz in range(1, Z):
                total = total + kz[zz]
            khalf[c] = total * SHARE
            send(khalf.at[c], khalf.at[c], k_s.at[9], k_r.at[9], (sib, t))

    got(khalf.at[1 - c], k_r.at[9])
    for half in range(2):
        for i in range(NB):
            kgrad[i, HALF * half:HALF * half + HALF, :] = khalf[half, i]

    other = (1 - c, 3 - c)
    for h in range(2):
        for off in range(Z):
            got(quarter(lax.rem(z + off, Z), other[h]), us_r.at[off, h])
        got(quarter(second, other[h]), us_r.at[8, h])
    for copy, when in sends:
        if when is None:
            copy.wait_send()
        else:
            pl.when(when)(copy.wait_send)


def per_device(
    glu_input, conv_kernel, norm_gain, norm_shift, out_weight, out_cotangent, root_stack, home
):
    lin = glu_input[:, 0].astype(F32)
    gate_sig = jax.nn.sigmoid(glu_input[:, 1].astype(F32))
    glu_out = (lin * gate_sig).astype(BF).transpose(1, 0, 2)

    vmem = pl.BlockSpec(memory_space=pltpu.VMEM)
    dma = pltpu.SemaphoreType.DMA
    sq = (NB, ROWS, ROWS)
    out = pl.pallas_call(
        kernel,
        out_shape=(
            jax.ShapeDtypeStruct((NB, NB, ROWS, BLOCK), BF),
            jax.ShapeDtypeStruct((NB, TAPS, ROWS), F32),
            jax.ShapeDtypeStruct(sq, F32),
        ),
        in_specs=[
            pl.BlockSpec(memory_space=pltpu.SMEM), vmem, pl.BlockSpec(memory_space=pl.ANY),
            vmem, vmem, vmem, vmem, vmem,
        ],
        out_specs=(vmem, vmem, vmem),
        scratch_shapes=[
            pltpu.VMEM((NB, TAPS, ROWS), F32),
            pltpu.VMEM((TENSOR, 2, 2, 32, ROWS), BF),
            pltpu.VMEM((NBLK, 32, ROWS), BF),
            pltpu.VMEM((NBLK, 32, ROWS), BF),
            pltpu.VMEM((2, QUART, ROWS), BF),
            pltpu.VMEM((2, QUART, BLOCK), BF),
            pltpu.VMEM((2, Z, QUADS, 32, ROWS), BF),
            pltpu.VMEM((2, ROWS, BLOCK), BF),
            pltpu.VMEM((2, NB, HALF, ROWS), BF),
            pltpu.VMEM((2, NB, HALF, ROWS), BF),
            pltpu.VMEM((NB, ROWS + TAPS, ROWS), F32),
            pltpu.VMEM(sq, F32),
            pltpu.VMEM(sq, BF),
            pltpu.VMEM(sq, BF),
            pltpu.VMEM((NB, ROWS + TAPS, ROWS), F32),
            pltpu.VMEM((NB, NB, ROWS, BLOCK), BF),
            pltpu.VMEM((NBLK, ROWS, COLS), BF),
            pltpu.VMEM((NBLK, ROWS, COLS), BF),
            pltpu.VMEM((NBLK, ROWS, COLS), F32),
            pltpu.VMEM((2, 2, 4, 64, COLS), BF),
            pltpu.VMEM((2, 2, 4, 64, COLS), BF),
            pltpu.VMEM((ROWS, COLS), BF),
            pltpu.VMEM((2, ROWS, COLS), BF),
            pltpu.VMEM((2, ROWS, COLS), BF),
            pltpu.VMEM((2, ROWS, COLS), BF),
            pltpu.VMEM((2, 2, ROWS, COLS), BF),
            pltpu.VMEM((2, TENSOR, ROWS, QUART), BF),
            pltpu.VMEM((2, NB, HALF, ROWS), F32),
            pltpu.VMEM((NB, HALF, ROWS), F32),
            pltpu.VMEM((NB, HALF, ROWS), F32),
            pltpu.VMEM((NB, HALF, ROWS), F32),
            pltpu.VMEM((NB, HALF, ROWS), F32),
            pltpu.VMEM((Z, NB, HALF, ROWS), F32),
            pltpu.VMEM((2, NB, HALF, ROWS), F32),
            dma,
            dma((2,)), dma((2,)),
            dma((8,)), dma((8,)),
            dma((9,)), dma((2, 8)),
            dma((9,)), dma((2, 8)),
            dma((2, 8)), dma((2, 8)),
            dma((2, 4)), dma((2, 4)),
            dma((9,)), dma((9,)),
            dma((2, 2, 4)), dma((2, 2, 4)),
            dma((2,)), dma((2,)),
            dma((2,)), dma((2,)),
            dma((2,)), dma((2,)),
            dma((2, 8)), dma((2, 8)),
            dma((2,)), dma((2,)),
            dma((2, 2, 4)), dma((2, 8)),
            dma((9, 2)), dma((9, 2)),
            dma((2, 2)), dma((2,)),
            dma((2,)), dma((2,)),
            dma((10,)), dma((10,)),
        ],
        compiler_params=pltpu.CompilerParams(
            collective_id=0, has_side_effects=True, vmem_limit_bytes=48 * 2**20
        ),
    )(
        home, glu_out, out_weight.transpose(0, 2, 1, 3), out_cotangent.transpose(1, 0, 2),
        root_stack, conv_kernel.transpose(1, 0, 2), norm_gain[:, None], norm_shift[:, None],
    )
    update, kernel_grad, input_grad = out
    input_grad = input_grad.transpose(1, 0, 2)
    glu_grad = jnp.stack(
        [input_grad * gate_sig, input_grad * lin * gate_sig * (1.0 - gate_sig)], axis=1
    ).astype(BF)
    return glu_grad, kernel_grad.transpose(1, 0, 2), update.transpose(0, 2, 1, 3)


def solution(mesh):
    placed = (
        P("dp", None, None, "tensor"),
        P(None, None, "tensor"),
        P(None, "tensor"),
        P(None, "tensor"),
        P(None, "tensor", None, None),
        P("dp", None, None),
        P("tensor", None, "dp", None),
        P(),
    )
    return jax.shard_map(
        per_device,
        mesh=mesh,
        in_specs=placed,
        out_specs=(
            P("dp", None, None, "tensor"),
            P(None, None, "tensor"),
            P(None, "tensor", None, None),
        ),
        check_vma=False,
    )
```

```python
import functools

import jax
import jax.numpy as jnp
from jax import lax
from jax.experimental import pallas as pl
from jax.experimental.pallas import tpu as pltpu
from jax.sharding import PartitionSpec as P

LEN = 2048
MESH = pl.DeviceIdType.MESH
BF = jnp.bfloat16
F32 = jnp.float32

Z = 8
QUADS = 4
TENSOR = 8
TAPS = 32
HALF = TAPS // 2
ROWS = 128
BLOCK = 1024
NB = 3
NBLK = 9
COLS = BLOCK // 2
QUART = BLOCK // 4
SHARE = LEN / (ROWS * Z * QUADS)

ORDER = (4, 3, 5, 2, 6, 1, 7, 0)
SPOT = {off: k for k, off in enumerate(ORDER)}
HOPS = ((4, 3), (3, 4))


def dot(a, b, dims):
    return lax.dot_general(a, b, (dims, ((), ())), preferred_element_type=F32)


def keep(dst, at, src, m):
    dst[at] = src[m]


def kernel(
    home, glu, weight_hbm, cot_hbm, roots_hbm, taps, gain, shift,
    upd, kgrad, igrad,
    cot, roots, tapf, cand, rpick, lpick, rrows, rfull, lfull, lturn,
    halo, cg_halo, gext, normed_s, at_s, cg_b, cgext, weight,
    gsend, gsib, gown, psend, precv, zsend, zrecv, erecv, gfull, wall,
    kpart, kin1, ksend2, kin2, ksum, kz, khalf,
    w_sem, cot_sem, roots_sem, halo_s, halo_r, s1_s, s1_r, r2_s, r2_r, l2_s, l2_r,
    r3_s, r3_r, l3_s, l3_r, gs_s, gs_r, p_s, p_r, z_s, z_r, ez_s, ez_r,
    c_s, c_r, wt_s, wt_r, uz_s, uz_r, uy_s, uy_r, us_s, us_r, ch_s, ch_r, k_s, k_r,
):
    d = lax.axis_index("dp")
    t = lax.axis_index("tensor")
    z = lax.div(d, 4)
    a = lax.rem(d, 4)
    yh = lax.div(a, 2)
    c = lax.rem(a, 2)
    sib = d + 1 - 2 * c
    par = d + 2 - 4 * yh

    def at_z(zz):
        return lax.rem(zz + 2 * Z, Z) * 4 + a

    quad = 2 * c + yh
    home_z = z == t

    def diagonal(m):
        tt = lax.rem(t + m, TENSOR)
        return (tt * 4 + a, tt)

    sends = []

    def send(src, dst, ss, rs, dev, when=None):
        copy = pltpu.make_async_remote_copy(
            src_ref=src, dst_ref=dst, send_sem=ss, recv_sem=rs,
            device_id=dev, device_id_type=MESH,
        )
        if when is None:
            copy.start()
        else:
            pl.when(when)(copy.start)
        sends.append((copy, when))

    def got(dst, rs):
        pltpu.make_async_remote_copy(
            src_ref=dst, dst_ref=dst, send_sem=s1_s.at[0], recv_sem=rs,
            device_id=(sib, t), device_id_type=MESH,
        ).wait_recv()

    barrier = pltpu.get_barrier_semaphore()

    def hello(dev):
        pl.semaphore_signal(barrier, inc=1, device_id=dev, device_id_type=MESH)

    hello((lax.rem(d + 31, 32), t))
    hello((lax.rem(d + 1, 32), t))
    for m in range(1, 4):
        hello((z * 4 + lax.rem(a + m, 4), t))
    for m in range(1, Z):
        hello((at_z(z + m), t))
    for m in range(1, TENSOR):
        hello((d, lax.rem(t + m, TENSOR)))

    r_quad = lax.div(z, 2)
    r_to = lax.rem(r_quad, 2) * 2 + lax.div(r_quad, 2)
    r_slot = lax.rem(z, 2) * 4 + a

    for n in range(Z):
        pl.when(8 * quad + n != d)(functools.partial(hello, (8 * quad + n, t)))
    for m in range(1, TENSOR):
        pl.when(home_z)(functools.partial(hello, diagonal(m)))

    roots_copy = pltpu.make_async_copy(roots_hbm, roots, roots_sem)
    roots_copy.start()
    cot_copy = pltpu.make_async_copy(cot_hbm, cot, cot_sem)
    cot_copy.start()
    w_copy = pltpu.make_async_copy(weight_hbm, weight, w_sem)
    w_copy.start()

    left_ok = (d != 0) & (lax.rem(d * ROWS + LEN // 2, LEN) != 0)
    right_ok = (d != 31) & (lax.rem((d + 1) * ROWS + LEN // 2, LEN) != 0)
    for i in range(NB):
        gext[i, HALF:HALF + ROWS, :] = glu[i].astype(F32)
        tapf[i] = taps[i].astype(F32)

    more = jnp.where(home_z, TENSOR - 1, 0) - jnp.where(r_to == a, 1, 0)
    pl.semaphore_wait(barrier, 2 + 3 + Z - 1 + TENSOR - 1 + Z + more)

    dn, up = (lax.rem(d + 31, 32), t), (lax.rem(d + 1, 32), t)
    send(glu.at[:, 0:HALF], halo.at[1], halo_s.at[0], halo_r.at[1], dn, left_ok)
    send(glu.at[:, ROWS - HALF:ROWS], halo.at[0], halo_s.at[1], halo_r.at[0], up, right_ok)
    roots_copy.wait()
    for m in range(1, TENSOR):
        tt = lax.rem(t + m, TENSOR)
        share_cols = pl.ds(pl.multiple_of(tt * ROWS, ROWS), ROWS)
        send(roots.at[:, :, :, share_cols], cand.at[t], s1_s.at[m], s1_r.at[m], (d, tt))
    cand[t] = roots[:, :, :, pl.ds(pl.multiple_of(t * ROWS, ROWS), ROWS)]

    def rim(side, ok, sem, src, dst, rows):
        @pl.when(ok)
        def _():
            got(src.at[side], sem.at[side])
            for i in range(NB):
                dst[i, rows, :] = src[side, i].astype(F32)

        @pl.when(jnp.logical_not(ok))
        def _():
            for i in range(NB):
                dst[i, rows, :] = jnp.zeros((HALF, ROWS), F32)

    low, high = pl.ds(0, HALF), pl.ds(HALF + ROWS, HALF)
    rim(0, left_ok, halo_r, halo, gext, low)
    rim(1, right_ok, halo_r, halo, gext, high)

    def conv(i, carry):
        total = jnp.zeros((ROWS, ROWS), F32)
        for j in range(TAPS):
            total = total + tapf[i, j:j + 1, :] * gext[i, j:j + ROWS, :]
        normed = total * gain[pl.ds(i, 1), :] + shift[pl.ds(i, 1), :]
        normed_s[i] = normed
        at_s[i] = (normed * jax.nn.sigmoid(normed)).T.astype(BF)
        return carry

    lax.fori_loop(0, NB, conv, 0)

    cot_copy.wait()
    own_cols = pl.ds(pl.multiple_of(c * COLS, COLS), COLS)
    sib_cols = pl.ds(pl.multiple_of((1 - c) * COLS, COLS), COLS)
    sequence = (0, 1, 2, 8, 3, 4, 5, 6, 7)
    for k in sequence:
        block = jnp.int32(8) if k == 8 else lax.rem(z + ORDER[k], Z)
        row = lax.div(block, NB)
        col = lax.rem(block, NB)
        left = at_s[row]
        gsend[k] = dot(left, cot[col, :, sib_cols], ((1,), (0,))).astype(BF)
        send(gsend.at[k], gsib.at[k], gs_s.at[k], gs_r.at[k], (sib, t))
        gown[k] = dot(left, cot[col, :, own_cols], ((1,), (0,)))

    own_part = pl.ds(pl.multiple_of(yh * QUART, QUART), QUART)
    par_part = pl.ds(pl.multiple_of((1 - yh) * QUART, QUART), QUART)
    for k in sequence:
        got(gsib.at[k], gs_r.at[k])
        psend[k] = (gown[k, :, par_part] + gsib[k, :, par_part].astype(F32)).astype(BF)
        send(psend.at[k], precv.at[k], p_s.at[k], p_r.at[k], (par, t))

    for m in range(1, TENSOR):
        got(cand.at[lax.rem(t + m, TENSOR)], s1_r.at[TENSOR - m])
    r_rows = pl.ds(pl.multiple_of(r_slot * 32, 32), 32)
    for m in range(NBLK):
        x = m // Z
        zz = t if x else lax.rem(z + m, Z)
        slot = home[8 if x else zz]
        own, which = lax.shift_right_logical(slot, 1), slot & 1
        lpick[m] = cand[own, which, 0]
        rpick[m] = cand[own, which, 1]
        r_dev = zz * 4 + r_to
        l_dev = zz * 4 + a
        send(rpick.at[m], rrows.at[x, r_rows], r2_s.at[m], r2_r.at[x, r_slot], (r_dev, t), r_dev != d)
        pl.when(r_dev == d)(functools.partial(keep, rrows, (x, r_rows), rpick, m))
        send(lpick.at[m], lfull.at[x, z, a], l2_s.at[m], l2_r.at[x, z], (l_dev, t), l_dev != d)
        pl.when(l_dev == d)(functools.partial(keep, lfull, (x, z, a), lpick, m))

    def pair_total(k):
        got(precv.at[k], p_r.at[k])
        both = gown[k, :, own_part] + gsib[k, :, own_part].astype(F32)
        return both + precv[k].astype(F32)

    def to_home(k):
        if k == 7:
            gown[k, :, own_part] = pair_total(k)
        elif k < 7:
            off = ORDER[k]
            zsend[k] = pair_total(k).astype(BF)
            send(zsend.at[k], zrecv.at[off], z_s.at[k], z_r.at[off], (at_z(z + off), t))
        else:
            total = pair_total(k)
            gown[k, :, own_part] = total
            zsend[k] = total.astype(BF)
            send(
                zsend.at[k], erecv.at[z], ez_s.at[0], ez_r.at[z], (at_z(t), t),
                jnp.logical_not(home_z),
            )

    for k in sequence[:5]:
        to_home(k)

    my_cols = pl.ds(pl.multiple_of(t * ROWS, ROWS), ROWS)

    def roots_in(x):
        for n in range(Z):
            source = 8 * quad + n
            rows = pl.ds(32 * n, 32)
            pl.when(source != d)(functools.partial(got, rrows.at[x, rows], r2_r.at[x, n]))
            pl.when(z != n)(functools.partial(got, lfull.at[x, n, a], l2_r.at[x, n]))
        rfull[x, :, my_cols] = rrows[x]

    def roots_out(x, when):
        for m in range(1, TENSOR):
            dev = diagonal(m) if x else (d, lax.rem(t + m, TENSOR))
            send(rrows.at[x], rfull.at[x, :, my_cols], r3_s.at[x, m], r3_r.at[x, m], dev, when)
        for m in range(1, QUADS):
            dev = (z * 4 + lax.rem(a + m, QUADS), t)
            send(lfull.at[x, :, a], lfull.at[x, :, a], l3_s.at[x, m], l3_r.at[x, m], dev, when)

    roots_in(0)
    roots_out(0, None)
    pl.when(home_z)(functools.partial(roots_in, 1))
    roots_out(1, home_z)

    for k in sequence[5:]:
        to_home(k)

    w_copy.wait()
    for i in range(NB):
        grad = jnp.zeros((ROWS, ROWS), F32)
        for j in range(NB):
            grad = grad + dot(cot[j], weight[i, j], ((1,), (1,)))
        normed = normed_s[i]
        sg = jax.nn.sigmoid(normed)
        cg = (grad * sg * (1.0 + normed * (1.0 - sg)) * gain[i:i + 1, :]).astype(BF)
        cg_b[i] = cg
        cgext[i, HALF:HALF + ROWS, :] = cg.astype(F32)
    send(cg_b.at[:, 0:HALF], cg_halo.at[1], ch_s.at[0], ch_r.at[1], dn, left_ok)
    send(cg_b.at[:, ROWS - HALF:ROWS], cg_halo.at[0], ch_s.at[1], ch_r.at[0], up, right_ok)

    def tap_grad(i, carry):
        cg = cgext[i, HALF:HALF + ROWS, :]
        for j in range(TAPS):
            terms = (cg * gext[i, j:j + ROWS, :]).reshape(ROWS // 8, 8, ROWS)
            row = jnp.sum(jnp.sum(terms, axis=0), axis=0, keepdims=True)
            kpart[j // HALF, i, j % HALF:j % HALF + 1, :] = row
        return carry

    lax.fori_loop(0, NB, tap_grad, 0)
    send(kpart.at[1 - c], kin1, k_s.at[0], k_r.at[0], (sib, t))

    def roots_all(x):
        for m in range(1, TENSOR):
            tt = lax.rem(t + m, TENSOR)
            cols = pl.ds(pl.multiple_of(tt * ROWS, ROWS), ROWS)
            got(rfull.at[x, :, cols], r3_r.at[x, TENSOR - m])
        for m in range(1, QUADS):
            got(lfull.at[x, :, lax.rem(a + m, QUADS)], l3_r.at[x, QUADS - m])
        for zz in range(Z):
            part = lfull[x, zz].reshape(ROWS, ROWS).astype(F32)
            lturn[x, :, ROWS * zz:ROWS * zz + ROWS] = part.T.astype(BF)

    def join(x):
        total = gown[7 + x, :, own_part]
        for n in range(Z):
            if x == 0 and n > 0:
                got(zrecv.at[n], z_r.at[n])
                total = total + zrecv[n].astype(F32)
            elif x == 1:
                pl.when(z != n)(functools.partial(got, erecv.at[n], ez_r.at[n]))
        if x == 1:
            erecv[z] = jnp.zeros((ROWS, QUART), BF)
            for n in range(Z):
                total = total + erecv[n].astype(F32)
        gfull[x, quad] = total.astype(BF)

    par_quad = 2 * c + 1 - yh

    def quarters_out(x, when):
        mine = gfull.at[x, quad]
        send(mine, mine, c_s.at[x, 0], c_r.at[x, 0], (par, t), when)
        send(mine, mine, c_s.at[x, 1], c_r.at[x, 1], (sib, t), when)

    def quarters_on(x, when):
        his = gfull.at[x, par_quad]
        send(his, his, c_s.at[x, 2], c_r.at[x, 2], (sib, t), when)

    def quarters_in(x):
        got(gfull.at[x, 2 * (1 - c) + yh], c_r.at[x, 1])
        got(gfull.at[x, 2 * (1 - c) + 1 - yh], c_r.at[x, 2])

    join(0)
    quarters_out(0, None)
    pl.when(home_z)(functools.partial(join, 1))
    quarters_out(1, home_z)

    got(kin1, k_r.at[0])
    ksend2[...] = kpart[c] + kin1[...]
    send(ksend2, kin2, k_s.at[1], k_r.at[1], (par, t))

    roots_all(0)
    pl.when(home_z)(functools.partial(roots_all, 1))

    got(gfull.at[0, par_quad], c_r.at[0, 0])
    quarters_on(0, None)
    pl.when(home_z)(functools.partial(got, gfull.at[1, par_quad], c_r.at[1, 0]))
    quarters_on(1, home_z)
    quarters_in(0)

    def right(x):
        part = jnp.zeros((ROWS, QUART), F32)
        for q in range(QUADS):
            part = part + dot(gfull[x, q], rfull[x, :, QUART * q:QUART * q + QUART], ((1,), (1,)))
        wall[x, t] = (part * SHARE).astype(BF)

    right(0)
    for m in range(1, TENSOR):
        dev = (d, lax.rem(t + m, TENSOR))
        send(wall.at[0, t], wall.at[0, t], wt_s.at[0, m], wt_r.at[0, m], dev)

    @pl.when(home_z)
    def _():
        quarters_in(1)
        right(1)

    for m in range(1, TENSOR):
        send(wall.at[1, t], wall.at[1, t], wt_s.at[1, m], wt_r.at[1, m], diagonal(m), home_z)

    got(kin2, k_r.at[1])
    ksum[...] = ksend2[...] + kin2[...]
    for m in range(1, Z):
        send(ksum, kz.at[z], k_s.at[1 + m], k_r.at[1 + m], (at_z(z + m), t))
    kz[z] = ksum[...]

    rim(0, left_ok, ch_r, cg_halo, cgext, low)
    rim(1, right_ok, ch_r, cg_halo, cgext, high)

    def back(i, carry):
        total = jnp.zeros((ROWS, ROWS), F32)
        for j in range(TAPS):
            total = total + tapf[i, j:j + 1, :] * cgext[i, TAPS - j:TAPS - j + ROWS, :]
        igrad[i] = total
        return carry

    lax.fori_loop(0, NB, back, 0)

    def quarter(block, q):
        cols = pl.ds(pl.multiple_of(q * QUART, QUART), QUART)
        return upd.at[lax.div(block, NB), lax.rem(block, NB), :, cols]

    def left_mult(x, block):
        for m in range(1, TENSOR):
            got(wall.at[x, lax.rem(t + m, TENSOR)], wt_r.at[x, TENSOR - m])
        part = dot(lturn[x], wall[x].reshape(BLOCK, QUART), ((1,), (0,)))
        quarter(block, quad)[...] = part.astype(BF)

    second = jnp.int32(Z)
    sib_quads = (2 * (1 - c) + yh, 2 * (1 - c) + 1 - yh)

    def piece(n, q):
        return quarter(second if n == Z else lax.rem(z + n, Z), q)

    def on(n, h, when=None):
        src = piece(n, par_quad if h else quad)
        if h == 0:
            send(src, src, uy_s.at[n], uy_r.at[n], (par, t), when)
        send(src, src, us_s.at[n, h], us_r.at[n, h], (sib, t), when)

    left_mult(0, z)
    for off in (3, 5, 4, 2, 6, 1, 7):
        src = piece(0, quad)
        send(src, src, uz_s.at[off], uz_r.at[off], (at_z(z + off), t))
    on(0, 0)

    @pl.when(home_z)
    def _():
        left_mult(1, second)

    for off in (3, 5, 4, 2, 6, 1, 7):
        src = piece(Z, quad)
        send(src, src, uz_s.at[Z + off], uz_r.at[Z], (at_z(z + off), t), home_z)

    for m in range(1, Z):
        got(kz.at[lax.rem(z + m, Z)], k_r.at[1 + Z - m])
    total = kz[0]
    for zz in range(1, Z):
        total = total + kz[zz]
    khalf[c] = total * SHARE
    send(khalf.at[c], khalf.at[c], k_s.at[9], k_r.at[9], (sib, t))

    for off in (1, 7, 2, 6, 3, 5, 4):
        got(piece(off, quad), uz_r.at[Z - off])
        on(off, 0)
    pl.when(jnp.logical_not(home_z))(functools.partial(got, piece(Z, quad), uz_r.at[Z]))
    on(Z, 0)
    for n in (0, 1, 7, 2, 6, 3, 5, 4, Z):
        got(piece(n, par_quad), uy_r.at[n])
        on(n, 1)

    got(khalf.at[1 - c], k_r.at[9])
    for half in range(2):
        for i in range(NB):
            kgrad[i, HALF * half:HALF * half + HALF, :] = khalf[half, i]

    for n in range(Z + 1):
        for h in range(2):
            got(piece(n, sib_quads[h]), us_r.at[n, h])

    for copy, when in sends:
        if when is None:
            copy.wait_send()
        else:
            pl.when(when)(copy.wait_send)


def per_device(
    glu_input, conv_kernel, norm_gain, norm_shift, out_weight, out_cotangent, root_stack, home
):
    lin = glu_input[:, 0].astype(F32)
    gate_sig = jax.nn.sigmoid(glu_input[:, 1].astype(F32))
    glu_out = (lin * gate_sig).astype(BF).transpose(1, 0, 2)

    vmem = pl.BlockSpec(memory_space=pltpu.VMEM)
    hbm = pl.BlockSpec(memory_space=pltpu.HBM)
    dma = pltpu.SemaphoreType.DMA
    sq = (NB, ROWS, ROWS)
    out = pl.pallas_call(
        kernel,
        out_shape=(
            jax.ShapeDtypeStruct((NB, NB, ROWS, BLOCK), BF),
            jax.ShapeDtypeStruct((NB, TAPS, ROWS), F32),
            jax.ShapeDtypeStruct(sq, F32),
        ),
        in_specs=[
            pl.BlockSpec(memory_space=pltpu.SMEM), vmem, hbm, hbm, hbm, vmem, vmem, vmem,
        ],
        out_specs=(vmem, vmem, vmem),
        scratch_shapes=[
            pltpu.VMEM((NB, ROWS, BLOCK), BF),
            pltpu.VMEM((2, 2, 32, BLOCK), BF),
            pltpu.VMEM((NB, TAPS, ROWS), F32),
            pltpu.VMEM((TENSOR, 2, 2, 32, ROWS), BF),
            pltpu.VMEM((NBLK, 32, ROWS), BF),
            pltpu.VMEM((NBLK, 32, ROWS), BF),
            pltpu.VMEM((2, QUART, ROWS), BF),
            pltpu.VMEM((2, QUART, BLOCK), BF),
            pltpu.VMEM((2, Z, QUADS, 32, ROWS), BF),
            pltpu.VMEM((2, ROWS, BLOCK), BF),
            pltpu.VMEM((2, NB, HALF, ROWS), BF),
            pltpu.VMEM((2, NB, HALF, ROWS), BF),
            pltpu.VMEM((NB, ROWS + TAPS, ROWS), F32),
            pltpu.VMEM(sq, F32),
            pltpu.VMEM(sq, BF),
            pltpu.VMEM(sq, BF),
            pltpu.VMEM((NB, ROWS + TAPS, ROWS), F32),
            pltpu.VMEM((NB, NB, ROWS, BLOCK), BF),
            pltpu.VMEM((NBLK, ROWS, COLS), BF),
            pltpu.VMEM((NBLK, ROWS, COLS), BF),
            pltpu.VMEM((NBLK, ROWS, COLS), F32),
            pltpu.VMEM((NBLK, ROWS, QUART), BF),
            pltpu.VMEM((NBLK, ROWS, QUART), BF),
            pltpu.VMEM((NBLK, ROWS, QUART), BF),
            pltpu.VMEM((Z, ROWS, QUART), BF),
            pltpu.VMEM((Z, ROWS, QUART), BF),
            pltpu.VMEM((2, QUADS, ROWS, QUART), BF),
            pltpu.VMEM((2, TENSOR, ROWS, QUART), BF),
            pltpu.VMEM((2, NB, HALF, ROWS), F32),
            pltpu.VMEM((NB, HALF, ROWS), F32),
            pltpu.VMEM((NB, HALF, ROWS), F32),
            pltpu.VMEM((NB, HALF, ROWS), F32),
            pltpu.VMEM((NB, HALF, ROWS), F32),
            pltpu.VMEM((Z, NB, HALF, ROWS), F32),
            pltpu.VMEM((2, NB, HALF, ROWS), F32),
            dma, dma, dma,
            dma((2,)), dma((2,)),
            dma((8,)), dma((8,)),
            dma((9,)), dma((2, 8)),
            dma((9,)), dma((2, 8)),
            dma((2, 8)), dma((2, 8)),
            dma((2, 4)), dma((2, 4)),
            dma((9,)), dma((9,)),
            dma((9,)), dma((9,)),
            dma((8,)), dma((8,)),
            dma((1,)), dma((8,)),
            dma((2, 3)), dma((2, 3)),
            dma((2, 8)), dma((2, 8)),
            dma((16,)), dma((9,)),
            dma((9,)), dma((9,)),
            dma((9, 2)), dma((9, 2)),
            dma((2,)), dma((2,)),
            dma((10,)), dma((10,)),
        ],
        compiler_params=pltpu.CompilerParams(
            collective_id=0, has_side_effects=True, vmem_limit_bytes=60 * 2**20
        ),
    )(
        home, glu_out, out_weight.transpose(0, 2, 1, 3), out_cotangent.transpose(1, 0, 2),
        root_stack, conv_kernel.transpose(1, 0, 2), norm_gain, norm_shift,
    )
    update, kernel_grad, input_grad = out
    input_grad = input_grad.transpose(1, 0, 2)
    glu_grad = jnp.stack(
        [input_grad * gate_sig, input_grad * lin * gate_sig * (1.0 - gate_sig)], axis=1
    ).astype(BF)
    return glu_grad, kernel_grad.transpose(1, 0, 2), update.transpose(0, 2, 1, 3)


def solution(mesh):
    placed = (
        P("dp", None, None, "tensor"),
        P(None, None, "tensor"),
        P(None, "tensor"),
        P(None, "tensor"),
        P(None, "tensor", None, None),
        P("dp", None, None),
        P("tensor", None, "dp", None),
        P(),
    )
    return jax.shard_map(
        per_device,
        mesh=mesh,
        in_specs=placed,
        out_specs=(
            P("dp", None, None, "tensor"),
            P(None, None, "tensor"),
            P(None, "tensor", None, None),
        ),
        check_vma=False,
    )
```

```python
import functools

import jax
import jax.numpy as jnp
from jax import lax
from jax.experimental import pallas as pl
from jax.experimental.pallas import tpu as pltpu
from jax.sharding import PartitionSpec as P

LEN = 2048
MESH = pl.DeviceIdType.MESH
BF = jnp.bfloat16
F32 = jnp.float32

Z = 8
QUADS = 4
TENSOR = 8
TAPS = 32
HALF = TAPS // 2
ROWS = 128
BLOCK = 1024
NB = 3
NBLK = 9
QUART = BLOCK // 4
SHARE = LEN / (ROWS * Z * QUADS)

ORDER = (4, 3, 5, 2, 6, 1, 7, 0)
SPOT = {off: k for k, off in enumerate(ORDER)}
HOPS = ((4, 3), (3, 4))


def dot(a, b, dims):
    return lax.dot_general(a, b, (dims, ((), ())), preferred_element_type=F32)


def keep(dst, at, src, m):
    dst[at] = src[m]


def kernel(
    home, glu, weight_hbm, cot_hbm, roots_hbm, taps, gain, shift,
    upd, kgrad, igrad,
    cot, roots, tapf, cand, rpick, lpick, rrows, rfull, lfull, lturn,
    halo, cg_halo, gext, normed_s, cg_b, cgext, weight,
    acts, ycols, gacc, relay, zsend, zrecv, erecv, gfull, wall,
    kpart, kin1, ksend2, kin2, ksum, kz, khalf,
    w_sem, cot_sem, roots_sem, halo_s, halo_r, s1_s, s1_r, r2_s, r2_r, l2_s, l2_r,
    r3_s, r3_r, l3_s, l3_r, yc_s, yc_r, at_s, at_r, yc_own, z_s, z_r, ez_s, ez_r,
    c_s, c_r, wt_s, wt_r, uz_s, uz_r, uy_s, uy_r, us_s, us_r, ch_s, ch_r, k_s, k_r,
):
    d = lax.axis_index("dp")
    t = lax.axis_index("tensor")
    z = lax.div(d, 4)
    a = lax.rem(d, 4)
    yh = lax.div(a, 2)
    c = lax.rem(a, 2)
    sib = d + 1 - 2 * c
    par = d + 2 - 4 * yh

    def at_z(zz):
        return lax.rem(zz + 2 * Z, Z) * 4 + a

    quad = 2 * c + yh
    home_z = z == t

    def diagonal(m):
        tt = lax.rem(t + m, TENSOR)
        return (tt * 4 + a, tt)

    sends = []

    def send(src, dst, ss, rs, dev, when=None):
        copy = pltpu.make_async_remote_copy(
            src_ref=src, dst_ref=dst, send_sem=ss, recv_sem=rs,
            device_id=dev, device_id_type=MESH,
        )
        if when is None:
            copy.start()
        else:
            pl.when(when)(copy.start)
        sends.append((copy, when))

    def got(dst, rs):
        pltpu.make_async_remote_copy(
            src_ref=dst, dst_ref=dst, send_sem=s1_s.at[0], recv_sem=rs,
            device_id=(sib, t), device_id_type=MESH,
        ).wait_recv()

    barrier = pltpu.get_barrier_semaphore()

    def hello(dev):
        pl.semaphore_signal(barrier, inc=1, device_id=dev, device_id_type=MESH)

    hello((lax.rem(d + 31, 32), t))
    hello((lax.rem(d + 1, 32), t))
    for m in range(1, 4):
        hello((z * 4 + lax.rem(a + m, 4), t))
    for m in range(1, Z):
        hello((at_z(z + m), t))
    for m in range(1, TENSOR):
        hello((d, lax.rem(t + m, TENSOR)))

    r_quad = lax.div(z, 2)
    r_to = lax.rem(r_quad, 2) * 2 + lax.div(r_quad, 2)
    r_slot = lax.rem(z, 2) * 4 + a

    for n in range(Z):
        pl.when(8 * quad + n != d)(functools.partial(hello, (8 * quad + n, t)))
    for m in range(1, TENSOR):
        pl.when(home_z)(functools.partial(hello, diagonal(m)))

    roots_copy = pltpu.make_async_copy(roots_hbm, roots, roots_sem)
    roots_copy.start()
    cot_copy = pltpu.make_async_copy(cot_hbm, cot, cot_sem)
    cot_copy.start()
    w_copy = pltpu.make_async_copy(weight_hbm, weight, w_sem)
    w_copy.start()

    left_ok = (d != 0) & (lax.rem(d * ROWS + LEN // 2, LEN) != 0)
    right_ok = (d != 31) & (lax.rem((d + 1) * ROWS + LEN // 2, LEN) != 0)
    for i in range(NB):
        gext[i, HALF:HALF + ROWS, :] = glu[i].astype(F32)
        tapf[i] = taps[i].astype(F32)

    more = jnp.where(home_z, TENSOR - 1, 0) - jnp.where(r_to == a, 1, 0)
    pl.semaphore_wait(barrier, 2 + 3 + Z - 1 + TENSOR - 1 + Z + more)

    dn, up = (lax.rem(d + 31, 32), t), (lax.rem(d + 1, 32), t)
    send(glu.at[:, 0:HALF], halo.at[1], halo_s.at[0], halo_r.at[1], dn, left_ok)
    send(glu.at[:, ROWS - HALF:ROWS], halo.at[0], halo_s.at[1], halo_r.at[0], up, right_ok)
    roots_copy.wait()
    def quad_of(aa):
        return 2 * lax.rem(aa, 2) + lax.div(aa, 2)

    def quad_cols(aa):
        return pl.ds(pl.multiple_of(quad_of(aa) * QUART, QUART), QUART)

    def frames_of(aa):
        return pl.ds(pl.multiple_of(aa * ROWS, ROWS), ROWS)

    my_frames = frames_of(a)
    y_own = pltpu.make_async_copy(cot_hbm.at[:, :, quad_cols(a)], ycols.at[:, my_frames], yc_own)
    y_own.start()
    for m in (2, 1, 3):
        aa = lax.rem(a + m, QUADS)
        src = cot_hbm.at[:, :, quad_cols(aa)]
        send(src, ycols.at[:, my_frames], yc_s.at[m], yc_r.at[m], (z * 4 + aa, t))

    for m in range(1, TENSOR):
        tt = lax.rem(t + m, TENSOR)
        share_cols = pl.ds(pl.multiple_of(tt * ROWS, ROWS), ROWS)
        send(roots.at[:, :, :, share_cols], cand.at[t], s1_s.at[m], s1_r.at[m], (d, tt))
    cand[t] = roots[:, :, :, pl.ds(pl.multiple_of(t * ROWS, ROWS), ROWS)]

    def rim(side, ok, sem, src, dst, rows):
        @pl.when(ok)
        def _():
            got(src.at[side], sem.at[side])
            for i in range(NB):
                dst[i, rows, :] = src[side, i].astype(F32)

        @pl.when(jnp.logical_not(ok))
        def _():
            for i in range(NB):
                dst[i, rows, :] = jnp.zeros((HALF, ROWS), F32)

    low, high = pl.ds(0, HALF), pl.ds(HALF + ROWS, HALF)
    rim(0, left_ok, halo_r, halo, gext, low)
    rim(1, right_ok, halo_r, halo, gext, high)

    def conv(i, carry):
        total = jnp.zeros((ROWS, ROWS), F32)
        for j in range(TAPS):
            total = total + tapf[i, j:j + 1, :] * gext[i, j:j + ROWS, :]
        normed = total * gain[pl.ds(i, 1), :] + shift[pl.ds(i, 1), :]
        normed_s[i] = normed
        acts[i, :, my_frames] = (normed * jax.nn.sigmoid(normed)).T.astype(BF)
        return carry

    lax.fori_loop(0, NB, conv, 0)

    a_par, a_sib = par - 4 * z, sib - 4 * z
    a_far = 3 - a

    def acts_of(aa):
        return acts.at[:, :, frames_of(aa)]

    send(acts_of(a), acts_of(a), at_s.at[0], at_r.at[0], (par, t))
    send(acts_of(a), acts_of(a), at_s.at[1], at_r.at[1], (sib, t))

    off_relay, off_plain = 2 + 4 * c, 6 - 4 * c
    offs = (4, 3, 5, None, off_plain, 1, 7, 0, off_relay)

    def product(n, chip):
        block = Z if n == 3 else lax.rem(z + offs[n], Z)
        row, col = (2, 2) if n == 3 else (lax.div(block, NB), lax.rem(block, NB))
        span = pl.ds(pl.multiple_of(chip * 256, 256), 256)
        return dot(acts[row, :, span], ycols[col, span, :], ((1,), (0,)))

    y_own.wait()
    got(ycols.at[:, frames_of(a_sib)], yc_r.at[lax.rem(a - a_sib + QUADS, QUADS)])
    got(acts_of(a_sib), at_r.at[1])
    for n in range(NBLK):
        gacc[n] = product(n, yh)

    for m in range(1, TENSOR):
        got(cand.at[lax.rem(t + m, TENSOR)], s1_r.at[TENSOR - m])
    r_rows = pl.ds(pl.multiple_of(r_slot * 32, 32), 32)
    for m in range(NBLK):
        x = m // Z
        zz = t if x else lax.rem(z + m, Z)
        slot = home[8 if x else zz]
        own, which = lax.shift_right_logical(slot, 1), slot & 1
        lpick[m] = cand[own, which, 0]
        rpick[m] = cand[own, which, 1]
        r_dev = zz * 4 + r_to
        l_dev = zz * 4 + a
        send(rpick.at[m], rrows.at[x, r_rows], r2_s.at[m], r2_r.at[x, r_slot], (r_dev, t), r_dev != d)
        pl.when(r_dev == d)(functools.partial(keep, rrows, (x, r_rows), rpick, m))
        send(lpick.at[m], lfull.at[x, z, a], l2_s.at[m], l2_r.at[x, z], (l_dev, t), l_dev != d)
        pl.when(l_dev == d)(functools.partial(keep, lfull, (x, z, a), lpick, m))

    got(acts_of(a_par), at_r.at[0])
    send(acts_of(a_par), acts_of(a_par), at_s.at[2], at_r.at[2], (sib, t))
    for aa in (a_par, a_far):
        got(ycols.at[:, frames_of(aa)], yc_r.at[lax.rem(a - aa + QUADS, QUADS)])
    got(acts_of(a_far), at_r.at[2])

    for n in range(NBLK):
        total = gacc[n] + product(n, 1 - yh)
        if n == 3:
            gacc[n] = total
            zsend[n] = total.astype(BF)
            send(
                zsend.at[n], erecv.at[z], ez_s.at[0], ez_r.at[z], (at_z(t), t),
                jnp.logical_not(home_z),
            )
        elif n == 0:
            zsend[n] = total.astype(BF)
            send(zsend.at[n], relay, z_s.at[n], z_r.at[4], (at_z(z + off_relay), t))
        elif n == 7:
            gacc[n] = total
        else:
            if n == 8:
                got(relay, z_r.at[4])
                total = total + relay[...].astype(F32)
            zsend[n] = total.astype(BF)
            send(
                zsend.at[n], zrecv.at[offs[n]], z_s.at[n], z_r.at[offs[n]],
                (at_z(z + offs[n]), t),
            )

    my_cols = pl.ds(pl.multiple_of(t * ROWS, ROWS), ROWS)

    def roots_in(x):
        for n in range(Z):
            source = 8 * quad + n
            rows = pl.ds(32 * n, 32)
            pl.when(source != d)(functools.partial(got, rrows.at[x, rows], r2_r.at[x, n]))
            pl.when(z != n)(functools.partial(got, lfull.at[x, n, a], l2_r.at[x, n]))
        rfull[x, :, my_cols] = rrows[x]

    def roots_out(x, when):
        for m in range(1, TENSOR):
            dev = diagonal(m) if x else (d, lax.rem(t + m, TENSOR))
            send(rrows.at[x], rfull.at[x, :, my_cols], r3_s.at[x, m], r3_r.at[x, m], dev, when)
        for m in range(1, QUADS):
            dev = (z * 4 + lax.rem(a + m, QUADS), t)
            send(lfull.at[x, :, a], lfull.at[x, :, a], l3_s.at[x, m], l3_r.at[x, m], dev, when)

    roots_in(0)
    roots_out(0, None)
    pl.when(home_z)(functools.partial(roots_in, 1))
    roots_out(1, home_z)

    cot_copy.wait()
    w_copy.wait()
    for i in range(NB):
        grad = jnp.zeros((ROWS, ROWS), F32)
        for j in range(NB):
            grad = grad + dot(cot[j], weight[i, j], ((1,), (1,)))
        normed = normed_s[i]
        sg = jax.nn.sigmoid(normed)
        cg = (grad * sg * (1.0 + normed * (1.0 - sg)) * gain[i:i + 1, :]).astype(BF)
        cg_b[i] = cg
        cgext[i, HALF:HALF + ROWS, :] = cg.astype(F32)
    send(cg_b.at[:, 0:HALF], cg_halo.at[1], ch_s.at[0], ch_r.at[1], dn, left_ok)
    send(cg_b.at[:, ROWS - HALF:ROWS], cg_halo.at[0], ch_s.at[1], ch_r.at[0], up, right_ok)

    def tap_grad(i, carry):
        cg = cgext[i, HALF:HALF + ROWS, :]
        for j in range(TAPS):
            terms = (cg * gext[i, j:j + ROWS, :]).reshape(ROWS // 8, 8, ROWS)
            row = jnp.sum(jnp.sum(terms, axis=0), axis=0, keepdims=True)
            kpart[j // HALF, i, j % HALF:j % HALF + 1, :] = row
        return carry

    lax.fori_loop(0, NB, tap_grad, 0)
    send(kpart.at[1 - c], kin1, k_s.at[0], k_r.at[0], (sib, t))

    def roots_all(x):
        for m in range(1, TENSOR):
            tt = lax.rem(t + m, TENSOR)
            cols = pl.ds(pl.multiple_of(tt * ROWS, ROWS), ROWS)
            got(rfull.at[x, :, cols], r3_r.at[x, TENSOR - m])
        for m in range(1, QUADS):
            got(lfull.at[x, :, lax.rem(a + m, QUADS)], l3_r.at[x, QUADS - m])
        for zz in range(Z):
            part = lfull[x, zz].reshape(ROWS, ROWS).astype(F32)
            lturn[x, :, ROWS * zz:ROWS * zz + ROWS] = part.T.astype(BF)

    def join(x):
        total = gacc[3 if x else 7]
        for n in range(Z):
            if x == 0 and n not in (0, 4):
                got(zrecv.at[n], z_r.at[n])
                total = total + zrecv[n].astype(F32)
            elif x == 1:
                pl.when(z != n)(functools.partial(got, erecv.at[n], ez_r.at[n]))
        if x == 1:
            erecv[z] = jnp.zeros((ROWS, QUART), BF)
            for n in range(Z):
                total = total + erecv[n].astype(F32)
        gfull[x, quad] = total.astype(BF)

    par_quad = 2 * c + 1 - yh

    def quarters_out(x, when):
        mine = gfull.at[x, quad]
        send(mine, mine, c_s.at[x, 0], c_r.at[x, 0], (par, t), when)
        send(mine, mine, c_s.at[x, 1], c_r.at[x, 1], (sib, t), when)

    def quarters_on(x, when):
        his = gfull.at[x, par_quad]
        send(his, his, c_s.at[x, 2], c_r.at[x, 2], (sib, t), when)

    def quarters_in(x):
        got(gfull.at[x, 2 * (1 - c) + yh], c_r.at[x, 1])
        got(gfull.at[x, 2 * (1 - c) + 1 - yh], c_r.at[x, 2])

    join(0)
    quarters_out(0, None)
    pl.when(home_z)(functools.partial(join, 1))
    quarters_out(1, home_z)

    got(kin1, k_r.at[0])
    ksend2[...] = kpart[c] + kin1[...]
    send(ksend2, kin2, k_s.at[1], k_r.at[1], (par, t))

    roots_all(0)
    pl.when(home_z)(functools.partial(roots_all, 1))

    got(gfull.at[0, par_quad], c_r.at[0, 0])
    quarters_on(0, None)
    pl.when(home_z)(functools.partial(got, gfull.at[1, par_quad], c_r.at[1, 0]))
    quarters_on(1, home_z)
    quarters_in(0)

    def right(x):
        part = jnp.zeros((ROWS, QUART), F32)
        for q in range(QUADS):
            part = part + dot(gfull[x, q], rfull[x, :, QUART * q:QUART * q + QUART], ((1,), (1,)))
        wall[x, t] = (part * SHARE).astype(BF)

    right(0)
    for m in range(1, TENSOR):
        dev = (d, lax.rem(t + m, TENSOR))
        send(wall.at[0, t], wall.at[0, t], wt_s.at[0, m], wt_r.at[0, m], dev)

    @pl.when(home_z)
    def _():
        quarters_in(1)
        right(1)

    for m in range(1, TENSOR):
        send(wall.at[1, t], wall.at[1, t], wt_s.at[1, m], wt_r.at[1, m], diagonal(m), home_z)

    got(kin2, k_r.at[1])
    ksum[...] = ksend2[...] + kin2[...]
    for m in range(1, Z):
        send(ksum, kz.at[z], k_s.at[1 + m], k_r.at[1 + m], (at_z(z + m), t))
    kz[z] = ksum[...]

    rim(0, left_ok, ch_r, cg_halo, cgext, low)
    rim(1, right_ok, ch_r, cg_halo, cgext, high)

    def back(i, carry):
        total = jnp.zeros((ROWS, ROWS), F32)
        for j in range(TAPS):
            total = total + tapf[i, j:j + 1, :] * cgext[i, TAPS - j:TAPS - j + ROWS, :]
        igrad[i] = total
        return carry

    lax.fori_loop(0, NB, back, 0)

    def quarter(block, q):
        cols = pl.ds(pl.multiple_of(q * QUART, QUART), QUART)
        return upd.at[lax.div(block, NB), lax.rem(block, NB), :, cols]

    def left_mult(x, block):
        for m in range(1, TENSOR):
            got(wall.at[x, lax.rem(t + m, TENSOR)], wt_r.at[x, TENSOR - m])
        part = dot(lturn[x], wall[x].reshape(BLOCK, QUART), ((1,), (0,)))
        quarter(block, quad)[...] = part.astype(BF)

    second = jnp.int32(Z)
    sib_quads = (2 * (1 - c) + yh, 2 * (1 - c) + 1 - yh)

    def piece(n, q):
        return quarter(second if n == Z else lax.rem(z + n, Z), q)

    def on(n, h, when=None):
        src = piece(n, par_quad if h else quad)
        if h == 0:
            send(src, src, uy_s.at[n], uy_r.at[n], (par, t), when)
        send(src, src, us_s.at[n, h], us_r.at[n, h], (sib, t), when)

    left_mult(0, z)
    for off in (3, 5, 2, 6, 1, 7):
        src = piece(0, quad)
        send(src, src, uz_s.at[off], uz_r.at[off], (at_z(z + off), t))
    on(0, 0)

    @pl.when(home_z)
    def _():
        left_mult(1, second)

    for off in (3, 5, 2, 6, 1, 7):
        src = piece(Z, quad)
        send(src, src, uz_s.at[Z + off], uz_r.at[Z], (at_z(z + off), t), home_z)

    for m in range(1, Z):
        got(kz.at[lax.rem(z + m, Z)], k_r.at[1 + Z - m])
    total = kz[0]
    for zz in range(1, Z):
        total = total + kz[zz]
    khalf[c] = total * SHARE
    send(khalf.at[c], khalf.at[c], k_s.at[9], k_r.at[9], (sib, t))

    def pass_on(n, land, when):
        src = piece(n, quad)
        send(src, src, uz_s.at[4 + land], uz_r.at[land], (at_z(z - 1 + 2 * c), t), when)

    for off in (3, 5, 2, 6, 1, 7):
        got(piece(off, quad), uz_r.at[Z - off])
        if off == 3:
            pass_on(3, 4, c == 0)
        if off == 5:
            pass_on(5, 4, c == 1)
        on(off, 0)
    pl.when(jnp.logical_not(home_z))(functools.partial(got, piece(Z, quad), uz_r.at[Z]))
    pass_on(Z, Z, lax.rem(t - z + Z, Z) == 3 + 2 * c)
    on(Z, 0)
    got(piece(4, quad), uz_r.at[4])
    on(4, 0)
    for n in (0, 3, 5, 2, 6, 1, 7, Z, 4):
        got(piece(n, par_quad), uy_r.at[n])
        on(n, 1)

    got(khalf.at[1 - c], k_r.at[9])
    for half in range(2):
        for i in range(NB):
            kgrad[i, HALF * half:HALF * half + HALF, :] = khalf[half, i]

    for n in range(Z + 1):
        for h in range(2):
            got(piece(n, sib_quads[h]), us_r.at[n, h])

    for copy, when in sends:
        if when is None:
            copy.wait_send()
        else:
            pl.when(when)(copy.wait_send)


def per_device(
    glu_input, conv_kernel, norm_gain, norm_shift, out_weight, out_cotangent, root_stack, home
):
    lin = glu_input[:, 0].astype(F32)
    gate_sig = jax.nn.sigmoid(glu_input[:, 1].astype(F32))
    glu_out = (lin * gate_sig).astype(BF).transpose(1, 0, 2)

    vmem = pl.BlockSpec(memory_space=pltpu.VMEM)
    hbm = pl.BlockSpec(memory_space=pltpu.HBM)
    dma = pltpu.SemaphoreType.DMA
    sq = (NB, ROWS, ROWS)
    out = pl.pallas_call(
        kernel,
        out_shape=(
            jax.ShapeDtypeStruct((NB, NB, ROWS, BLOCK), BF),
            jax.ShapeDtypeStruct((NB, TAPS, ROWS), F32),
            jax.ShapeDtypeStruct(sq, F32),
        ),
        in_specs=[
            pl.BlockSpec(memory_space=pltpu.SMEM), vmem, hbm, hbm, hbm, vmem, vmem, vmem,
        ],
        out_specs=(vmem, vmem, vmem),
        scratch_shapes=[
            pltpu.VMEM((NB, ROWS, BLOCK), BF),
            pltpu.VMEM((2, 2, 32, BLOCK), BF),
            pltpu.VMEM((NB, TAPS, ROWS), F32),
            pltpu.VMEM((TENSOR, 2, 2, 32, ROWS), BF),
            pltpu.VMEM((NBLK, 32, ROWS), BF),
            pltpu.VMEM((NBLK, 32, ROWS), BF),
            pltpu.VMEM((2, QUART, ROWS), BF),
            pltpu.VMEM((2, QUART, BLOCK), BF),
            pltpu.VMEM((2, Z, QUADS, 32, ROWS), BF),
            pltpu.VMEM((2, ROWS, BLOCK), BF),
            pltpu.VMEM((2, NB, HALF, ROWS), BF),
            pltpu.VMEM((2, NB, HALF, ROWS), BF),
            pltpu.VMEM((NB, ROWS + TAPS, ROWS), F32),
            pltpu.VMEM(sq, F32),
            pltpu.VMEM(sq, BF),
            pltpu.VMEM((NB, ROWS + TAPS, ROWS), F32),
            pltpu.VMEM((NB, NB, ROWS, BLOCK), BF),
            pltpu.VMEM((NB, ROWS, QUADS * ROWS), BF),
            pltpu.VMEM((NB, QUADS * ROWS, QUART), BF),
            pltpu.VMEM((NBLK, ROWS, QUART), F32),
            pltpu.VMEM((ROWS, QUART), BF),
            pltpu.VMEM((NBLK, ROWS, QUART), BF),
            pltpu.VMEM((Z, ROWS, QUART), BF),
            pltpu.VMEM((Z, ROWS, QUART), BF),
            pltpu.VMEM((2, QUADS, ROWS, QUART), BF),
            pltpu.VMEM((2, TENSOR, ROWS, QUART), BF),
            pltpu.VMEM((2, NB, HALF, ROWS), F32),
            pltpu.VMEM((NB, HALF, ROWS), F32),
            pltpu.VMEM((NB, HALF, ROWS), F32),
            pltpu.VMEM((NB, HALF, ROWS), F32),
            pltpu.VMEM((NB, HALF, ROWS), F32),
            pltpu.VMEM((Z, NB, HALF, ROWS), F32),
            pltpu.VMEM((2, NB, HALF, ROWS), F32),
            dma, dma, dma,
            dma((2,)), dma((2,)),
            dma((8,)), dma((8,)),
            dma((9,)), dma((2, 8)),
            dma((9,)), dma((2, 8)),
            dma((2, 8)), dma((2, 8)),
            dma((2, 4)), dma((2, 4)),
            dma((4,)), dma((4,)),
            dma((3,)), dma((3,)),
            dma,
            dma((9,)), dma((8,)),
            dma((1,)), dma((8,)),
            dma((2, 3)), dma((2, 3)),
            dma((2, 8)), dma((2, 8)),
            dma((16,)), dma((9,)),
            dma((9,)), dma((9,)),
            dma((9, 2)), dma((9, 2)),
            dma((2,)), dma((2,)),
            dma((10,)), dma((10,)),
        ],
        compiler_params=pltpu.CompilerParams(
            collective_id=0, has_side_effects=True, vmem_limit_bytes=60 * 2**20
        ),
    )(
        home, glu_out, out_weight.transpose(0, 2, 1, 3), out_cotangent.transpose(1, 0, 2),
        root_stack, conv_kernel.transpose(1, 0, 2), norm_gain, norm_shift,
    )
    update, kernel_grad, input_grad = out
    input_grad = input_grad.transpose(1, 0, 2)
    glu_grad = jnp.stack(
        [input_grad * gate_sig, input_grad * lin * gate_sig * (1.0 - gate_sig)], axis=1
    ).astype(BF)
    return glu_grad, kernel_grad.transpose(1, 0, 2), update.transpose(0, 2, 1, 3)


def solution(mesh):
    placed = (
        P("dp", None, None, "tensor"),
        P(None, None, "tensor"),
        P(None, "tensor"),
        P(None, "tensor"),
        P(None, "tensor", None, None),
        P("dp", None, None),
        P("tensor", None, "dp", None),
        P(),
    )
    return jax.shard_map(
        per_device,
        mesh=mesh,
        in_specs=placed,
        out_specs=(
            P("dp", None, None, "tensor"),
            P(None, None, "tensor"),
            P(None, "tensor", None, None),
        ),
        check_vma=False,
    )
```

```python
import functools

import jax
import jax.numpy as jnp
from jax import lax
from jax.experimental import pallas as pl
from jax.experimental.pallas import tpu as pltpu
from jax.sharding import PartitionSpec as P

LEN = 2048
MESH = pl.DeviceIdType.MESH
BF = jnp.bfloat16
F32 = jnp.float32

Z = 8
QUADS = 4
TENSOR = 8
TAPS = 32
HALF = TAPS // 2
ROWS = 128
BLOCK = 1024
NB = 3
NBLK = 9
QUART = BLOCK // 4
SHARE = LEN / (ROWS * Z * QUADS)

ORDER = (4, 3, 5, 2, 6, 1, 7, 0)
SPOT = {off: k for k, off in enumerate(ORDER)}
HOPS = ((4, 3), (3, 4))


def dot(a, b, dims):
    return lax.dot_general(a, b, (dims, ((), ())), preferred_element_type=F32)


def keep(dst, at, src, m):
    dst[at] = src[m]


def kernel(
    home, glu_hbm, weight_hbm, cot_hbm, roots_hbm, taps, gain, shift,
    upd, kgrad, ggrad,
    raw, glu, cot, roots, tapf, cand, rpick, lpick, rrows, rfull, lfull, lturn,
    halo, cg_halo, gext, normed_s, cg_b, cgext, weight,
    acts, ycols, gacc, relay, zsend, zrecv, erecv, gfull, wall,
    kpart, kin1, ksend2, kin2, ksum, kz, khalf,
    raw_sem, w_sem, cot_sem, roots_sem, halo_s, halo_r, s1_s, s1_r, r2_s, r2_r, l2_s, l2_r,
    r3_s, r3_r, l3_s, l3_r, yc_s, yc_r, ys_s, ys_r, yx_s, yx_r, at_s, at_r, yc_own, z_s, z_r, ez_s, ez_r,
    c_s, c_r, wt_s, wt_r, uz_s, uz_r, uy_s, uy_r, us_s, us_r, ch_s, ch_r, k_s, k_r,
):
    d = lax.axis_index("dp")
    t = lax.axis_index("tensor")
    z = lax.div(d, 4)
    a = lax.rem(d, 4)
    yh = lax.div(a, 2)
    c = lax.rem(a, 2)
    sib = d + 1 - 2 * c
    par = d + 2 - 4 * yh

    def at_z(zz):
        return lax.rem(zz + 2 * Z, Z) * 4 + a

    quad = 2 * c + yh
    home_z = z == t

    def diagonal(m):
        tt = lax.rem(t + m, TENSOR)
        return (tt * 4 + a, tt)

    sends = []

    def send(src, dst, ss, rs, dev, when=None):
        copy = pltpu.make_async_remote_copy(
            src_ref=src, dst_ref=dst, send_sem=ss, recv_sem=rs,
            device_id=dev, device_id_type=MESH,
        )
        if when is None:
            copy.start()
        else:
            pl.when(when)(copy.start)
        sends.append((copy, when))

    def got(dst, rs):
        pltpu.make_async_remote_copy(
            src_ref=dst, dst_ref=dst, send_sem=s1_s.at[0], recv_sem=rs,
            device_id=(sib, t), device_id_type=MESH,
        ).wait_recv()

    barrier = pltpu.get_barrier_semaphore()

    def hello(dev):
        pl.semaphore_signal(barrier, inc=1, device_id=dev, device_id_type=MESH)

    hello((lax.rem(d + 31, 32), t))
    hello((lax.rem(d + 1, 32), t))
    for m in range(1, 4):
        hello((z * 4 + lax.rem(a + m, 4), t))
    for m in range(1, Z):
        hello((at_z(z + m), t))
    for m in range(1, TENSOR):
        hello((d, lax.rem(t + m, TENSOR)))

    r_quad = lax.div(z, 2)
    r_to = lax.rem(r_quad, 2) * 2 + lax.div(r_quad, 2)
    r_slot = lax.rem(z, 2) * 4 + a

    for n in range(Z):
        pl.when(8 * quad + n != d)(functools.partial(hello, (8 * quad + n, t)))
    for m in range(1, TENSOR):
        pl.when(home_z)(functools.partial(hello, diagonal(m)))

    raw_copy = pltpu.make_async_copy(glu_hbm, raw, raw_sem)
    raw_copy.start()
    roots_copy = pltpu.make_async_copy(roots_hbm, roots, roots_sem)
    roots_copy.start()
    cot_copy = pltpu.make_async_copy(cot_hbm, cot, cot_sem)
    cot_copy.start()
    w_copy = pltpu.make_async_copy(weight_hbm, weight, w_sem)
    w_copy.start()

    left_ok = (d != 0) & (lax.rem(d * ROWS + LEN // 2, LEN) != 0)
    right_ok = (d != 31) & (lax.rem((d + 1) * ROWS + LEN // 2, LEN) != 0)
    raw_copy.wait()

    def halves(i):
        both = raw[:, i].astype(F32)
        return both[:, 0, :], both[:, 1, :]

    for i in range(NB):
        lin, gate = halves(i)
        glu[i] = (lin * jax.nn.sigmoid(gate)).astype(BF)
        gext[i, HALF:HALF + ROWS, :] = glu[i].astype(F32)
        tapf[i] = taps[i].astype(F32)

    more = jnp.where(home_z, TENSOR - 1, 0) - jnp.where(r_to == a, 1, 0)
    pl.semaphore_wait(barrier, 2 + 3 + Z - 1 + TENSOR - 1 + Z + more)

    dn, up = (lax.rem(d + 31, 32), t), (lax.rem(d + 1, 32), t)
    send(glu.at[:, 0:HALF], halo.at[1], halo_s.at[0], halo_r.at[1], dn, left_ok)
    send(glu.at[:, ROWS - HALF:ROWS], halo.at[0], halo_s.at[1], halo_r.at[0], up, right_ok)
    roots_copy.wait()
    def quad_of(aa):
        return 2 * lax.rem(aa, 2) + lax.div(aa, 2)

    def quad_cols(aa):
        return pl.ds(pl.multiple_of(quad_of(aa) * QUART, QUART), QUART)

    def frames_of(aa):
        return pl.ds(pl.multiple_of(aa * ROWS, ROWS), ROWS)

    my_frames = frames_of(a)
    y_own = pltpu.make_async_copy(cot_hbm.at[:, :, quad_cols(a)], ycols.at[:, my_frames], yc_own)
    y_own.start()
    a_par, a_sib, a_far = a + 2 - 4 * yh, a + 1 - 2 * c, 3 - a
    x = lax.rem(t, 4)

    def piece_of(aa, xx):
        rows = pl.ds(pl.multiple_of(aa * ROWS + xx * 32, 32), 32)
        return ycols.at[:, rows]

    x_rows = pl.ds(pl.multiple_of(x * 32, 32), 32)
    for n, aa in enumerate((a_par, a_far)):
        src = cot_hbm.at[:, x_rows, quad_cols(aa)]
        send(src, piece_of(a, x), yc_s.at[n], yc_r.at[n], (z * 4 + aa, t))
    src = cot_hbm.at[:, :, quad_cols(a_sib)]
    send(src, ycols.at[:, my_frames], ys_s.at[0], ys_r.at[0], (sib, t))

    for m in range(1, TENSOR):
        tt = lax.rem(t + m, TENSOR)
        share_cols = pl.ds(pl.multiple_of(tt * ROWS, ROWS), ROWS)
        send(roots.at[:, :, :, share_cols], cand.at[t], s1_s.at[m], s1_r.at[m], (d, tt))
    cand[t] = roots[:, :, :, pl.ds(pl.multiple_of(t * ROWS, ROWS), ROWS)]

    def rim(side, ok, sem, src, dst, rows):
        @pl.when(ok)
        def _():
            got(src.at[side], sem.at[side])
            for i in range(NB):
                dst[i, rows, :] = src[side, i].astype(F32)

        @pl.when(jnp.logical_not(ok))
        def _():
            for i in range(NB):
                dst[i, rows, :] = jnp.zeros((HALF, ROWS), F32)

    low, high = pl.ds(0, HALF), pl.ds(HALF + ROWS, HALF)
    rim(0, left_ok, halo_r, halo, gext, low)
    rim(1, right_ok, halo_r, halo, gext, high)

    for n, aa in enumerate((a_par, a_far)):
        src = piece_of(aa, x)
        got(src, yc_r.at[n])
        for m in range(1, 4):
            dev = (d, t - x + lax.rem(x + m, 4))
            send(src, src, yx_s.at[n, m], yx_r.at[n, m], dev)

    def conv(i, carry):
        total = jnp.zeros((ROWS, ROWS), F32)
        for j in range(TAPS):
            total = total + tapf[i, j:j + 1, :] * gext[i, j:j + ROWS, :]
        normed = total * gain[pl.ds(i, 1), :] + shift[pl.ds(i, 1), :]
        normed_s[i] = normed
        acts[i, :, my_frames] = (normed * jax.nn.sigmoid(normed)).T.astype(BF)
        return carry

    lax.fori_loop(0, NB, conv, 0)


    def acts_of(aa):
        return acts.at[:, :, frames_of(aa)]

    send(acts_of(a), acts_of(a), at_s.at[0], at_r.at[0], (par, t))
    send(acts_of(a), acts_of(a), at_s.at[1], at_r.at[1], (sib, t))

    off_relay, off_plain = 2 + 4 * c, 6 - 4 * c
    offs = (4, 3, 5, None, off_plain, 1, 7, 0, off_relay)

    def product(n, chip):
        block = Z if n == 3 else lax.rem(z + offs[n], Z)
        row, col = (2, 2) if n == 3 else (lax.div(block, NB), lax.rem(block, NB))
        span = pl.ds(pl.multiple_of(chip * 256, 256), 256)
        return dot(acts[row, :, span], ycols[col, span, :], ((1,), (0,)))

    y_own.wait()
    got(ycols.at[:, frames_of(a_sib)], ys_r.at[0])
    got(acts_of(a_sib), at_r.at[1])
    for n in range(NBLK):
        gacc[n] = product(n, yh)

    for m in range(1, TENSOR):
        got(cand.at[lax.rem(t + m, TENSOR)], s1_r.at[TENSOR - m])
    r_rows = pl.ds(pl.multiple_of(r_slot * 32, 32), 32)
    for m in range(NBLK):
        x = m // Z
        zz = t if x else lax.rem(z + m, Z)
        slot = home[8 if x else zz]
        own, which = lax.shift_right_logical(slot, 1), slot & 1
        lpick[m] = cand[own, which, 0]
        rpick[m] = cand[own, which, 1]
        r_dev = zz * 4 + r_to
        l_dev = zz * 4 + a
        send(rpick.at[m], rrows.at[x, r_rows], r2_s.at[m], r2_r.at[x, r_slot], (r_dev, t), r_dev != d)
        pl.when(r_dev == d)(functools.partial(keep, rrows, (x, r_rows), rpick, m))
        send(lpick.at[m], lfull.at[x, z, a], l2_s.at[m], l2_r.at[x, z], (l_dev, t), l_dev != d)
        pl.when(l_dev == d)(functools.partial(keep, lfull, (x, z, a), lpick, m))

    got(acts_of(a_par), at_r.at[0])
    send(acts_of(a_par), acts_of(a_par), at_s.at[2], at_r.at[2], (sib, t))
    for n, aa in enumerate((a_par, a_far)):
        for m in range(1, 4):
            got(piece_of(aa, lax.rem(x + 4 - m, 4)), yx_r.at[n, m])
    got(acts_of(a_far), at_r.at[2])

    e_off = lax.rem(z - t + Z, Z)
    e_far = (e_off > 1) & (e_off < 7)
    e_low = (e_off < 4) | ((e_off == 4) & (c == 0))
    e_via = at_z(jnp.where(e_low, t + 1, t - 1))

    def e_merge(sources, odd):
        for n in sources:
            got(erecv.at[n], ez_r.at[n])

        @pl.when(c == odd)
        def _():
            got(erecv.at[4], ez_r.at[4])

        @pl.when(c != odd)
        def _():
            erecv[4] = jnp.zeros((ROWS, QUART), BF)

        total = gacc[3] + erecv[4].astype(F32)
        for n in sources:
            total = total + erecv[n].astype(F32)
        zsend[3] = total.astype(BF)

    for n in range(NBLK):
        total = gacc[n] + product(n, 1 - yh)
        if n == 3:
            gacc[n] = total
            zsend[n] = total.astype(BF)
            send(zsend.at[n], erecv.at[e_off], ez_s.at[0], ez_r.at[e_off], (e_via, t), e_far)
        elif n == 0:
            zsend[n] = total.astype(BF)
            send(zsend.at[n], relay, z_s.at[n], z_r.at[4], (at_z(z + off_relay), t))
        elif n == 7:
            gacc[n] = total
        else:
            if n == 8:
                got(relay, z_r.at[4])
                total = total + relay[...].astype(F32)
            zsend[n] = total.astype(BF)
            send(
                zsend.at[n], zrecv.at[offs[n]], z_s.at[n], z_r.at[offs[n]],
                (at_z(z + offs[n]), t),
            )

    pl.when(e_off == 1)(functools.partial(e_merge, (2, 3), 0))
    pl.when(e_off == 7)(functools.partial(e_merge, (5, 6), 1))
    near = (e_off == 1) | (e_off == 7)
    send(zsend.at[3], erecv.at[e_off], ez_s.at[0], ez_r.at[e_off], (at_z(t), t), near)

    my_cols = pl.ds(pl.multiple_of(t * ROWS, ROWS), ROWS)

    def roots_in(x):
        for n in range(Z):
            source = 8 * quad + n
            rows = pl.ds(32 * n, 32)
            pl.when(source != d)(functools.partial(got, rrows.at[x, rows], r2_r.at[x, n]))
            pl.when(z != n)(functools.partial(got, lfull.at[x, n, a], l2_r.at[x, n]))
        rfull[x, :, my_cols] = rrows[x]

    def roots_out(x, when):
        for m in range(1, TENSOR):
            dev = diagonal(m) if x else (d, lax.rem(t + m, TENSOR))
            send(rrows.at[x], rfull.at[x, :, my_cols], r3_s.at[x, m], r3_r.at[x, m], dev, when)
        for m in range(1, QUADS):
            dev = (z * 4 + lax.rem(a + m, QUADS), t)
            send(lfull.at[x, :, a], lfull.at[x, :, a], l3_s.at[x, m], l3_r.at[x, m], dev, when)

    roots_in(0)
    roots_out(0, None)
    pl.when(home_z)(functools.partial(roots_in, 1))
    roots_out(1, home_z)

    cot_copy.wait()
    w_copy.wait()
    for i in range(NB):
        grad = jnp.zeros((ROWS, ROWS), F32)
        for j in range(NB):
            grad = grad + dot(cot[j], weight[i, j], ((1,), (1,)))
        normed = normed_s[i]
        sg = jax.nn.sigmoid(normed)
        cg = (grad * sg * (1.0 + normed * (1.0 - sg)) * gain[i:i + 1, :]).astype(BF)
        cg_b[i] = cg
        cgext[i, HALF:HALF + ROWS, :] = cg.astype(F32)
    send(cg_b.at[:, 0:HALF], cg_halo.at[1], ch_s.at[0], ch_r.at[1], dn, left_ok)
    send(cg_b.at[:, ROWS - HALF:ROWS], cg_halo.at[0], ch_s.at[1], ch_r.at[0], up, right_ok)

    def tap_grad(i, carry):
        cg = cgext[i, HALF:HALF + ROWS, :]
        for j in range(TAPS):
            terms = (cg * gext[i, j:j + ROWS, :]).reshape(ROWS // 8, 8, ROWS)
            row = jnp.sum(jnp.sum(terms, axis=0), axis=0, keepdims=True)
            kpart[j // HALF, i, j % HALF:j % HALF + 1, :] = row
        return carry

    lax.fori_loop(0, NB, tap_grad, 0)
    send(kpart.at[1 - c], kin1, k_s.at[0], k_r.at[0], (sib, t))

    def roots_all(x):
        for m in range(1, TENSOR):
            tt = lax.rem(t + m, TENSOR)
            cols = pl.ds(pl.multiple_of(tt * ROWS, ROWS), ROWS)
            got(rfull.at[x, :, cols], r3_r.at[x, TENSOR - m])
        for m in range(1, QUADS):
            got(lfull.at[x, :, lax.rem(a + m, QUADS)], l3_r.at[x, QUADS - m])
        for zz in range(Z):
            part = lfull[x, zz].reshape(ROWS, ROWS).astype(F32)
            lturn[x, :, ROWS * zz:ROWS * zz + ROWS] = part.T.astype(BF)

    def join(x):
        total = gacc[3 if x else 7]
        for n in range(Z):
            if x == 0 and n not in (0, 4):
                got(zrecv.at[n], z_r.at[n])
                total = total + zrecv[n].astype(F32)
            elif x == 1 and n in (1, 7):
                got(erecv.at[n], ez_r.at[n])
                total = total + erecv[n].astype(F32)
        gfull[x, quad] = total.astype(BF)

    par_quad = 2 * c + 1 - yh

    def quarters_out(x, when):
        mine = gfull.at[x, quad]
        send(mine, mine, c_s.at[x, 0], c_r.at[x, 0], (par, t), when)
        send(mine, mine, c_s.at[x, 1], c_r.at[x, 1], (sib, t), when)

    def quarters_on(x, when):
        his = gfull.at[x, par_quad]
        send(his, his, c_s.at[x, 2], c_r.at[x, 2], (sib, t), when)

    def quarters_in(x):
        got(gfull.at[x, 2 * (1 - c) + yh], c_r.at[x, 1])
        got(gfull.at[x, 2 * (1 - c) + 1 - yh], c_r.at[x, 2])

    join(0)
    quarters_out(0, None)
    pl.when(home_z)(functools.partial(join, 1))
    quarters_out(1, home_z)

    got(kin1, k_r.at[0])
    ksend2[...] = kpart[c] + kin1[...]
    send(ksend2, kin2, k_s.at[1], k_r.at[1], (par, t))

    roots_all(0)
    pl.when(home_z)(functools.partial(roots_all, 1))

    got(gfull.at[0, par_quad], c_r.at[0, 0])
    quarters_on(0, None)
    pl.when(home_z)(functools.partial(got, gfull.at[1, par_quad], c_r.at[1, 0]))
    quarters_on(1, home_z)
    quarters_in(0)

    def right(x):
        part = jnp.zeros((ROWS, QUART), F32)
        for q in range(QUADS):
            part = part + dot(gfull[x, q], rfull[x, :, QUART * q:QUART * q + QUART], ((1,), (1,)))
        wall[x, t] = (part * SHARE).astype(BF)

    right(0)
    for m in range(1, TENSOR):
        dev = (d, lax.rem(t + m, TENSOR))
        send(wall.at[0, t], wall.at[0, t], wt_s.at[0, m], wt_r.at[0, m], dev)

    @pl.when(home_z)
    def _():
        quarters_in(1)
        right(1)

    for m in range(1, TENSOR):
        send(wall.at[1, t], wall.at[1, t], wt_s.at[1, m], wt_r.at[1, m], diagonal(m), home_z)

    got(kin2, k_r.at[1])
    ksum[...] = ksend2[...] + kin2[...]
    for m in range(1, Z):
        send(ksum, kz.at[z], k_s.at[1 + m], k_r.at[1 + m], (at_z(z + m), t))
    kz[z] = ksum[...]

    rim(0, left_ok, ch_r, cg_halo, cgext, low)
    rim(1, right_ok, ch_r, cg_halo, cgext, high)

    for i in range(NB):
        total = jnp.zeros((ROWS, ROWS), F32)
        for j in range(TAPS):
            total = total + tapf[i, j:j + 1, :] * cgext[i, TAPS - j:TAPS - j + ROWS, :]
        lin, gate = halves(i)
        sg = jax.nn.sigmoid(gate)
        total = total * sg
        ggrad[:, i, 0, :] = total.astype(BF)
        ggrad[:, i, 1, :] = (total * lin * (1.0 - sg)).astype(BF)

    def quarter(block, q):
        cols = pl.ds(pl.multiple_of(q * QUART, QUART), QUART)
        return upd.at[lax.div(block, NB), lax.rem(block, NB), :, cols]

    def left_mult(x, block):
        for m in range(1, TENSOR):
            got(wall.at[x, lax.rem(t + m, TENSOR)], wt_r.at[x, TENSOR - m])
        part = dot(lturn[x], wall[x].reshape(BLOCK, QUART), ((1,), (0,)))
        quarter(block, quad)[...] = part.astype(BF)

    second = jnp.int32(Z)
    sib_quads = (2 * (1 - c) + yh, 2 * (1 - c) + 1 - yh)

    def piece(n, q):
        return quarter(second if n == Z else lax.rem(z + n, Z), q)

    def on(n, h, when=None):
        src = piece(n, par_quad if h else quad)
        if h == 0:
            send(src, src, uy_s.at[n], uy_r.at[n], (par, t), when)
        send(src, src, us_s.at[n, h], us_r.at[n, h], (sib, t), when)

    left_mult(0, z)
    for off in (3, 5, 2, 6, 1, 7):
        src = piece(0, quad)
        send(src, src, uz_s.at[off], uz_r.at[off], (at_z(z + off), t))
    on(0, 0)

    @pl.when(home_z)
    def _():
        left_mult(1, second)

    for off in (3, 5, 2, 6, 1, 7):
        src = piece(Z, quad)
        send(src, src, uz_s.at[Z + off], uz_r.at[Z], (at_z(z + off), t), home_z)

    for m in range(1, Z):
        got(kz.at[lax.rem(z + m, Z)], k_r.at[1 + Z - m])
    total = kz[0]
    for zz in range(1, Z):
        total = total + kz[zz]
    khalf[c] = total * SHARE
    send(khalf.at[c], khalf.at[c], k_s.at[9], k_r.at[9], (sib, t))

    def pass_on(n, land, when):
        src = piece(n, quad)
        send(src, src, uz_s.at[4 + land], uz_r.at[land], (at_z(z - 1 + 2 * c), t), when)

    for off in (3, 5, 2, 6, 1, 7):
        got(piece(off, quad), uz_r.at[Z - off])
        if off == 3:
            pass_on(3, 4, c == 0)
        if off == 5:
            pass_on(5, 4, c == 1)
        on(off, 0)
    pl.when(jnp.logical_not(home_z))(functools.partial(got, piece(Z, quad), uz_r.at[Z]))
    pass_on(Z, Z, lax.rem(t - z + Z, Z) == 3 + 2 * c)
    on(Z, 0)
    got(piece(4, quad), uz_r.at[4])
    on(4, 0)
    for n in (0, 3, 5, 2, 6, 1, 7, Z, 4):
        got(piece(n, par_quad), uy_r.at[n])
        on(n, 1)

    got(khalf.at[1 - c], k_r.at[9])
    for half in range(2):
        for i in range(NB):
            kgrad[i, HALF * half:HALF * half + HALF, :] = khalf[half, i]

    for n in range(Z + 1):
        for h in range(2):
            got(piece(n, sib_quads[h]), us_r.at[n, h])

    for copy, when in sends:
        if when is None:
            copy.wait_send()
        else:
            pl.when(when)(copy.wait_send)


def per_device(
    glu_input, conv_kernel, norm_gain, norm_shift, out_weight, out_cotangent, root_stack, home
):
    vmem = pl.BlockSpec(memory_space=pltpu.VMEM)
    hbm = pl.BlockSpec(memory_space=pltpu.HBM)
    dma = pltpu.SemaphoreType.DMA
    sq = (NB, ROWS, ROWS)
    out = pl.pallas_call(
        kernel,
        out_shape=(
            jax.ShapeDtypeStruct((NB, NB, ROWS, BLOCK), BF),
            jax.ShapeDtypeStruct((NB, TAPS, ROWS), F32),
            jax.ShapeDtypeStruct((ROWS, NB, 2, ROWS), BF),
        ),
        in_specs=[
            pl.BlockSpec(memory_space=pltpu.SMEM), hbm, hbm, hbm, hbm, vmem, vmem, vmem,
        ],
        out_specs=(vmem, vmem, vmem),
        scratch_shapes=[
            pltpu.VMEM((ROWS, NB, 2, ROWS), BF),
            pltpu.VMEM(sq, BF),
            pltpu.VMEM((NB, ROWS, BLOCK), BF),
            pltpu.VMEM((2, 2, 32, BLOCK), BF),
            pltpu.VMEM((NB, TAPS, ROWS), F32),
            pltpu.VMEM((TENSOR, 2, 2, 32, ROWS), BF),
            pltpu.VMEM((NBLK, 32, ROWS), BF),
            pltpu.VMEM((NBLK, 32, ROWS), BF),
            pltpu.VMEM((2, QUART, ROWS), BF),
            pltpu.VMEM((2, QUART, BLOCK), BF),
            pltpu.VMEM((2, Z, QUADS, 32, ROWS), BF),
            pltpu.VMEM((2, ROWS, BLOCK), BF),
            pltpu.VMEM((2, NB, HALF, ROWS), BF),
            pltpu.VMEM((2, NB, HALF, ROWS), BF),
            pltpu.VMEM((NB, ROWS + TAPS, ROWS), F32),
            pltpu.VMEM(sq, F32),
            pltpu.VMEM(sq, BF),
            pltpu.VMEM((NB, ROWS + TAPS, ROWS), F32),
            pltpu.VMEM((NB, NB, ROWS, BLOCK), BF),
            pltpu.VMEM((NB, ROWS, QUADS * ROWS), BF),
            pltpu.VMEM((NB, QUADS * ROWS, QUART), BF),
            pltpu.VMEM((NBLK, ROWS, QUART), F32),
            pltpu.VMEM((ROWS, QUART), BF),
            pltpu.VMEM((NBLK, ROWS, QUART), BF),
            pltpu.VMEM((Z, ROWS, QUART), BF),
            pltpu.VMEM((Z, ROWS, QUART), BF),
            pltpu.VMEM((2, QUADS, ROWS, QUART), BF),
            pltpu.VMEM((2, TENSOR, ROWS, QUART), BF),
            pltpu.VMEM((2, NB, HALF, ROWS), F32),
            pltpu.VMEM((NB, HALF, ROWS), F32),
            pltpu.VMEM((NB, HALF, ROWS), F32),
            pltpu.VMEM((NB, HALF, ROWS), F32),
            pltpu.VMEM((NB, HALF, ROWS), F32),
            pltpu.VMEM((Z, NB, HALF, ROWS), F32),
            pltpu.VMEM((2, NB, HALF, ROWS), F32),
            dma, dma, dma, dma,
            dma((2,)), dma((2,)),
            dma((8,)), dma((8,)),
            dma((9,)), dma((2, 8)),
            dma((9,)), dma((2, 8)),
            dma((2, 8)), dma((2, 8)),
            dma((2, 4)), dma((2, 4)),
            dma((2,)), dma((2,)),
            dma((1,)), dma((1,)),
            dma((2, 4)), dma((2, 4)),
            dma((3,)), dma((3,)),
            dma,
            dma((9,)), dma((8,)),
            dma((1,)), dma((8,)),
            dma((2, 3)), dma((2, 3)),
            dma((2, 8)), dma((2, 8)),
            dma((16,)), dma((9,)),
            dma((9,)), dma((9,)),
            dma((9, 2)), dma((9, 2)),
            dma((2,)), dma((2,)),
            dma((10,)), dma((10,)),
        ],
        compiler_params=pltpu.CompilerParams(
            collective_id=0, has_side_effects=True, vmem_limit_bytes=60 * 2**20
        ),
    )(
        home, glu_input.transpose(0, 2, 1, 3), out_weight.transpose(0, 2, 1, 3), out_cotangent.transpose(1, 0, 2),
        root_stack, conv_kernel.transpose(1, 0, 2), norm_gain, norm_shift,
    )
    update, kernel_grad, glu_grad = out
    return glu_grad.transpose(0, 2, 1, 3), kernel_grad.transpose(1, 0, 2), update.transpose(0, 2, 1, 3)


def solution(mesh):
    placed = (
        P("dp", None, None, "tensor"),
        P(None, None, "tensor"),
        P(None, "tensor"),
        P(None, "tensor"),
        P(None, "tensor", None, None),
        P("dp", None, None),
        P("tensor", None, "dp", None),
        P(),
    )
    return jax.shard_map(
        per_device,
        mesh=mesh,
        in_specs=placed,
        out_specs=(
            P("dp", None, None, "tensor"),
            P(None, None, "tensor"),
            P(None, "tensor", None, None),
        ),
        check_vma=False,
    )
```

```python
import functools

import jax
import jax.numpy as jnp
from jax import lax
from jax.experimental import pallas as pl
from jax.experimental.pallas import tpu as pltpu
from jax.sharding import PartitionSpec as P

LEN = 2048
MESH = pl.DeviceIdType.MESH
BF = jnp.bfloat16
F32 = jnp.float32

Z = 8
QUADS = 4
TENSOR = 8
TAPS = 32
HALF = TAPS // 2
ROWS = 128
BLOCK = 1024
NB = 3
NBLK = 9
QUART = BLOCK // 4
SHARE = LEN / (ROWS * Z * QUADS)

ORDER = (4, 3, 5, 2, 6, 1, 7, 0)
SPOT = {off: k for k, off in enumerate(ORDER)}
HOPS = ((4, 3), (3, 4))


def dot(a, b, dims):
    return lax.dot_general(a, b, (dims, ((), ())), preferred_element_type=F32)


def keep(dst, at, src, m):
    dst[at] = src[m]


def kernel(
    home, glu_hbm, weight_hbm, cot_hbm, roots_hbm, taps, gain, shift,
    upd, kgrad, ggrad,
    raw, glu, cot, roots, tapf, cand, rpick, lpick, rrows, rfull, lfull, lturn,
    halo, cg_halo, gext, normed_s, cg_b, cgext, weight,
    acts, ycols, gacc, relay, zsend, zrecv, erecv, gfull, wall,
    kpart, kin1, ksend2, kin2, ksum, kz, khalf,
    raw_sem, w_sem, cot_sem, roots_sem, halo_s, halo_r, s1_s, s1_r, r2_s, r2_r, l2_s, l2_r,
    r3_s, r3_r, l3_s, l3_r, yc_s, yc_r, ys_s, ys_r, yx_s, yx_r, at_s, at_r, yc_own, z_s, z_r, ez_s, ez_r,
    c_s, c_r, wt_s, wt_r, uz_s, uz_r, uy_s, uy_r, us_s, us_r, ch_s, ch_r, k_s, k_r,
):
    d = lax.axis_index("dp")
    t = lax.axis_index("tensor")
    z = lax.div(d, 4)
    a = lax.rem(d, 4)
    yh = lax.div(a, 2)
    c = lax.rem(a, 2)
    sib = d + 1 - 2 * c
    par = d + 2 - 4 * yh

    def at_z(zz):
        return lax.rem(zz + 2 * Z, Z) * 4 + a

    quad = 2 * c + yh
    home_z = z == t

    def diagonal(m):
        tt = lax.rem(t + m, TENSOR)
        return (tt * 4 + a, tt)

    sends = []

    def send(src, dst, ss, rs, dev, when=None):
        copy = pltpu.make_async_remote_copy(
            src_ref=src, dst_ref=dst, send_sem=ss, recv_sem=rs,
            device_id=dev, device_id_type=MESH,
        )
        if when is None:
            copy.start()
        else:
            pl.when(when)(copy.start)
        sends.append((copy, when))

    def got(dst, rs):
        pltpu.make_async_remote_copy(
            src_ref=dst, dst_ref=dst, send_sem=s1_s.at[0], recv_sem=rs,
            device_id=(sib, t), device_id_type=MESH,
        ).wait_recv()

    barrier = pltpu.get_barrier_semaphore()

    def hello(dev):
        pl.semaphore_signal(barrier, inc=1, device_id=dev, device_id_type=MESH)

    hello((lax.rem(d + 31, 32), t))
    hello((lax.rem(d + 1, 32), t))
    for m in range(1, 4):
        hello((z * 4 + lax.rem(a + m, 4), t))
    for m in range(1, Z):
        hello((at_z(z + m), t))
    for m in range(1, TENSOR):
        hello((d, lax.rem(t + m, TENSOR)))

    r_quad = lax.div(z, 2)
    r_to = lax.rem(r_quad, 2) * 2 + lax.div(r_quad, 2)
    r_slot = lax.rem(z, 2) * 4 + a

    for n in range(Z):
        pl.when(8 * quad + n != d)(functools.partial(hello, (8 * quad + n, t)))
    for m in range(1, TENSOR):
        pl.when(home_z)(functools.partial(hello, diagonal(m)))

    raw_copy = pltpu.make_async_copy(glu_hbm, raw, raw_sem)
    raw_copy.start()
    roots_copy = pltpu.make_async_copy(roots_hbm, roots, roots_sem)
    roots_copy.start()
    cot_copy = pltpu.make_async_copy(cot_hbm, cot, cot_sem)
    cot_copy.start()
    w_copy = pltpu.make_async_copy(weight_hbm, weight, w_sem)
    w_copy.start()

    left_ok = (d != 0) & (lax.rem(d * ROWS + LEN // 2, LEN) != 0)
    right_ok = (d != 31) & (lax.rem((d + 1) * ROWS + LEN // 2, LEN) != 0)
    raw_copy.wait()

    def halves(i):
        both = raw[:, i].astype(F32)
        return both[:, 0, :], both[:, 1, :]

    for i in range(NB):
        lin, gate = halves(i)
        glu[i] = (lin * jax.nn.sigmoid(gate)).astype(BF)
        gext[i, HALF:HALF + ROWS, :] = glu[i].astype(F32)
        tapf[i] = taps[i].astype(F32)

    more = jnp.where(home_z, TENSOR - 1, 0) - jnp.where(r_to == a, 1, 0)
    pl.semaphore_wait(barrier, 2 + 3 + Z - 1 + TENSOR - 1 + Z + more)

    dn, up = (lax.rem(d + 31, 32), t), (lax.rem(d + 1, 32), t)
    send(glu.at[:, 0:HALF], halo.at[1], halo_s.at[0], halo_r.at[1], dn, left_ok)
    send(glu.at[:, ROWS - HALF:ROWS], halo.at[0], halo_s.at[1], halo_r.at[0], up, right_ok)
    roots_copy.wait()
    def quad_of(aa):
        return 2 * lax.rem(aa, 2) + lax.div(aa, 2)

    def quad_cols(aa):
        return pl.ds(pl.multiple_of(quad_of(aa) * QUART, QUART), QUART)

    def frames_of(aa):
        return pl.ds(pl.multiple_of(aa * ROWS, ROWS), ROWS)

    my_frames = frames_of(a)
    y_own = pltpu.make_async_copy(cot_hbm.at[:, :, quad_cols(a)], ycols.at[:, my_frames], yc_own)
    y_own.start()
    a_par, a_sib, a_far = a + 2 - 4 * yh, a + 1 - 2 * c, 3 - a
    my_x = lax.rem(t, 4)

    def piece_of(aa, xx):
        rows = pl.ds(pl.multiple_of(aa * ROWS + xx * 32, 32), 32)
        return ycols.at[:, rows]

    x_rows = pl.ds(pl.multiple_of(my_x * 32, 32), 32)
    for n, aa in enumerate((a_par, a_far)):
        src = cot_hbm.at[:, x_rows, quad_cols(aa)]
        send(src, piece_of(a, my_x), yc_s.at[n], yc_r.at[n], (z * 4 + aa, t))
    src = cot_hbm.at[:, :, quad_cols(a_sib)]
    send(src, ycols.at[:, my_frames], ys_s.at[0], ys_r.at[0], (sib, t))

    for m in range(1, TENSOR):
        tt = lax.rem(t + m, TENSOR)
        share_cols = pl.ds(pl.multiple_of(tt * ROWS, ROWS), ROWS)
        send(roots.at[:, :, :, share_cols], cand.at[t], s1_s.at[m], s1_r.at[m], (d, tt))
    cand[t] = roots[:, :, :, pl.ds(pl.multiple_of(t * ROWS, ROWS), ROWS)]

    def rim(side, ok, sem, src, dst, rows):
        @pl.when(ok)
        def _():
            got(src.at[side], sem.at[side])
            for i in range(NB):
                dst[i, rows, :] = src[side, i].astype(F32)

        @pl.when(jnp.logical_not(ok))
        def _():
            for i in range(NB):
                dst[i, rows, :] = jnp.zeros((HALF, ROWS), F32)

    low, high = pl.ds(0, HALF), pl.ds(HALF + ROWS, HALF)
    rim(0, left_ok, halo_r, halo, gext, low)
    rim(1, right_ok, halo_r, halo, gext, high)

    for n, aa in enumerate((a_par, a_far)):
        src = piece_of(aa, my_x)
        got(src, yc_r.at[n])
        for m in range(1, 4):
            dev = (d, t - my_x + lax.rem(my_x + m, 4))
            send(src, src, yx_s.at[n, m], yx_r.at[n, m], dev)

    def conv(i, carry):
        total = jnp.zeros((ROWS, ROWS), F32)
        for j in range(TAPS):
            total = total + tapf[i, j:j + 1, :] * gext[i, j:j + ROWS, :]
        normed = total * gain[pl.ds(i, 1), :] + shift[pl.ds(i, 1), :]
        normed_s[i] = normed
        acts[i, :, my_frames] = (normed * jax.nn.sigmoid(normed)).T.astype(BF)
        return carry

    lax.fori_loop(0, NB, conv, 0)


    def acts_of(aa):
        return acts.at[:, :, frames_of(aa)]

    send(acts_of(a), acts_of(a), at_s.at[0], at_r.at[0], (par, t))
    send(acts_of(a), acts_of(a), at_s.at[1], at_r.at[1], (sib, t))

    for m in range(1, TENSOR):
        got(cand.at[lax.rem(t + m, TENSOR)], s1_r.at[TENSOR - m])
    r_rows = pl.ds(pl.multiple_of(r_slot * 32, 32), 32)
    for m in range(NBLK):
        x = m // Z
        zz = t if x else lax.rem(z + m, Z)
        slot = home[8 if x else zz]
        own, which = lax.shift_right_logical(slot, 1), slot & 1
        lpick[m] = cand[own, which, 0]
        rpick[m] = cand[own, which, 1]
        r_dev = zz * 4 + r_to
        l_dev = zz * 4 + a
        send(rpick.at[m], rrows.at[x, r_rows], r2_s.at[m], r2_r.at[x, r_slot], (r_dev, t), r_dev != d)
        pl.when(r_dev == d)(functools.partial(keep, rrows, (x, r_rows), rpick, m))
        send(lpick.at[m], lfull.at[x, z, a], l2_s.at[m], l2_r.at[x, z], (l_dev, t), l_dev != d)
        pl.when(l_dev == d)(functools.partial(keep, lfull, (x, z, a), lpick, m))

    off_relay, off_plain = 2 + 4 * c, 6 - 4 * c
    offs = (4, 3, 5, None, off_plain, 1, 7, 0, off_relay)

    def product(n, chip):
        block = Z if n == 3 else lax.rem(z + offs[n], Z)
        row, col = (2, 2) if n == 3 else (lax.div(block, NB), lax.rem(block, NB))
        span = pl.ds(pl.multiple_of(chip * 256, 256), 256)
        return dot(acts[row, :, span], ycols[col, span, :], ((1,), (0,)))

    y_own.wait()
    got(ycols.at[:, frames_of(a_sib)], ys_r.at[0])
    got(acts_of(a_sib), at_r.at[1])
    for n in range(NBLK):
        gacc[n] = product(n, yh)

    got(acts_of(a_par), at_r.at[0])
    send(acts_of(a_par), acts_of(a_par), at_s.at[2], at_r.at[2], (sib, t))
    for n, aa in enumerate((a_par, a_far)):
        for m in range(1, 4):
            got(piece_of(aa, lax.rem(my_x + 4 - m, 4)), yx_r.at[n, m])
    got(acts_of(a_far), at_r.at[2])

    e_off = lax.rem(z - t + Z, Z)
    e_far = (e_off > 1) & (e_off < 7)
    e_low = (e_off < 4) | ((e_off == 4) & (c == 0))
    e_via = at_z(jnp.where(e_low, t + 1, t - 1))

    def e_merge(sources, odd):
        for n in sources:
            got(erecv.at[n], ez_r.at[n])

        @pl.when(c == odd)
        def _():
            got(erecv.at[4], ez_r.at[4])

        @pl.when(c != odd)
        def _():
            erecv[4] = jnp.zeros((ROWS, QUART), BF)

        total = gacc[3] + erecv[4].astype(F32)
        for n in sources:
            total = total + erecv[n].astype(F32)
        zsend[3] = total.astype(BF)

    my_cols = pl.ds(pl.multiple_of(t * ROWS, ROWS), ROWS)

    def roots_in(x):
        for n in range(Z):
            source = 8 * quad + n
            rows = pl.ds(32 * n, 32)
            pl.when(source != d)(functools.partial(got, rrows.at[x, rows], r2_r.at[x, n]))
            pl.when(z != n)(functools.partial(got, lfull.at[x, n, a], l2_r.at[x, n]))
        rfull[x, :, my_cols] = rrows[x]

    def roots_out(x, when):
        for m in range(1, TENSOR):
            dev = diagonal(m) if x else (d, lax.rem(t + m, TENSOR))
            send(rrows.at[x], rfull.at[x, :, my_cols], r3_s.at[x, m], r3_r.at[x, m], dev, when)
        mine = lfull.at[x, :, a]
        send(mine, mine, l3_s.at[x, 0], l3_r.at[x, 0], (par, t), when)
        send(mine, mine, l3_s.at[x, 1], l3_r.at[x, 1], (sib, t), when)

    def left_on(x, when):
        his = lfull.at[x, :, a_par]
        if when is None:
            got(his, l3_r.at[x, 0])
        else:
            pl.when(when)(functools.partial(got, his, l3_r.at[x, 0]))
        send(his, his, l3_s.at[x, 2], l3_r.at[x, 2], (sib, t), when)

    for n in range(NBLK):
        if n == 3:
            roots_in(0)
            roots_out(0, None)
            pl.when(home_z)(functools.partial(roots_in, 1))
            roots_out(1, home_z)
        total = gacc[n] + product(n, 1 - yh)
        if n == 3:
            gacc[n] = total
            zsend[n] = total.astype(BF)
            send(zsend.at[n], erecv.at[e_off], ez_s.at[0], ez_r.at[e_off], (e_via, t), e_far)
        elif n == 0:
            zsend[n] = total.astype(BF)
            send(zsend.at[n], relay, z_s.at[n], z_r.at[4], (at_z(z + off_relay), t))
        elif n == 7:
            gacc[n] = total
        else:
            if n == 8:
                got(relay, z_r.at[4])
                total = total + relay[...].astype(F32)
            zsend[n] = total.astype(BF)
            send(
                zsend.at[n], zrecv.at[offs[n]], z_s.at[n], z_r.at[offs[n]],
                (at_z(z + offs[n]), t),
            )

    pl.when(e_off == 1)(functools.partial(e_merge, (2, 3), 0))
    pl.when(e_off == 7)(functools.partial(e_merge, (5, 6), 1))
    near = (e_off == 1) | (e_off == 7)
    send(zsend.at[3], erecv.at[e_off], ez_s.at[0], ez_r.at[e_off], (at_z(t), t), near)

    cot_copy.wait()
    w_copy.wait()
    for i in range(NB):
        grad = jnp.zeros((ROWS, ROWS), F32)
        for j in range(NB):
            grad = grad + dot(cot[j], weight[i, j], ((1,), (1,)))
        normed = normed_s[i]
        sg = jax.nn.sigmoid(normed)
        cg = (grad * sg * (1.0 + normed * (1.0 - sg)) * gain[i:i + 1, :]).astype(BF)
        cg_b[i] = cg
        cgext[i, HALF:HALF + ROWS, :] = cg.astype(F32)
    send(cg_b.at[:, 0:HALF], cg_halo.at[1], ch_s.at[0], ch_r.at[1], dn, left_ok)
    send(cg_b.at[:, ROWS - HALF:ROWS], cg_halo.at[0], ch_s.at[1], ch_r.at[0], up, right_ok)

    left_on(0, None)
    left_on(1, home_z)

    def tap_grad(i, carry):
        cg = cgext[i, HALF:HALF + ROWS, :]
        for j in range(TAPS):
            terms = (cg * gext[i, j:j + ROWS, :]).reshape(ROWS // 8, 8, ROWS)
            row = jnp.sum(jnp.sum(terms, axis=0), axis=0, keepdims=True)
            kpart[j // HALF, i, j % HALF:j % HALF + 1, :] = row
        return carry

    lax.fori_loop(0, NB, tap_grad, 0)
    send(kpart.at[1 - c], kin1, k_s.at[0], k_r.at[0], (sib, t))

    def roots_all(x):
        for m in range(1, TENSOR):
            tt = lax.rem(t + m, TENSOR)
            cols = pl.ds(pl.multiple_of(tt * ROWS, ROWS), ROWS)
            got(rfull.at[x, :, cols], r3_r.at[x, TENSOR - m])
        got(lfull.at[x, :, a_sib], l3_r.at[x, 1])
        got(lfull.at[x, :, a_far], l3_r.at[x, 2])
        for zz in range(Z):
            part = lfull[x, zz].reshape(ROWS, ROWS).astype(F32)
            lturn[x, :, ROWS * zz:ROWS * zz + ROWS] = part.T.astype(BF)

    def join(x):
        total = gacc[3 if x else 7]
        for n in range(Z):
            if x == 0 and n not in (0, 4):
                got(zrecv.at[n], z_r.at[n])
                total = total + zrecv[n].astype(F32)
            elif x == 1 and n in (1, 7):
                got(erecv.at[n], ez_r.at[n])
                total = total + erecv[n].astype(F32)
        gfull[x, quad] = total.astype(BF)

    par_quad = 2 * c + 1 - yh

    def quarters_out(x, when):
        mine = gfull.at[x, quad]
        send(mine, mine, c_s.at[x, 0], c_r.at[x, 0], (par, t), when)
        send(mine, mine, c_s.at[x, 1], c_r.at[x, 1], (sib, t), when)

    def quarters_on(x, when):
        his = gfull.at[x, par_quad]
        send(his, his, c_s.at[x, 2], c_r.at[x, 2], (sib, t), when)

    def quarters_in(x):
        got(gfull.at[x, 2 * (1 - c) + yh], c_r.at[x, 1])
        got(gfull.at[x, 2 * (1 - c) + 1 - yh], c_r.at[x, 2])

    join(0)
    quarters_out(0, None)
    pl.when(home_z)(functools.partial(join, 1))
    quarters_out(1, home_z)

    got(kin1, k_r.at[0])
    ksend2[...] = kpart[c] + kin1[...]
    send(ksend2, kin2, k_s.at[1], k_r.at[1], (par, t))

    roots_all(0)
    pl.when(home_z)(functools.partial(roots_all, 1))

    got(gfull.at[0, par_quad], c_r.at[0, 0])
    quarters_on(0, None)
    pl.when(home_z)(functools.partial(got, gfull.at[1, par_quad], c_r.at[1, 0]))
    quarters_on(1, home_z)
    quarters_in(0)

    def right(x):
        part = jnp.zeros((ROWS, QUART), F32)
        for q in range(QUADS):
            part = part + dot(gfull[x, q], rfull[x, :, QUART * q:QUART * q + QUART], ((1,), (1,)))
        wall[x, t] = (part * SHARE).astype(BF)

    right(0)
    for m in range(1, TENSOR):
        dev = (d, lax.rem(t + m, TENSOR))
        send(wall.at[0, t], wall.at[0, t], wt_s.at[0, m], wt_r.at[0, m], dev)

    @pl.when(home_z)
    def _():
        quarters_in(1)
        right(1)

    for m in range(1, TENSOR):
        send(wall.at[1, t], wall.at[1, t], wt_s.at[1, m], wt_r.at[1, m], diagonal(m), home_z)

    got(kin2, k_r.at[1])
    ksum[...] = ksend2[...] + kin2[...]
    for m in range(1, Z):
        send(ksum, kz.at[z], k_s.at[1 + m], k_r.at[1 + m], (at_z(z + m), t))
    kz[z] = ksum[...]

    rim(0, left_ok, ch_r, cg_halo, cgext, low)
    rim(1, right_ok, ch_r, cg_halo, cgext, high)

    for i in range(NB):
        total = jnp.zeros((ROWS, ROWS), F32)
        for j in range(TAPS):
            total = total + tapf[i, j:j + 1, :] * cgext[i, TAPS - j:TAPS - j + ROWS, :]
        lin, gate = halves(i)
        sg = jax.nn.sigmoid(gate)
        total = total * sg
        ggrad[:, i, 0, :] = total.astype(BF)
        ggrad[:, i, 1, :] = (total * lin * (1.0 - sg)).astype(BF)

    def quarter(block, q):
        cols = pl.ds(pl.multiple_of(q * QUART, QUART), QUART)
        return upd.at[lax.div(block, NB), lax.rem(block, NB), :, cols]

    def left_mult(x, block):
        for m in range(1, TENSOR):
            got(wall.at[x, lax.rem(t + m, TENSOR)], wt_r.at[x, TENSOR - m])
        part = dot(lturn[x], wall[x].reshape(BLOCK, QUART), ((1,), (0,)))
        quarter(block, quad)[...] = part.astype(BF)

    second = jnp.int32(Z)
    sib_quads = (2 * (1 - c) + yh, 2 * (1 - c) + 1 - yh)

    def piece(n, q):
        return quarter(second if n == Z else lax.rem(z + n, Z), q)

    def on(n, h, when=None):
        src = piece(n, par_quad if h else quad)
        if h == 0:
            send(src, src, uy_s.at[n], uy_r.at[n], (par, t), when)
        send(src, src, us_s.at[n, h], us_r.at[n, h], (sib, t), when)

    left_mult(0, z)
    for off in (1, 7, 3, 5, 2, 6):
        src = piece(0, quad)
        send(src, src, uz_s.at[off], uz_r.at[off], (at_z(z + off), t))
    on(0, 0)

    @pl.when(home_z)
    def _():
        left_mult(1, second)

    for off in (1, 7, 3, 5, 2, 6):
        src = piece(Z, quad)
        send(src, src, uz_s.at[Z + off], uz_r.at[Z], (at_z(z + off), t), home_z)

    for m in range(1, Z):
        got(kz.at[lax.rem(z + m, Z)], k_r.at[1 + Z - m])
    total = kz[0]
    for zz in range(1, Z):
        total = total + kz[zz]
    khalf[c] = total * SHARE
    send(khalf.at[c], khalf.at[c], k_s.at[9], k_r.at[9], (sib, t))

    def pass_on(n, land, when):
        src = piece(n, quad)
        send(src, src, uz_s.at[4 + land], uz_r.at[land], (at_z(z - 1 + 2 * c), t), when)

    for off in (1, 7, 3, 5, 2, 6):
        got(piece(off, quad), uz_r.at[Z - off])
        if off == 3:
            pass_on(3, 4, c == 0)
        if off == 5:
            pass_on(5, 4, c == 1)
        on(off, 0)
    pl.when(jnp.logical_not(home_z))(functools.partial(got, piece(Z, quad), uz_r.at[Z]))
    pass_on(Z, Z, lax.rem(t - z + Z, Z) == 3 + 2 * c)
    on(Z, 0)
    got(piece(4, quad), uz_r.at[4])
    on(4, 0)
    for n in (0, 1, 7, 3, 5, 2, 6, Z, 4):
        got(piece(n, par_quad), uy_r.at[n])
        on(n, 1)

    got(khalf.at[1 - c], k_r.at[9])
    for half in range(2):
        for i in range(NB):
            kgrad[i, HALF * half:HALF * half + HALF, :] = khalf[half, i]

    for n in range(Z + 1):
        for h in range(2):
            got(piece(n, sib_quads[h]), us_r.at[n, h])

    for copy, when in sends:
        if when is None:
            copy.wait_send()
        else:
            pl.when(when)(copy.wait_send)


def hand_over(upd, kgrad, ggrad, upd_out, kgrad_out, ggrad_out, sems):
    copies = [
        pltpu.make_async_copy(kgrad, kgrad_out, sems.at[NBLK]),
        pltpu.make_async_copy(ggrad, ggrad_out, sems.at[NBLK + 1]),
    ]
    for b in range(NBLK):
        at = (b // NB, b % NB)
        copies.append(pltpu.make_async_copy(upd.at[at], upd_out.at[at], sems.at[b]))
    for copy in copies:
        copy.start()
    for copy in copies:
        copy.wait()


def per_device(
    glu_input, conv_kernel, norm_gain, norm_shift, out_weight, out_cotangent, root_stack, home
):
    vmem = pl.BlockSpec(memory_space=pltpu.VMEM)
    hbm = pl.BlockSpec(memory_space=pltpu.HBM)
    dma = pltpu.SemaphoreType.DMA
    sq = (NB, ROWS, ROWS)
    out = pl.pallas_call(
        kernel,
        out_shape=(
            jax.ShapeDtypeStruct((NB, NB, ROWS, BLOCK), BF),
            jax.ShapeDtypeStruct((NB, TAPS, ROWS), F32),
            jax.ShapeDtypeStruct((ROWS, NB, 2, ROWS), BF),
        ),
        in_specs=[
            pl.BlockSpec(memory_space=pltpu.SMEM), hbm, hbm, hbm, hbm, vmem, vmem, vmem,
        ],
        out_specs=(vmem, vmem, vmem),
        scratch_shapes=[
            pltpu.VMEM((ROWS, NB, 2, ROWS), BF),
            pltpu.VMEM(sq, BF),
            pltpu.VMEM((NB, ROWS, BLOCK), BF),
            pltpu.VMEM((2, 2, 32, BLOCK), BF),
            pltpu.VMEM((NB, TAPS, ROWS), F32),
            pltpu.VMEM((TENSOR, 2, 2, 32, ROWS), BF),
            pltpu.VMEM((NBLK, 32, ROWS), BF),
            pltpu.VMEM((NBLK, 32, ROWS), BF),
            pltpu.VMEM((2, QUART, ROWS), BF),
            pltpu.VMEM((2, QUART, BLOCK), BF),
            pltpu.VMEM((2, Z, QUADS, 32, ROWS), BF),
            pltpu.VMEM((2, ROWS, BLOCK), BF),
            pltpu.VMEM((2, NB, HALF, ROWS), BF),
            pltpu.VMEM((2, NB, HALF, ROWS), BF),
            pltpu.VMEM((NB, ROWS + TAPS, ROWS), F32),
            pltpu.VMEM(sq, F32),
            pltpu.VMEM(sq, BF),
            pltpu.VMEM((NB, ROWS + TAPS, ROWS), F32),
            pltpu.VMEM((NB, NB, ROWS, BLOCK), BF),
            pltpu.VMEM((NB, ROWS, QUADS * ROWS), BF),
            pltpu.VMEM((NB, QUADS * ROWS, QUART), BF),
            pltpu.VMEM((NBLK, ROWS, QUART), F32),
            pltpu.VMEM((ROWS, QUART), BF),
            pltpu.VMEM((NBLK, ROWS, QUART), BF),
            pltpu.VMEM((Z, ROWS, QUART), BF),
            pltpu.VMEM((Z, ROWS, QUART), BF),
            pltpu.VMEM((2, QUADS, ROWS, QUART), BF),
            pltpu.VMEM((2, TENSOR, ROWS, QUART), BF),
            pltpu.VMEM((2, NB, HALF, ROWS), F32),
            pltpu.VMEM((NB, HALF, ROWS), F32),
            pltpu.VMEM((NB, HALF, ROWS), F32),
            pltpu.VMEM((NB, HALF, ROWS), F32),
            pltpu.VMEM((NB, HALF, ROWS), F32),
            pltpu.VMEM((Z, NB, HALF, ROWS), F32),
            pltpu.VMEM((2, NB, HALF, ROWS), F32),
            dma, dma, dma, dma,
            dma((2,)), dma((2,)),
            dma((8,)), dma((8,)),
            dma((9,)), dma((2, 8)),
            dma((9,)), dma((2, 8)),
            dma((2, 8)), dma((2, 8)),
            dma((2, 4)), dma((2, 4)),
            dma((2,)), dma((2,)),
            dma((1,)), dma((1,)),
            dma((2, 4)), dma((2, 4)),
            dma((3,)), dma((3,)),
            dma,
            dma((9,)), dma((8,)),
            dma((1,)), dma((8,)),
            dma((2, 3)), dma((2, 3)),
            dma((2, 8)), dma((2, 8)),
            dma((16,)), dma((9,)),
            dma((9,)), dma((9,)),
            dma((9, 2)), dma((9, 2)),
            dma((2,)), dma((2,)),
            dma((10,)), dma((10,)),
        ],
        compiler_params=pltpu.CompilerParams(
            collective_id=0, has_side_effects=True, vmem_limit_bytes=60 * 2**20
        ),
    )(
        home, glu_input.transpose(0, 2, 1, 3), out_weight.transpose(0, 2, 1, 3), out_cotangent.transpose(1, 0, 2),
        root_stack, conv_kernel.transpose(1, 0, 2), norm_gain, norm_shift,
    )
    update, kernel_grad, glu_grad = pl.pallas_call(
        hand_over,
        out_shape=[jax.ShapeDtypeStruct(x.shape, x.dtype) for x in out],
        in_specs=[hbm] * 3,
        out_specs=[hbm] * 3,
        scratch_shapes=[dma((NBLK + 2,))],
        compiler_params=pltpu.CompilerParams(vmem_limit_bytes=60 * 2**20),
    )(*out)
    return glu_grad.transpose(0, 2, 1, 3), kernel_grad.transpose(1, 0, 2), update.transpose(0, 2, 1, 3)


def solution(mesh):
    placed = (
        P("dp", None, None, "tensor"),
        P(None, None, "tensor"),
        P(None, "tensor"),
        P(None, "tensor"),
        P(None, "tensor", None, None),
        P("dp", None, None),
        P("tensor", None, "dp", None),
        P(),
    )
    return jax.shard_map(
        per_device,
        mesh=mesh,
        in_specs=placed,
        out_specs=(
            P("dp", None, None, "tensor"),
            P(None, None, "tensor"),
            P(None, "tensor", None, None),
        ),
        check_vma=False,
    )
```

```python
import functools

import jax
import jax.numpy as jnp
from jax import lax
from jax.experimental import pallas as pl
from jax.experimental.pallas import tpu as pltpu
from jax.sharding import PartitionSpec as P

LEN = 2048
MESH = pl.DeviceIdType.MESH
BF = jnp.bfloat16
F32 = jnp.float32

Z = 8
QUADS = 4
TENSOR = 8
TAPS = 32
HALF = TAPS // 2
ROWS = 128
BLOCK = 1024
NB = 3
NBLK = 9
QUART = BLOCK // 4
SHARE = LEN / (ROWS * Z * QUADS)

ORDER = (4, 3, 5, 2, 6, 1, 7, 0)
SPOT = {off: k for k, off in enumerate(ORDER)}
HOPS = ((4, 3), (3, 4))


def dot(a, b, dims):
    return lax.dot_general(a, b, (dims, ((), ())), preferred_element_type=F32)


def keep(dst, at, src, m):
    dst[at] = src[m]


def kernel(
    home, glu_hbm, weight_hbm, cot_hbm, roots_hbm, taps, gain, shift,
    upd, kgrad, ggrad,
    raw, glu, cot, roots, tapf, cand, rpick, lpick, rrows, rfull, lfull, lturn,
    halo, cg_halo, gext, normed_s, cg_b, cgext, weight,
    acts, ycols, gacc, relay, zsend, zrecv, erecv, gfull, wall,
    kpart, kin1, ksend2, kin2, ksum, kz, khalf,
    raw_sem, w_sem, cot_sem, roots_sem, halo_s, halo_r, s1_s, s1_r, r2_s, r2_r, l2_s, l2_r,
    r3_s, r3_r, l3_s, l3_r, yc_s, yc_r, ys_s, ys_r, yx_s, yx_r, at_s, at_r, yc_own, z_s, z_r, ez_s, ez_r,
    c_s, c_r, wt_s, wt_r, uz_s, uz_r, uy_s, uy_r, us_s, us_r, ch_s, ch_r, k_s, k_r,
):
    d = lax.axis_index("dp")
    t = lax.axis_index("tensor")
    z = lax.div(d, 4)
    a = lax.rem(d, 4)
    yh = lax.div(a, 2)
    c = lax.rem(a, 2)
    sib = d + 1 - 2 * c
    par = d + 2 - 4 * yh

    def at_z(zz):
        return lax.rem(zz + 2 * Z, Z) * 4 + a

    quad = 2 * c + yh
    home_z = z == t

    def diagonal(m):
        tt = lax.rem(t + m, TENSOR)
        return (tt * 4 + a, tt)

    sends = []

    def send(src, dst, ss, rs, dev, when=None):
        copy = pltpu.make_async_remote_copy(
            src_ref=src, dst_ref=dst, send_sem=ss, recv_sem=rs,
            device_id=dev, device_id_type=MESH,
        )
        if when is None:
            copy.start()
        else:
            pl.when(when)(copy.start)
        sends.append((copy, when))

    def got(dst, rs):
        pltpu.make_async_remote_copy(
            src_ref=dst, dst_ref=dst, send_sem=s1_s.at[0], recv_sem=rs,
            device_id=(sib, t), device_id_type=MESH,
        ).wait_recv()

    barrier = pltpu.get_barrier_semaphore()

    def hello(dev):
        pl.semaphore_signal(barrier, inc=1, device_id=dev, device_id_type=MESH)

    hello((lax.rem(d + 31, 32), t))
    hello((lax.rem(d + 1, 32), t))
    for m in range(1, 4):
        hello((z * 4 + lax.rem(a + m, 4), t))
    for m in range(1, Z):
        hello((at_z(z + m), t))
    for m in range(1, TENSOR):
        hello((d, lax.rem(t + m, TENSOR)))

    r_quad = lax.div(z, 2)
    r_to = lax.rem(r_quad, 2) * 2 + lax.div(r_quad, 2)
    r_slot = lax.rem(z, 2) * 4 + a

    for n in range(Z):
        pl.when(8 * quad + n != d)(functools.partial(hello, (8 * quad + n, t)))
    for m in range(1, TENSOR):
        pl.when(home_z)(functools.partial(hello, diagonal(m)))

    raw_copy = pltpu.make_async_copy(glu_hbm, raw, raw_sem)
    raw_copy.start()
    roots_copy = pltpu.make_async_copy(roots_hbm, roots, roots_sem)
    roots_copy.start()
    cot_copy = pltpu.make_async_copy(cot_hbm, cot, cot_sem)
    cot_copy.start()
    w_copy = pltpu.make_async_copy(weight_hbm, weight, w_sem)
    w_copy.start()

    left_ok = (d != 0) & (lax.rem(d * ROWS + LEN // 2, LEN) != 0)
    right_ok = (d != 31) & (lax.rem((d + 1) * ROWS + LEN // 2, LEN) != 0)
    raw_copy.wait()

    def halves(i):
        both = raw[:, i].astype(F32)
        return both[:, 0, :], both[:, 1, :]

    for i in range(NB):
        lin, gate = halves(i)
        glu[i] = (lin * jax.nn.sigmoid(gate)).astype(BF)
        gext[i, HALF:HALF + ROWS, :] = glu[i].astype(F32)
        tapf[i] = taps[i].astype(F32)

    more = jnp.where(home_z, TENSOR - 1, 0) - jnp.where(r_to == a, 1, 0)
    pl.semaphore_wait(barrier, 2 + 3 + Z - 1 + TENSOR - 1 + Z + more)

    dn, up = (lax.rem(d + 31, 32), t), (lax.rem(d + 1, 32), t)
    send(glu.at[:, 0:HALF], halo.at[1], halo_s.at[0], halo_r.at[1], dn, left_ok)
    send(glu.at[:, ROWS - HALF:ROWS], halo.at[0], halo_s.at[1], halo_r.at[0], up, right_ok)
    roots_copy.wait()
    def quad_of(aa):
        return 2 * lax.rem(aa, 2) + lax.div(aa, 2)

    def quad_cols(aa):
        return pl.ds(pl.multiple_of(quad_of(aa) * QUART, QUART), QUART)

    def frames_of(aa):
        return pl.ds(pl.multiple_of(aa * ROWS, ROWS), ROWS)

    my_frames = frames_of(a)
    y_own = pltpu.make_async_copy(cot_hbm.at[:, :, quad_cols(a)], ycols.at[:, my_frames], yc_own)
    y_own.start()
    a_par, a_sib, a_far = a + 2 - 4 * yh, a + 1 - 2 * c, 3 - a
    my_x = lax.rem(t, 4)

    def piece_of(aa, xx):
        rows = pl.ds(pl.multiple_of(aa * ROWS + xx * 32, 32), 32)
        return ycols.at[:, rows]

    x_rows = pl.ds(pl.multiple_of(my_x * 32, 32), 32)
    for n, aa in enumerate((a_par, a_far)):
        src = cot_hbm.at[:, x_rows, quad_cols(aa)]
        send(src, piece_of(a, my_x), yc_s.at[n], yc_r.at[n], (z * 4 + aa, t))
    src = cot_hbm.at[:, :, quad_cols(a_sib)]
    send(src, ycols.at[:, my_frames], ys_s.at[0], ys_r.at[0], (sib, t))

    for m in range(1, TENSOR):
        tt = lax.rem(t + m, TENSOR)
        share_cols = pl.ds(pl.multiple_of(tt * ROWS, ROWS), ROWS)
        send(roots.at[:, :, :, share_cols], cand.at[t], s1_s.at[m], s1_r.at[m], (d, tt))
    cand[t] = roots[:, :, :, pl.ds(pl.multiple_of(t * ROWS, ROWS), ROWS)]

    def rim(side, ok, sem, src, dst, rows):
        @pl.when(ok)
        def _():
            got(src.at[side], sem.at[side])
            for i in range(NB):
                dst[i, rows, :] = src[side, i].astype(F32)

        @pl.when(jnp.logical_not(ok))
        def _():
            for i in range(NB):
                dst[i, rows, :] = jnp.zeros((HALF, ROWS), F32)

    low, high = pl.ds(0, HALF), pl.ds(HALF + ROWS, HALF)
    rim(0, left_ok, halo_r, halo, gext, low)
    rim(1, right_ok, halo_r, halo, gext, high)

    for n, aa in enumerate((a_par, a_far)):
        src = piece_of(aa, my_x)
        got(src, yc_r.at[n])
        for m in range(1, 4):
            dev = (d, t - my_x + lax.rem(my_x + m, 4))
            send(src, src, yx_s.at[n, m], yx_r.at[n, m], dev)

    def conv(i, carry):
        total = jnp.zeros((ROWS, ROWS), F32)
        for j in range(TAPS):
            total = total + tapf[i, j:j + 1, :] * gext[i, j:j + ROWS, :]
        normed = total * gain[pl.ds(i, 1), :] + shift[pl.ds(i, 1), :]
        normed_s[i] = normed
        acts[i, :, my_frames] = (normed * jax.nn.sigmoid(normed)).T.astype(BF)
        return carry

    lax.fori_loop(0, NB, conv, 0)


    def acts_of(aa):
        return acts.at[:, :, frames_of(aa)]

    send(acts_of(a), acts_of(a), at_s.at[0], at_r.at[0], (par, t))
    send(acts_of(a), acts_of(a), at_s.at[1], at_r.at[1], (sib, t))

    for m in range(1, TENSOR):
        got(cand.at[lax.rem(t + m, TENSOR)], s1_r.at[TENSOR - m])
    r_rows = pl.ds(pl.multiple_of(r_slot * 32, 32), 32)
    for m in range(NBLK):
        x = m // Z
        zz = t if x else lax.rem(z + m, Z)
        slot = home[8 if x else zz]
        own, which = lax.shift_right_logical(slot, 1), slot & 1
        lpick[m] = cand[own, which, 0]
        rpick[m] = cand[own, which, 1]
        r_dev = zz * 4 + r_to
        l_dev = zz * 4 + a
        send(rpick.at[m], rrows.at[x, r_rows], r2_s.at[m], r2_r.at[x, r_slot], (r_dev, t), r_dev != d)
        pl.when(r_dev == d)(functools.partial(keep, rrows, (x, r_rows), rpick, m))
        send(lpick.at[m], lfull.at[x, z, a], l2_s.at[m], l2_r.at[x, z], (l_dev, t), l_dev != d)
        pl.when(l_dev == d)(functools.partial(keep, lfull, (x, z, a), lpick, m))

    off_relay, off_plain = 2 + 4 * c, 6 - 4 * c
    offs = (4, 3, 5, None, off_plain, 1, 7, 0, off_relay)

    def product(n, chip):
        block = Z if n == 3 else lax.rem(z + offs[n], Z)
        row, col = (2, 2) if n == 3 else (lax.div(block, NB), lax.rem(block, NB))
        span = pl.ds(pl.multiple_of(chip * 256, 256), 256)
        return dot(acts[row, :, span], ycols[col, span, :], ((1,), (0,)))

    y_own.wait()
    got(ycols.at[:, frames_of(a_sib)], ys_r.at[0])
    got(acts_of(a_sib), at_r.at[1])
    for n in range(NBLK):
        gacc[n] = product(n, yh)

    got(acts_of(a_par), at_r.at[0])
    send(acts_of(a_par), acts_of(a_par), at_s.at[2], at_r.at[2], (sib, t))
    for n, aa in enumerate((a_par, a_far)):
        for m in range(1, 4):
            got(piece_of(aa, lax.rem(my_x + 4 - m, 4)), yx_r.at[n, m])
    got(acts_of(a_far), at_r.at[2])

    e_off = lax.rem(z - t + Z, Z)
    e_far = (e_off > 1) & (e_off < 7)
    e_low = (e_off < 4) | ((e_off == 4) & (c == 0))
    e_via = at_z(jnp.where(e_low, t + 1, t - 1))

    def e_merge(sources, odd):
        for n in sources:
            got(erecv.at[n], ez_r.at[n])

        @pl.when(c == odd)
        def _():
            got(erecv.at[4], ez_r.at[4])

        @pl.when(c != odd)
        def _():
            erecv[4] = jnp.zeros((ROWS, QUART), BF)

        total = gacc[3] + erecv[4].astype(F32)
        for n in sources:
            total = total + erecv[n].astype(F32)
        zsend[3] = total.astype(BF)

    my_cols = pl.ds(pl.multiple_of(t * ROWS, ROWS), ROWS)

    def roots_in(x):
        for n in range(Z):
            source = 8 * quad + n
            rows = pl.ds(32 * n, 32)
            pl.when(source != d)(functools.partial(got, rrows.at[x, rows], r2_r.at[x, n]))
            pl.when(z != n)(functools.partial(got, lfull.at[x, n, a], l2_r.at[x, n]))
        rfull[x, :, my_cols] = rrows[x]

    def roots_out(x, when):
        for m in range(1, TENSOR):
            dev = diagonal(m) if x else (d, lax.rem(t + m, TENSOR))
            send(rrows.at[x], rfull.at[x, :, my_cols], r3_s.at[x, m], r3_r.at[x, m], dev, when)
        mine = lfull.at[x, :, a]
        send(mine, mine, l3_s.at[x, 0], l3_r.at[x, 0], (par, t), when)
        send(mine, mine, l3_s.at[x, 1], l3_r.at[x, 1], (sib, t), when)

    def left_on(x, when):
        his = lfull.at[x, :, a_par]
        if when is None:
            got(his, l3_r.at[x, 0])
        else:
            pl.when(when)(functools.partial(got, his, l3_r.at[x, 0]))
        send(his, his, l3_s.at[x, 2], l3_r.at[x, 2], (sib, t), when)

    for n in range(NBLK):
        if n == 3:
            roots_in(0)
            roots_out(0, None)
            pl.when(home_z)(functools.partial(roots_in, 1))
            roots_out(1, home_z)
        total = gacc[n] + product(n, 1 - yh)
        if n == 3:
            gacc[n] = total
            zsend[n] = total.astype(BF)
            send(zsend.at[n], erecv.at[e_off], ez_s.at[0], ez_r.at[e_off], (e_via, t), e_far)
        elif n == 0:
            zsend[n] = total.astype(BF)
            send(zsend.at[n], relay, z_s.at[n], z_r.at[4], (at_z(z + off_relay), t))
        elif n == 7:
            gacc[n] = total
        else:
            if n == 8:
                got(relay, z_r.at[4])
                total = total + relay[...].astype(F32)
            zsend[n] = total.astype(BF)
            send(
                zsend.at[n], zrecv.at[offs[n]], z_s.at[n], z_r.at[offs[n]],
                (at_z(z + offs[n]), t),
            )

    pl.when(e_off == 1)(functools.partial(e_merge, (2, 3), 0))
    pl.when(e_off == 7)(functools.partial(e_merge, (5, 6), 1))
    near = (e_off == 1) | (e_off == 7)
    send(zsend.at[3], erecv.at[e_off], ez_s.at[0], ez_r.at[e_off], (at_z(t), t), near)

    cot_copy.wait()
    w_copy.wait()
    for i in range(NB):
        grad = jnp.zeros((ROWS, ROWS), F32)
        for j in range(NB):
            grad = grad + dot(cot[j], weight[i, j], ((1,), (1,)))
        normed = normed_s[i]
        sg = jax.nn.sigmoid(normed)
        cg = (grad * sg * (1.0 + normed * (1.0 - sg)) * gain[i:i + 1, :]).astype(BF)
        cg_b[i] = cg
        cgext[i, HALF:HALF + ROWS, :] = cg.astype(F32)
    send(cg_b.at[:, 0:HALF], cg_halo.at[1], ch_s.at[0], ch_r.at[1], dn, left_ok)
    send(cg_b.at[:, ROWS - HALF:ROWS], cg_halo.at[0], ch_s.at[1], ch_r.at[0], up, right_ok)

    left_on(0, None)
    left_on(1, home_z)

    def tap_grad(i, carry):
        cg = cgext[i, HALF:HALF + ROWS, :]
        for j in range(TAPS):
            terms = (cg * gext[i, j:j + ROWS, :]).reshape(ROWS // 8, 8, ROWS)
            row = jnp.sum(jnp.sum(terms, axis=0), axis=0, keepdims=True)
            kpart[j // HALF, i, j % HALF:j % HALF + 1, :] = row
        return carry

    lax.fori_loop(0, NB, tap_grad, 0)
    send(kpart.at[1 - c], kin1, k_s.at[0], k_r.at[0], (sib, t))

    def roots_all(x):
        for m in range(1, TENSOR):
            tt = lax.rem(t + m, TENSOR)
            cols = pl.ds(pl.multiple_of(tt * ROWS, ROWS), ROWS)
            got(rfull.at[x, :, cols], r3_r.at[x, TENSOR - m])
        got(lfull.at[x, :, a_sib], l3_r.at[x, 1])
        got(lfull.at[x, :, a_far], l3_r.at[x, 2])
        for zz in range(Z):
            part = lfull[x, zz].reshape(ROWS, ROWS).astype(F32)
            lturn[x, :, ROWS * zz:ROWS * zz + ROWS] = part.T.astype(BF)

    def join(x):
        total = gacc[3 if x else 7]
        for n in range(Z):
            if x == 0 and n not in (0, 4):
                got(zrecv.at[n], z_r.at[n])
                total = total + zrecv[n].astype(F32)
            elif x == 1 and n in (1, 7):
                got(erecv.at[n], ez_r.at[n])
                total = total + erecv[n].astype(F32)
        gfull[x, quad] = total.astype(BF)

    par_quad = 2 * c + 1 - yh

    def quarters_out(x, when):
        mine = gfull.at[x, quad]
        send(mine, mine, c_s.at[x, 0], c_r.at[x, 0], (par, t), when)
        send(mine, mine, c_s.at[x, 1], c_r.at[x, 1], (sib, t), when)

    def quarters_on(x, when):
        his = gfull.at[x, par_quad]
        send(his, his, c_s.at[x, 2], c_r.at[x, 2], (sib, t), when)

    def quarters_in(x):
        got(gfull.at[x, 2 * (1 - c) + yh], c_r.at[x, 1])
        got(gfull.at[x, 2 * (1 - c) + 1 - yh], c_r.at[x, 2])

    join(0)
    quarters_out(0, None)
    pl.when(home_z)(functools.partial(join, 1))
    quarters_out(1, home_z)

    got(kin1, k_r.at[0])
    ksend2[...] = kpart[c] + kin1[...]
    send(ksend2, kin2, k_s.at[1], k_r.at[1], (par, t))

    roots_all(0)
    pl.when(home_z)(functools.partial(roots_all, 1))

    got(gfull.at[0, par_quad], c_r.at[0, 0])
    quarters_on(0, None)
    pl.when(home_z)(functools.partial(got, gfull.at[1, par_quad], c_r.at[1, 0]))
    quarters_on(1, home_z)
    quarters_in(0)

    def right(x):
        part = jnp.zeros((ROWS, QUART), F32)
        for q in range(QUADS):
            part = part + dot(gfull[x, q], rfull[x, :, QUART * q:QUART * q + QUART], ((1,), (1,)))
        wall[x, t] = (part * SHARE).astype(BF)

    right(0)
    for m in range(1, TENSOR):
        dev = (d, lax.rem(t + m, TENSOR))
        send(wall.at[0, t], wall.at[0, t], wt_s.at[0, m], wt_r.at[0, m], dev)

    @pl.when(home_z)
    def _():
        quarters_in(1)
        right(1)

    for m in range(1, TENSOR):
        send(wall.at[1, t], wall.at[1, t], wt_s.at[1, m], wt_r.at[1, m], diagonal(m), home_z)

    got(kin2, k_r.at[1])
    ksum[...] = ksend2[...] + kin2[...]
    for m in range(1, Z):
        send(ksum, kz.at[z], k_s.at[1 + m], k_r.at[1 + m], (at_z(z + m), t))
    kz[z] = ksum[...]

    rim(0, left_ok, ch_r, cg_halo, cgext, low)
    rim(1, right_ok, ch_r, cg_halo, cgext, high)

    for i in range(NB):
        total = jnp.zeros((ROWS, ROWS), F32)
        for j in range(TAPS):
            total = total + tapf[i, j:j + 1, :] * cgext[i, TAPS - j:TAPS - j + ROWS, :]
        lin, gate = halves(i)
        sg = jax.nn.sigmoid(gate)
        total = total * sg
        ggrad[:, i, 0, :] = total.astype(BF)
        ggrad[:, i, 1, :] = (total * lin * (1.0 - sg)).astype(BF)

    def quarter(block, q):
        cols = pl.ds(pl.multiple_of(q * QUART, QUART), QUART)
        return upd.at[lax.div(block, NB), lax.rem(block, NB), :, cols]

    def left_mult(x, block):
        for m in range(1, TENSOR):
            got(wall.at[x, lax.rem(t + m, TENSOR)], wt_r.at[x, TENSOR - m])
        part = dot(lturn[x], wall[x].reshape(BLOCK, QUART), ((1,), (0,)))
        quarter(block, quad)[...] = part.astype(BF)

    second = jnp.int32(Z)
    sib_quads = (2 * (1 - c) + yh, 2 * (1 - c) + 1 - yh)

    def piece(n, q):
        return quarter(second if n == Z else lax.rem(z + n, Z), q)

    def on(n, h, when=None):
        src = piece(n, par_quad if h else quad)
        if h == 0:
            send(src, src, uy_s.at[n], uy_r.at[n], (par, t), when)
        send(src, src, us_s.at[n, h], us_r.at[n, h], (sib, t), when)

    left_mult(0, z)
    for off in (3, 5, 2, 6, 1, 7):
        src = piece(0, quad)
        send(src, src, uz_s.at[off], uz_r.at[off], (at_z(z + off), t))
    on(0, 0)

    @pl.when(home_z)
    def _():
        left_mult(1, second)

    for off in (3, 5, 2, 6, 1, 7):
        src = piece(Z, quad)
        send(src, src, uz_s.at[Z + off], uz_r.at[Z], (at_z(z + off), t), home_z)

    for m in range(1, Z):
        got(kz.at[lax.rem(z + m, Z)], k_r.at[1 + Z - m])
    total = kz[0]
    for zz in range(1, Z):
        total = total + kz[zz]
    khalf[c] = total * SHARE
    send(khalf.at[c], khalf.at[c], k_s.at[9], k_r.at[9], (sib, t))

    def pass_on(n, land, when):
        src = piece(n, quad)
        send(src, src, uz_s.at[4 + land], uz_r.at[land], (at_z(z - 1 + 2 * c), t), when)

    for off in (3, 5, 2, 6, 1, 7):
        got(piece(off, quad), uz_r.at[Z - off])
        if off == 3:
            pass_on(3, 4, c == 0)
        if off == 5:
            pass_on(5, 4, c == 1)
        on(off, 0)
    pl.when(jnp.logical_not(home_z))(functools.partial(got, piece(Z, quad), uz_r.at[Z]))
    pass_on(Z, Z, lax.rem(t - z + Z, Z) == 3 + 2 * c)
    on(Z, 0)
    got(piece(4, quad), uz_r.at[4])
    on(4, 0)
    for n in (0, 3, 5, 2, 6, 1, 7, Z, 4):
        got(piece(n, par_quad), uy_r.at[n])
        on(n, 1)

    got(khalf.at[1 - c], k_r.at[9])
    for half in range(2):
        for i in range(NB):
            kgrad[i, HALF * half:HALF * half + HALF, :] = khalf[half, i]

    for n in range(Z + 1):
        for h in range(2):
            got(piece(n, sib_quads[h]), us_r.at[n, h])

    for copy, when in sends:
        if when is None:
            copy.wait_send()
        else:
            pl.when(when)(copy.wait_send)


def hand_over(upd, kgrad, ggrad, upd_out, kgrad_out, ggrad_out, upd_v, kgrad_v, ggrad_v, ins, outs):
    legs = [(kgrad, kgrad_v, kgrad_out), (ggrad, ggrad_v, ggrad_out)]
    for b in range(NBLK):
        at = (b // NB, b % NB)
        legs.append((upd.at[at], upd_v.at[at], upd_out.at[at]))
    arrive = [pltpu.make_async_copy(x, y, ins.at[n]) for n, (x, y, _) in enumerate(legs)]
    leave = [pltpu.make_async_copy(y, w, outs.at[n]) for n, (_, y, w) in enumerate(legs)]
    for copy in arrive:
        copy.start()
    for copy, then in zip(arrive, leave):
        copy.wait()
        then.start()
    for copy in leave:
        copy.wait()


def per_device(
    glu_input, conv_kernel, norm_gain, norm_shift, out_weight, out_cotangent, root_stack, home
):
    vmem = pl.BlockSpec(memory_space=pltpu.VMEM)
    hbm = pl.BlockSpec(memory_space=pltpu.HBM)
    dma = pltpu.SemaphoreType.DMA
    sq = (NB, ROWS, ROWS)
    out = pl.pallas_call(
        kernel,
        out_shape=(
            jax.ShapeDtypeStruct((NB, NB, ROWS, BLOCK), BF),
            jax.ShapeDtypeStruct((NB, TAPS, ROWS), F32),
            jax.ShapeDtypeStruct((ROWS, NB, 2, ROWS), BF),
        ),
        in_specs=[
            pl.BlockSpec(memory_space=pltpu.SMEM), hbm, hbm, hbm, hbm, vmem, vmem, vmem,
        ],
        out_specs=(vmem, vmem, vmem),
        scratch_shapes=[
            pltpu.VMEM((ROWS, NB, 2, ROWS), BF),
            pltpu.VMEM(sq, BF),
            pltpu.VMEM((NB, ROWS, BLOCK), BF),
            pltpu.VMEM((2, 2, 32, BLOCK), BF),
            pltpu.VMEM((NB, TAPS, ROWS), F32),
            pltpu.VMEM((TENSOR, 2, 2, 32, ROWS), BF),
            pltpu.VMEM((NBLK, 32, ROWS), BF),
            pltpu.VMEM((NBLK, 32, ROWS), BF),
            pltpu.VMEM((2, QUART, ROWS), BF),
            pltpu.VMEM((2, QUART, BLOCK), BF),
            pltpu.VMEM((2, Z, QUADS, 32, ROWS), BF),
            pltpu.VMEM((2, ROWS, BLOCK), BF),
            pltpu.VMEM((2, NB, HALF, ROWS), BF),
            pltpu.VMEM((2, NB, HALF, ROWS), BF),
            pltpu.VMEM((NB, ROWS + TAPS, ROWS), F32),
            pltpu.VMEM(sq, F32),
            pltpu.VMEM(sq, BF),
            pltpu.VMEM((NB, ROWS + TAPS, ROWS), F32),
            pltpu.VMEM((NB, NB, ROWS, BLOCK), BF),
            pltpu.VMEM((NB, ROWS, QUADS * ROWS), BF),
            pltpu.VMEM((NB, QUADS * ROWS, QUART), BF),
            pltpu.VMEM((NBLK, ROWS, QUART), F32),
            pltpu.VMEM((ROWS, QUART), BF),
            pltpu.VMEM((NBLK, ROWS, QUART), BF),
            pltpu.VMEM((Z, ROWS, QUART), BF),
            pltpu.VMEM((Z, ROWS, QUART), BF),
            pltpu.VMEM((2, QUADS, ROWS, QUART), BF),
            pltpu.VMEM((2, TENSOR, ROWS, QUART), BF),
            pltpu.VMEM((2, NB, HALF, ROWS), F32),
            pltpu.VMEM((NB, HALF, ROWS), F32),
            pltpu.VMEM((NB, HALF, ROWS), F32),
            pltpu.VMEM((NB, HALF, ROWS), F32),
            pltpu.VMEM((NB, HALF, ROWS), F32),
            pltpu.VMEM((Z, NB, HALF, ROWS), F32),
            pltpu.VMEM((2, NB, HALF, ROWS), F32),
            dma, dma, dma, dma,
            dma((2,)), dma((2,)),
            dma((8,)), dma((8,)),
            dma((9,)), dma((2, 8)),
            dma((9,)), dma((2, 8)),
            dma((2, 8)), dma((2, 8)),
            dma((2, 4)), dma((2, 4)),
            dma((2,)), dma((2,)),
            dma((1,)), dma((1,)),
            dma((2, 4)), dma((2, 4)),
            dma((3,)), dma((3,)),
            dma,
            dma((9,)), dma((8,)),
            dma((1,)), dma((8,)),
            dma((2, 3)), dma((2, 3)),
            dma((2, 8)), dma((2, 8)),
            dma((16,)), dma((9,)),
            dma((9,)), dma((9,)),
            dma((9, 2)), dma((9, 2)),
            dma((2,)), dma((2,)),
            dma((10,)), dma((10,)),
        ],
        compiler_params=pltpu.CompilerParams(
            collective_id=0, has_side_effects=True, vmem_limit_bytes=60 * 2**20
        ),
    )(
        home, glu_input.transpose(0, 2, 1, 3), out_weight.transpose(0, 2, 1, 3), out_cotangent.transpose(1, 0, 2),
        root_stack, conv_kernel.transpose(1, 0, 2), norm_gain, norm_shift,
    )
    update, kernel_grad, glu_grad = pl.pallas_call(
        hand_over,
        out_shape=[jax.ShapeDtypeStruct(x.shape, x.dtype) for x in out],
        in_specs=[hbm] * 3,
        out_specs=[hbm] * 3,
        scratch_shapes=[pltpu.VMEM(x.shape, x.dtype) for x in out]
        + [dma((NBLK + 2,)), dma((NBLK + 2,))],
        compiler_params=pltpu.CompilerParams(vmem_limit_bytes=60 * 2**20),
    )(*out)
    return glu_grad.transpose(0, 2, 1, 3), kernel_grad.transpose(1, 0, 2), update.transpose(0, 2, 1, 3)


def solution(mesh):
    placed = (
        P("dp", None, None, "tensor"),
        P(None, None, "tensor"),
        P(None, "tensor"),
        P(None, "tensor"),
        P(None, "tensor", None, None),
        P("dp", None, None),
        P("tensor", None, "dp", None),
        P(),
    )
    return jax.shard_map(
        per_device,
        mesh=mesh,
        in_specs=placed,
        out_specs=(
            P("dp", None, None, "tensor"),
            P(None, None, "tensor"),
            P(None, "tensor", None, None),
        ),
        check_vma=False,
    )
```

```python
import functools

import jax
import jax.numpy as jnp
from jax import lax
from jax.experimental import pallas as pl
from jax.experimental.pallas import tpu as pltpu
from jax.sharding import PartitionSpec as P

LEN = 2048
MESH = pl.DeviceIdType.MESH
BF = jnp.bfloat16
F32 = jnp.float32

Z = 8
QUADS = 4
TENSOR = 8
TAPS = 32
HALF = TAPS // 2
ROWS = 128
BLOCK = 1024
NB = 3
NBLK = 9
QUART = BLOCK // 4
SHARE = LEN / (ROWS * Z * QUADS)

ORDER = (4, 3, 5, 2, 6, 1, 7, 0)
SPOT = {off: k for k, off in enumerate(ORDER)}
HOPS = ((4, 3), (3, 4))


def dot(a, b, dims):
    return lax.dot_general(a, b, (dims, ((), ())), preferred_element_type=F32)


def keep(dst, at, src, m):
    dst[at] = src[m]


def kernel(
    home, glu_hbm, weight_hbm, cot_hbm, roots_hbm, taps, gain, shift,
    upd_out, kgrad, ggrad,
    upd, raw, glu, cot, roots, tapf, cand, rpick, lpick, rrows, rfull, lfull, lturn,
    halo, cg_halo, gext, normed_s, cg_b, cgext, weight,
    acts, ycols, gacc, relay, zsend, zrecv, erecv, gfull, wall,
    kpart, kin1, ksend2, kin2, ksum, kz, khalf,
    out_sem, raw_sem, w_sem, cot_sem, roots_sem, halo_s, halo_r, s1_s, s1_r, r2_s, r2_r, l2_s, l2_r,
    r3_s, r3_r, l3_s, l3_r, yc_s, yc_r, ys_s, ys_r, yx_s, yx_r, at_s, at_r, yc_own, z_s, z_r, ez_s, ez_r,
    c_s, c_r, wt_s, wt_r, uz_s, uz_r, uy_s, uy_r, us_s, us_r, ch_s, ch_r, k_s, k_r,
):
    d = lax.axis_index("dp")
    t = lax.axis_index("tensor")
    z = lax.div(d, 4)
    a = lax.rem(d, 4)
    yh = lax.div(a, 2)
    c = lax.rem(a, 2)
    sib = d + 1 - 2 * c
    par = d + 2 - 4 * yh

    def at_z(zz):
        return lax.rem(zz + 2 * Z, Z) * 4 + a

    quad = 2 * c + yh
    home_z = z == t

    def diagonal(m):
        tt = lax.rem(t + m, TENSOR)
        return (tt * 4 + a, tt)

    sends = []

    def send(src, dst, ss, rs, dev, when=None):
        copy = pltpu.make_async_remote_copy(
            src_ref=src, dst_ref=dst, send_sem=ss, recv_sem=rs,
            device_id=dev, device_id_type=MESH,
        )
        if when is None:
            copy.start()
        else:
            pl.when(when)(copy.start)
        sends.append((copy, when))

    def got(dst, rs):
        pltpu.make_async_remote_copy(
            src_ref=dst, dst_ref=dst, send_sem=s1_s.at[0], recv_sem=rs,
            device_id=(sib, t), device_id_type=MESH,
        ).wait_recv()

    barrier = pltpu.get_barrier_semaphore()

    def hello(dev):
        pl.semaphore_signal(barrier, inc=1, device_id=dev, device_id_type=MESH)

    hello((lax.rem(d + 31, 32), t))
    hello((lax.rem(d + 1, 32), t))
    for m in range(1, 4):
        hello((z * 4 + lax.rem(a + m, 4), t))
    for m in range(1, Z):
        hello((at_z(z + m), t))
    for m in range(1, TENSOR):
        hello((d, lax.rem(t + m, TENSOR)))

    r_quad = lax.div(z, 2)
    r_to = lax.rem(r_quad, 2) * 2 + lax.div(r_quad, 2)
    r_slot = lax.rem(z, 2) * 4 + a

    for n in range(Z):
        pl.when(8 * quad + n != d)(functools.partial(hello, (8 * quad + n, t)))
    for m in range(1, TENSOR):
        pl.when(home_z)(functools.partial(hello, diagonal(m)))

    raw_copy = pltpu.make_async_copy(glu_hbm, raw, raw_sem)
    raw_copy.start()
    roots_copy = pltpu.make_async_copy(roots_hbm, roots, roots_sem)
    roots_copy.start()
    cot_copy = pltpu.make_async_copy(cot_hbm, cot, cot_sem)
    cot_copy.start()
    w_copy = pltpu.make_async_copy(weight_hbm, weight, w_sem)
    w_copy.start()

    left_ok = (d != 0) & (lax.rem(d * ROWS + LEN // 2, LEN) != 0)
    right_ok = (d != 31) & (lax.rem((d + 1) * ROWS + LEN // 2, LEN) != 0)
    raw_copy.wait()

    def halves(i):
        both = raw[:, i].astype(F32)
        return both[:, 0, :], both[:, 1, :]

    for i in range(NB):
        lin, gate = halves(i)
        glu[i] = (lin * jax.nn.sigmoid(gate)).astype(BF)
        gext[i, HALF:HALF + ROWS, :] = glu[i].astype(F32)
        tapf[i] = taps[i].astype(F32)

    more = jnp.where(home_z, TENSOR - 1, 0) - jnp.where(r_to == a, 1, 0)
    pl.semaphore_wait(barrier, 2 + 3 + Z - 1 + TENSOR - 1 + Z + more)

    dn, up = (lax.rem(d + 31, 32), t), (lax.rem(d + 1, 32), t)
    send(glu.at[:, 0:HALF], halo.at[1], halo_s.at[0], halo_r.at[1], dn, left_ok)
    send(glu.at[:, ROWS - HALF:ROWS], halo.at[0], halo_s.at[1], halo_r.at[0], up, right_ok)
    roots_copy.wait()
    def quad_of(aa):
        return 2 * lax.rem(aa, 2) + lax.div(aa, 2)

    def quad_cols(aa):
        return pl.ds(pl.multiple_of(quad_of(aa) * QUART, QUART), QUART)

    def frames_of(aa):
        return pl.ds(pl.multiple_of(aa * ROWS, ROWS), ROWS)

    my_frames = frames_of(a)
    y_own = pltpu.make_async_copy(cot_hbm.at[:, :, quad_cols(a)], ycols.at[:, my_frames], yc_own)
    y_own.start()
    a_par, a_sib, a_far = a + 2 - 4 * yh, a + 1 - 2 * c, 3 - a
    my_x = lax.rem(t, 4)

    def piece_of(aa, xx):
        rows = pl.ds(pl.multiple_of(aa * ROWS + xx * 32, 32), 32)
        return ycols.at[:, rows]

    x_rows = pl.ds(pl.multiple_of(my_x * 32, 32), 32)
    for n, aa in enumerate((a_par, a_far)):
        src = cot_hbm.at[:, x_rows, quad_cols(aa)]
        send(src, piece_of(a, my_x), yc_s.at[n], yc_r.at[n], (z * 4 + aa, t))
    src = cot_hbm.at[:, :, quad_cols(a_sib)]
    send(src, ycols.at[:, my_frames], ys_s.at[0], ys_r.at[0], (sib, t))

    for m in range(1, TENSOR):
        tt = lax.rem(t + m, TENSOR)
        share_cols = pl.ds(pl.multiple_of(tt * ROWS, ROWS), ROWS)
        send(roots.at[:, :, :, share_cols], cand.at[t], s1_s.at[m], s1_r.at[m], (d, tt))
    cand[t] = roots[:, :, :, pl.ds(pl.multiple_of(t * ROWS, ROWS), ROWS)]

    def rim(side, ok, sem, src, dst, rows):
        @pl.when(ok)
        def _():
            got(src.at[side], sem.at[side])
            for i in range(NB):
                dst[i, rows, :] = src[side, i].astype(F32)

        @pl.when(jnp.logical_not(ok))
        def _():
            for i in range(NB):
                dst[i, rows, :] = jnp.zeros((HALF, ROWS), F32)

    low, high = pl.ds(0, HALF), pl.ds(HALF + ROWS, HALF)
    rim(0, left_ok, halo_r, halo, gext, low)
    rim(1, right_ok, halo_r, halo, gext, high)

    for n, aa in enumerate((a_par, a_far)):
        src = piece_of(aa, my_x)
        got(src, yc_r.at[n])
        for m in range(1, 4):
            dev = (d, t - my_x + lax.rem(my_x + m, 4))
            send(src, src, yx_s.at[n, m], yx_r.at[n, m], dev)

    def conv(i, carry):
        total = jnp.zeros((ROWS, ROWS), F32)
        for j in range(TAPS):
            total = total + tapf[i, j:j + 1, :] * gext[i, j:j + ROWS, :]
        normed = total * gain[pl.ds(i, 1), :] + shift[pl.ds(i, 1), :]
        normed_s[i] = normed
        acts[i, :, my_frames] = (normed * jax.nn.sigmoid(normed)).T.astype(BF)
        return carry

    lax.fori_loop(0, NB, conv, 0)


    def acts_of(aa):
        return acts.at[:, :, frames_of(aa)]

    send(acts_of(a), acts_of(a), at_s.at[0], at_r.at[0], (par, t))
    send(acts_of(a), acts_of(a), at_s.at[1], at_r.at[1], (sib, t))

    for m in range(1, TENSOR):
        got(cand.at[lax.rem(t + m, TENSOR)], s1_r.at[TENSOR - m])
    r_rows = pl.ds(pl.multiple_of(r_slot * 32, 32), 32)
    for m in range(NBLK):
        x = m // Z
        zz = t if x else lax.rem(z + m, Z)
        slot = home[8 if x else zz]
        own, which = lax.shift_right_logical(slot, 1), slot & 1
        lpick[m] = cand[own, which, 0]
        rpick[m] = cand[own, which, 1]
        r_dev = zz * 4 + r_to
        l_dev = zz * 4 + a
        send(rpick.at[m], rrows.at[x, r_rows], r2_s.at[m], r2_r.at[x, r_slot], (r_dev, t), r_dev != d)
        pl.when(r_dev == d)(functools.partial(keep, rrows, (x, r_rows), rpick, m))
        send(lpick.at[m], lfull.at[x, z, a], l2_s.at[m], l2_r.at[x, z], (l_dev, t), l_dev != d)
        pl.when(l_dev == d)(functools.partial(keep, lfull, (x, z, a), lpick, m))

    off_relay, off_plain = 2 + 4 * c, 6 - 4 * c
    offs = (4, 3, 5, None, off_plain, 1, 7, 0, off_relay)

    def product(n, chip):
        block = Z if n == 3 else lax.rem(z + offs[n], Z)
        row, col = (2, 2) if n == 3 else (lax.div(block, NB), lax.rem(block, NB))
        span = pl.ds(pl.multiple_of(chip * 256, 256), 256)
        return dot(acts[row, :, span], ycols[col, span, :], ((1,), (0,)))

    y_own.wait()
    got(ycols.at[:, frames_of(a_sib)], ys_r.at[0])
    got(acts_of(a_sib), at_r.at[1])
    for n in range(NBLK):
        gacc[n] = product(n, yh)

    got(acts_of(a_par), at_r.at[0])
    send(acts_of(a_par), acts_of(a_par), at_s.at[2], at_r.at[2], (sib, t))
    for n, aa in enumerate((a_par, a_far)):
        for m in range(1, 4):
            got(piece_of(aa, lax.rem(my_x + 4 - m, 4)), yx_r.at[n, m])
    got(acts_of(a_far), at_r.at[2])

    e_off = lax.rem(z - t + Z, Z)
    e_far = (e_off > 1) & (e_off < 7)
    e_low = (e_off < 4) | ((e_off == 4) & (c == 0))
    e_via = at_z(jnp.where(e_low, t + 1, t - 1))

    def e_merge(sources, odd):
        for n in sources:
            got(erecv.at[n], ez_r.at[n])

        @pl.when(c == odd)
        def _():
            got(erecv.at[4], ez_r.at[4])

        @pl.when(c != odd)
        def _():
            erecv[4] = jnp.zeros((ROWS, QUART), BF)

        total = gacc[3] + erecv[4].astype(F32)
        for n in sources:
            total = total + erecv[n].astype(F32)
        zsend[3] = total.astype(BF)

    my_cols = pl.ds(pl.multiple_of(t * ROWS, ROWS), ROWS)

    def roots_in(x):
        for n in range(Z):
            source = 8 * quad + n
            rows = pl.ds(32 * n, 32)
            pl.when(source != d)(functools.partial(got, rrows.at[x, rows], r2_r.at[x, n]))
            pl.when(z != n)(functools.partial(got, lfull.at[x, n, a], l2_r.at[x, n]))
        rfull[x, :, my_cols] = rrows[x]

    def roots_out(x, when):
        for m in range(1, TENSOR):
            dev = diagonal(m) if x else (d, lax.rem(t + m, TENSOR))
            send(rrows.at[x], rfull.at[x, :, my_cols], r3_s.at[x, m], r3_r.at[x, m], dev, when)
        mine = lfull.at[x, :, a]
        send(mine, mine, l3_s.at[x, 0], l3_r.at[x, 0], (par, t), when)
        send(mine, mine, l3_s.at[x, 1], l3_r.at[x, 1], (sib, t), when)

    def left_on(x, when):
        his = lfull.at[x, :, a_par]
        if when is None:
            got(his, l3_r.at[x, 0])
        else:
            pl.when(when)(functools.partial(got, his, l3_r.at[x, 0]))
        send(his, his, l3_s.at[x, 2], l3_r.at[x, 2], (sib, t), when)

    for n in range(NBLK):
        if n == 3:
            roots_in(0)
            roots_out(0, None)
            pl.when(home_z)(functools.partial(roots_in, 1))
            roots_out(1, home_z)
        total = gacc[n] + product(n, 1 - yh)
        if n == 3:
            gacc[n] = total
            zsend[n] = total.astype(BF)
            send(zsend.at[n], erecv.at[e_off], ez_s.at[0], ez_r.at[e_off], (e_via, t), e_far)
        elif n == 0:
            zsend[n] = total.astype(BF)
            send(zsend.at[n], relay, z_s.at[n], z_r.at[4], (at_z(z + off_relay), t))
        elif n == 7:
            gacc[n] = total
        else:
            if n == 8:
                got(relay, z_r.at[4])
                total = total + relay[...].astype(F32)
            zsend[n] = total.astype(BF)
            send(
                zsend.at[n], zrecv.at[offs[n]], z_s.at[n], z_r.at[offs[n]],
                (at_z(z + offs[n]), t),
            )

    pl.when(e_off == 1)(functools.partial(e_merge, (2, 3), 0))
    pl.when(e_off == 7)(functools.partial(e_merge, (5, 6), 1))
    near = (e_off == 1) | (e_off == 7)
    send(zsend.at[3], erecv.at[e_off], ez_s.at[0], ez_r.at[e_off], (at_z(t), t), near)

    cot_copy.wait()
    w_copy.wait()
    for i in range(NB):
        grad = jnp.zeros((ROWS, ROWS), F32)
        for j in range(NB):
            grad = grad + dot(cot[j], weight[i, j], ((1,), (1,)))
        normed = normed_s[i]
        sg = jax.nn.sigmoid(normed)
        cg = (grad * sg * (1.0 + normed * (1.0 - sg)) * gain[i:i + 1, :]).astype(BF)
        cg_b[i] = cg
        cgext[i, HALF:HALF + ROWS, :] = cg.astype(F32)
    send(cg_b.at[:, 0:HALF], cg_halo.at[1], ch_s.at[0], ch_r.at[1], dn, left_ok)
    send(cg_b.at[:, ROWS - HALF:ROWS], cg_halo.at[0], ch_s.at[1], ch_r.at[0], up, right_ok)

    left_on(0, None)
    left_on(1, home_z)

    def tap_grad(i, carry):
        cg = cgext[i, HALF:HALF + ROWS, :]
        for j in range(TAPS):
            terms = (cg * gext[i, j:j + ROWS, :]).reshape(ROWS // 8, 8, ROWS)
            row = jnp.sum(jnp.sum(terms, axis=0), axis=0, keepdims=True)
            kpart[j // HALF, i, j % HALF:j % HALF + 1, :] = row
        return carry

    lax.fori_loop(0, NB, tap_grad, 0)
    send(kpart.at[1 - c], kin1, k_s.at[0], k_r.at[0], (sib, t))

    def roots_all(x):
        for m in range(1, TENSOR):
            tt = lax.rem(t + m, TENSOR)
            cols = pl.ds(pl.multiple_of(tt * ROWS, ROWS), ROWS)
            got(rfull.at[x, :, cols], r3_r.at[x, TENSOR - m])
        got(lfull.at[x, :, a_sib], l3_r.at[x, 1])
        got(lfull.at[x, :, a_far], l3_r.at[x, 2])
        for zz in range(Z):
            part = lfull[x, zz].reshape(ROWS, ROWS).astype(F32)
            lturn[x, :, ROWS * zz:ROWS * zz + ROWS] = part.T.astype(BF)

    def join(x):
        total = gacc[3 if x else 7]
        for n in range(Z):
            if x == 0 and n not in (0, 4):
                got(zrecv.at[n], z_r.at[n])
                total = total + zrecv[n].astype(F32)
            elif x == 1 and n in (1, 7):
                got(erecv.at[n], ez_r.at[n])
                total = total + erecv[n].astype(F32)
        gfull[x, quad] = total.astype(BF)

    par_quad = 2 * c + 1 - yh

    def quarters_out(x, when):
        mine = gfull.at[x, quad]
        send(mine, mine, c_s.at[x, 0], c_r.at[x, 0], (par, t), when)
        send(mine, mine, c_s.at[x, 1], c_r.at[x, 1], (sib, t), when)

    def quarters_on(x, when):
        his = gfull.at[x, par_quad]
        send(his, his, c_s.at[x, 2], c_r.at[x, 2], (sib, t), when)

    def quarters_in(x):
        got(gfull.at[x, 2 * (1 - c) + yh], c_r.at[x, 1])
        got(gfull.at[x, 2 * (1 - c) + 1 - yh], c_r.at[x, 2])

    join(0)
    quarters_out(0, None)
    pl.when(home_z)(functools.partial(join, 1))
    quarters_out(1, home_z)

    got(kin1, k_r.at[0])
    ksend2[...] = kpart[c] + kin1[...]
    send(ksend2, kin2, k_s.at[1], k_r.at[1], (par, t))

    roots_all(0)
    pl.when(home_z)(functools.partial(roots_all, 1))

    got(gfull.at[0, par_quad], c_r.at[0, 0])
    quarters_on(0, None)
    pl.when(home_z)(functools.partial(got, gfull.at[1, par_quad], c_r.at[1, 0]))
    quarters_on(1, home_z)
    quarters_in(0)

    def right(x):
        part = jnp.zeros((ROWS, QUART), F32)
        for q in range(QUADS):
            part = part + dot(gfull[x, q], rfull[x, :, QUART * q:QUART * q + QUART], ((1,), (1,)))
        wall[x, t] = (part * SHARE).astype(BF)

    right(0)
    for m in range(1, TENSOR):
        dev = (d, lax.rem(t + m, TENSOR))
        send(wall.at[0, t], wall.at[0, t], wt_s.at[0, m], wt_r.at[0, m], dev)

    @pl.when(home_z)
    def _():
        quarters_in(1)
        right(1)

    for m in range(1, TENSOR):
        send(wall.at[1, t], wall.at[1, t], wt_s.at[1, m], wt_r.at[1, m], diagonal(m), home_z)

    got(kin2, k_r.at[1])
    ksum[...] = ksend2[...] + kin2[...]
    for m in range(1, Z):
        send(ksum, kz.at[z], k_s.at[1 + m], k_r.at[1 + m], (at_z(z + m), t))
    kz[z] = ksum[...]

    rim(0, left_ok, ch_r, cg_halo, cgext, low)
    rim(1, right_ok, ch_r, cg_halo, cgext, high)

    for i in range(NB):
        total = jnp.zeros((ROWS, ROWS), F32)
        for j in range(TAPS):
            total = total + tapf[i, j:j + 1, :] * cgext[i, TAPS - j:TAPS - j + ROWS, :]
        lin, gate = halves(i)
        sg = jax.nn.sigmoid(gate)
        total = total * sg
        ggrad[:, i, 0, :] = total.astype(BF)
        ggrad[:, i, 1, :] = (total * lin * (1.0 - sg)).astype(BF)

    def quarter(block, q):
        cols = pl.ds(pl.multiple_of(q * QUART, QUART), QUART)
        return upd.at[lax.div(block, NB), lax.rem(block, NB), :, cols]

    def left_mult(x, block):
        for m in range(1, TENSOR):
            got(wall.at[x, lax.rem(t + m, TENSOR)], wt_r.at[x, TENSOR - m])
        part = dot(lturn[x], wall[x].reshape(BLOCK, QUART), ((1,), (0,)))
        quarter(block, quad)[...] = part.astype(BF)

    second = jnp.int32(Z)
    sib_quads = (2 * (1 - c) + yh, 2 * (1 - c) + 1 - yh)

    def piece(n, q):
        return quarter(second if n == Z else lax.rem(z + n, Z), q)

    leaving = []

    def leave(n, q, spot):
        block = second if n == Z else lax.rem(z + n, Z)
        cols = pl.ds(pl.multiple_of(q * QUART, QUART), QUART)
        dst = upd_out.at[lax.div(block, NB), lax.rem(block, NB), :, cols]
        copy = pltpu.make_async_copy(piece(n, q), dst, out_sem.at[n, spot])
        copy.start()
        leaving.append(copy)

    def on(n, h, when=None):
        src = piece(n, par_quad if h else quad)
        if h == 0:
            send(src, src, uy_s.at[n], uy_r.at[n], (par, t), when)
        send(src, src, us_s.at[n, h], us_r.at[n, h], (sib, t), when)
        leave(n, par_quad if h else quad, h)

    left_mult(0, z)
    for off in (3, 5, 2, 6, 1, 7):
        src = piece(0, quad)
        send(src, src, uz_s.at[off], uz_r.at[off], (at_z(z + off), t))
    on(0, 0)

    @pl.when(home_z)
    def _():
        left_mult(1, second)

    for off in (3, 5, 2, 6, 1, 7):
        src = piece(Z, quad)
        send(src, src, uz_s.at[Z + off], uz_r.at[Z], (at_z(z + off), t), home_z)

    for m in range(1, Z):
        got(kz.at[lax.rem(z + m, Z)], k_r.at[1 + Z - m])
    total = kz[0]
    for zz in range(1, Z):
        total = total + kz[zz]
    khalf[c] = total * SHARE
    send(khalf.at[c], khalf.at[c], k_s.at[9], k_r.at[9], (sib, t))

    def pass_on(n, land, when):
        src = piece(n, quad)
        send(src, src, uz_s.at[4 + land], uz_r.at[land], (at_z(z - 1 + 2 * c), t), when)

    for off in (3, 5, 2, 6, 1, 7):
        got(piece(off, quad), uz_r.at[Z - off])
        if off == 3:
            pass_on(3, 4, c == 0)
        if off == 5:
            pass_on(5, 4, c == 1)
        on(off, 0)
    pl.when(jnp.logical_not(home_z))(functools.partial(got, piece(Z, quad), uz_r.at[Z]))
    pass_on(Z, Z, lax.rem(t - z + Z, Z) == 3 + 2 * c)
    on(Z, 0)
    got(piece(4, quad), uz_r.at[4])
    on(4, 0)
    for n in (0, 3, 5, 2, 6, 1, 7, Z, 4):
        got(piece(n, par_quad), uy_r.at[n])
        on(n, 1)

    got(khalf.at[1 - c], k_r.at[9])
    for half in range(2):
        for i in range(NB):
            kgrad[i, HALF * half:HALF * half + HALF, :] = khalf[half, i]

    for n in range(Z + 1):
        for h in range(2):
            got(piece(n, sib_quads[h]), us_r.at[n, h])
            leave(n, sib_quads[h], 2 + h)

    for copy in leaving:
        copy.wait()
    for copy, when in sends:
        if when is None:
            copy.wait_send()
        else:
            pl.when(when)(copy.wait_send)


def hand_over(upd, kgrad, ggrad, upd_out, kgrad_out, ggrad_out, upd_v, kgrad_v, ggrad_v, ins, outs):
    legs = [(kgrad, kgrad_v, kgrad_out), (ggrad, ggrad_v, ggrad_out)]
    for b in range(NBLK):
        at = (b // NB, b % NB)
        legs.append((upd.at[at], upd_v.at[at], upd_out.at[at]))
    arrive = [pltpu.make_async_copy(x, y, ins.at[n]) for n, (x, y, _) in enumerate(legs)]
    leave = [pltpu.make_async_copy(y, w, outs.at[n]) for n, (_, y, w) in enumerate(legs)]
    for copy in arrive:
        copy.start()
    for copy, then in zip(arrive, leave):
        copy.wait()
        then.start()
    for copy in leave:
        copy.wait()


def per_device(
    glu_input, conv_kernel, norm_gain, norm_shift, out_weight, out_cotangent, root_stack, home
):
    vmem = pl.BlockSpec(memory_space=pltpu.VMEM)
    hbm = pl.BlockSpec(memory_space=pltpu.HBM)
    dma = pltpu.SemaphoreType.DMA
    sq = (NB, ROWS, ROWS)
    out = pl.pallas_call(
        kernel,
        out_shape=(
            jax.ShapeDtypeStruct((NB, NB, ROWS, BLOCK), BF),
            jax.ShapeDtypeStruct((NB, TAPS, ROWS), F32),
            jax.ShapeDtypeStruct((ROWS, NB, 2, ROWS), BF),
        ),
        in_specs=[
            pl.BlockSpec(memory_space=pltpu.SMEM), hbm, hbm, hbm, hbm, vmem, vmem, vmem,
        ],
        out_specs=(hbm, vmem, vmem),
        scratch_shapes=[
            pltpu.VMEM((NB, NB, ROWS, BLOCK), BF),
            pltpu.VMEM((ROWS, NB, 2, ROWS), BF),
            pltpu.VMEM(sq, BF),
            pltpu.VMEM((NB, ROWS, BLOCK), BF),
            pltpu.VMEM((2, 2, 32, BLOCK), BF),
            pltpu.VMEM((NB, TAPS, ROWS), F32),
            pltpu.VMEM((TENSOR, 2, 2, 32, ROWS), BF),
            pltpu.VMEM((NBLK, 32, ROWS), BF),
            pltpu.VMEM((NBLK, 32, ROWS), BF),
            pltpu.VMEM((2, QUART, ROWS), BF),
            pltpu.VMEM((2, QUART, BLOCK), BF),
            pltpu.VMEM((2, Z, QUADS, 32, ROWS), BF),
            pltpu.VMEM((2, ROWS, BLOCK), BF),
            pltpu.VMEM((2, NB, HALF, ROWS), BF),
            pltpu.VMEM((2, NB, HALF, ROWS), BF),
            pltpu.VMEM((NB, ROWS + TAPS, ROWS), F32),
            pltpu.VMEM(sq, F32),
            pltpu.VMEM(sq, BF),
            pltpu.VMEM((NB, ROWS + TAPS, ROWS), F32),
            pltpu.VMEM((NB, NB, ROWS, BLOCK), BF),
            pltpu.VMEM((NB, ROWS, QUADS * ROWS), BF),
            pltpu.VMEM((NB, QUADS * ROWS, QUART), BF),
            pltpu.VMEM((NBLK, ROWS, QUART), F32),
            pltpu.VMEM((ROWS, QUART), BF),
            pltpu.VMEM((NBLK, ROWS, QUART), BF),
            pltpu.VMEM((Z, ROWS, QUART), BF),
            pltpu.VMEM((Z, ROWS, QUART), BF),
            pltpu.VMEM((2, QUADS, ROWS, QUART), BF),
            pltpu.VMEM((2, TENSOR, ROWS, QUART), BF),
            pltpu.VMEM((2, NB, HALF, ROWS), F32),
            pltpu.VMEM((NB, HALF, ROWS), F32),
            pltpu.VMEM((NB, HALF, ROWS), F32),
            pltpu.VMEM((NB, HALF, ROWS), F32),
            pltpu.VMEM((NB, HALF, ROWS), F32),
            pltpu.VMEM((Z, NB, HALF, ROWS), F32),
            pltpu.VMEM((2, NB, HALF, ROWS), F32),
            dma((NBLK, 4)),
            dma, dma, dma, dma,
            dma((2,)), dma((2,)),
            dma((8,)), dma((8,)),
            dma((9,)), dma((2, 8)),
            dma((9,)), dma((2, 8)),
            dma((2, 8)), dma((2, 8)),
            dma((2, 4)), dma((2, 4)),
            dma((2,)), dma((2,)),
            dma((1,)), dma((1,)),
            dma((2, 4)), dma((2, 4)),
            dma((3,)), dma((3,)),
            dma,
            dma((9,)), dma((8,)),
            dma((1,)), dma((8,)),
            dma((2, 3)), dma((2, 3)),
            dma((2, 8)), dma((2, 8)),
            dma((16,)), dma((9,)),
            dma((9,)), dma((9,)),
            dma((9, 2)), dma((9, 2)),
            dma((2,)), dma((2,)),
            dma((10,)), dma((10,)),
        ],
        compiler_params=pltpu.CompilerParams(
            collective_id=0, has_side_effects=True, vmem_limit_bytes=60 * 2**20
        ),
    )(
        home, glu_input.transpose(0, 2, 1, 3), out_weight.transpose(0, 2, 1, 3), out_cotangent.transpose(1, 0, 2),
        root_stack, conv_kernel.transpose(1, 0, 2), norm_gain, norm_shift,
    )
    update, kernel_grad, glu_grad = pl.pallas_call(
        hand_over,
        out_shape=[jax.ShapeDtypeStruct(x.shape, x.dtype) for x in out],
        in_specs=[hbm] * 3,
        out_specs=[hbm] * 3,
        scratch_shapes=[pltpu.VMEM(x.shape, x.dtype) for x in out]
        + [dma((NBLK + 2,)), dma((NBLK + 2,))],
        compiler_params=pltpu.CompilerParams(vmem_limit_bytes=60 * 2**20),
    )(*out)
    return glu_grad.transpose(0, 2, 1, 3), kernel_grad.transpose(1, 0, 2), update.transpose(0, 2, 1, 3)


def solution(mesh):
    placed = (
        P("dp", None, None, "tensor"),
        P(None, None, "tensor"),
        P(None, "tensor"),
        P(None, "tensor"),
        P(None, "tensor", None, None),
        P("dp", None, None),
        P("tensor", None, "dp", None),
        P(),
    )
    return jax.shard_map(
        per_device,
        mesh=mesh,
        in_specs=placed,
        out_specs=(
            P("dp", None, None, "tensor"),
            P(None, None, "tensor"),
            P(None, "tensor", None, None),
        ),
        check_vma=False,
    )
```

```python
import functools

import jax
import jax.numpy as jnp
from jax import lax
from jax.experimental import pallas as pl
from jax.experimental.pallas import tpu as pltpu
from jax.sharding import PartitionSpec as P

LEN = 2048
MESH = pl.DeviceIdType.MESH
BF = jnp.bfloat16
F32 = jnp.float32

Z = 8
QUADS = 4
TENSOR = 8
TAPS = 32
HALF = TAPS // 2
ROWS = 128
BLOCK = 1024
NB = 3
NBLK = 9
QUART = BLOCK // 4
SHARE = LEN / (ROWS * Z * QUADS)

ORDER = (4, 3, 5, 2, 6, 1, 7, 0)
SPOT = {off: k for k, off in enumerate(ORDER)}
HOPS = ((4, 3), (3, 4))


def dot(a, b, dims):
    return lax.dot_general(a, b, (dims, ((), ())), preferred_element_type=F32)


def keep(dst, at, src, m):
    dst[at] = src[m]


def kernel(
    home, glu_hbm, weight_hbm, cot_hbm, roots_hbm, taps, gain, shift,
    upd, kgrad, ggrad,
    raw, glu, cot, roots, tapf, cand, rpick, lpick, rrows, rfull, lfull, lturn,
    halo, cg_halo, gext, normed_s, cg_b, cgext, weight,
    acts, ycols, gacc, relay, zsend, zrecv, erecv, gfull, wall,
    kpart, kin1, ksend2, kin2, ksum, kz, khalf,
    raw_sem, w_sem, cot_sem, roots_sem, halo_s, halo_r, s1_s, s1_r, r2_s, r2_r, l2_s, l2_r,
    r3_s, r3_r, l3_s, l3_r, yc_s, yc_r, ys_s, ys_r, yx_s, yx_r, at_s, at_r, yc_own, z_s, z_r, ez_s, ez_r,
    c_s, c_r, wt_s, wt_r, uz_s, uz_r, uy_s, uy_r, us_s, us_r, ch_s, ch_r, k_s, k_r,
):
    d = lax.axis_index("dp")
    t = lax.axis_index("tensor")
    z = lax.div(d, 4)
    a = lax.rem(d, 4)
    yh = lax.div(a, 2)
    c = lax.rem(a, 2)
    sib = d + 1 - 2 * c
    par = d + 2 - 4 * yh

    def at_z(zz):
        return lax.rem(zz + 2 * Z, Z) * 4 + a

    quad = 2 * c + yh
    home_z = z == t

    def diagonal(m):
        tt = lax.rem(t + m, TENSOR)
        return (tt * 4 + a, tt)

    sends = []

    def send(src, dst, ss, rs, dev, when=None):
        copy = pltpu.make_async_remote_copy(
            src_ref=src, dst_ref=dst, send_sem=ss, recv_sem=rs,
            device_id=dev, device_id_type=MESH,
        )
        if when is None:
            copy.start()
        else:
            pl.when(when)(copy.start)
        sends.append((copy, when))

    def got(dst, rs):
        pltpu.make_async_remote_copy(
            src_ref=dst, dst_ref=dst, send_sem=s1_s.at[0], recv_sem=rs,
            device_id=(sib, t), device_id_type=MESH,
        ).wait_recv()

    barrier = pltpu.get_barrier_semaphore()

    def hello(dev):
        pl.semaphore_signal(barrier, inc=1, device_id=dev, device_id_type=MESH)

    hello((lax.rem(d + 31, 32), t))
    hello((lax.rem(d + 1, 32), t))
    for m in range(1, 4):
        hello((z * 4 + lax.rem(a + m, 4), t))
    for m in range(1, Z):
        hello((at_z(z + m), t))
    for m in range(1, TENSOR):
        hello((d, lax.rem(t + m, TENSOR)))

    r_quad = lax.div(z, 2)
    r_to = lax.rem(r_quad, 2) * 2 + lax.div(r_quad, 2)
    r_slot = lax.rem(z, 2) * 4 + a

    for n in range(Z):
        pl.when(8 * quad + n != d)(functools.partial(hello, (8 * quad + n, t)))
    for m in range(1, TENSOR):
        pl.when(home_z)(functools.partial(hello, diagonal(m)))

    raw_copy = pltpu.make_async_copy(glu_hbm, raw, raw_sem)
    raw_copy.start()
    roots_copy = pltpu.make_async_copy(roots_hbm, roots, roots_sem)
    roots_copy.start()
    cot_copy = pltpu.make_async_copy(cot_hbm, cot, cot_sem)
    cot_copy.start()
    w_copy = pltpu.make_async_copy(weight_hbm, weight, w_sem)
    w_copy.start()

    left_ok = (d != 0) & (lax.rem(d * ROWS + LEN // 2, LEN) != 0)
    right_ok = (d != 31) & (lax.rem((d + 1) * ROWS + LEN // 2, LEN) != 0)
    raw_copy.wait()

    def halves(i):
        both = raw[:, i].astype(F32)
        return both[:, 0, :], both[:, 1, :]

    for i in range(NB):
        lin, gate = halves(i)
        glu[i] = (lin * jax.nn.sigmoid(gate)).astype(BF)
        gext[i, HALF:HALF + ROWS, :] = glu[i].astype(F32)
        tapf[i] = taps[i].astype(F32)

    more = jnp.where(home_z, TENSOR - 1, 0) - jnp.where(r_to == a, 1, 0)
    pl.semaphore_wait(barrier, 2 + 3 + Z - 1 + TENSOR - 1 + Z + more)

    dn, up = (lax.rem(d + 31, 32), t), (lax.rem(d + 1, 32), t)
    send(glu.at[:, 0:HALF], halo.at[1], halo_s.at[0], halo_r.at[1], dn, left_ok)
    send(glu.at[:, ROWS - HALF:ROWS], halo.at[0], halo_s.at[1], halo_r.at[0], up, right_ok)
    roots_copy.wait()
    def quad_of(aa):
        return 2 * lax.rem(aa, 2) + lax.div(aa, 2)

    def quad_cols(aa):
        return pl.ds(pl.multiple_of(quad_of(aa) * QUART, QUART), QUART)

    def frames_of(aa):
        return pl.ds(pl.multiple_of(aa * ROWS, ROWS), ROWS)

    my_frames = frames_of(a)
    y_own = pltpu.make_async_copy(cot_hbm.at[:, :, quad_cols(a)], ycols.at[:, my_frames], yc_own)
    y_own.start()
    a_par, a_sib, a_far = a + 2 - 4 * yh, a + 1 - 2 * c, 3 - a
    my_x = lax.rem(t, 4)

    def piece_of(aa, xx):
        rows = pl.ds(pl.multiple_of(aa * ROWS + xx * 32, 32), 32)
        return ycols.at[:, rows]

    x_rows = pl.ds(pl.multiple_of(my_x * 32, 32), 32)
    for n, aa in enumerate((a_par, a_far)):
        src = cot_hbm.at[:, x_rows, quad_cols(aa)]
        send(src, piece_of(a, my_x), yc_s.at[n], yc_r.at[n], (z * 4 + aa, t))
    src = cot_hbm.at[:, :, quad_cols(a_sib)]
    send(src, ycols.at[:, my_frames], ys_s.at[0], ys_r.at[0], (sib, t))

    for m in range(1, TENSOR):
        tt = lax.rem(t + m, TENSOR)
        share_cols = pl.ds(pl.multiple_of(tt * ROWS, ROWS), ROWS)
        send(roots.at[:, :, :, share_cols], cand.at[t], s1_s.at[m], s1_r.at[m], (d, tt))
    cand[t] = roots[:, :, :, pl.ds(pl.multiple_of(t * ROWS, ROWS), ROWS)]

    def rim(side, ok, sem, src, dst, rows):
        @pl.when(ok)
        def _():
            got(src.at[side], sem.at[side])
            for i in range(NB):
                dst[i, rows, :] = src[side, i].astype(F32)

        @pl.when(jnp.logical_not(ok))
        def _():
            for i in range(NB):
                dst[i, rows, :] = jnp.zeros((HALF, ROWS), F32)

    low, high = pl.ds(0, HALF), pl.ds(HALF + ROWS, HALF)
    rim(0, left_ok, halo_r, halo, gext, low)
    rim(1, right_ok, halo_r, halo, gext, high)

    for n, aa in enumerate((a_par, a_far)):
        src = piece_of(aa, my_x)
        got(src, yc_r.at[n])
        for m in range(1, 4):
            dev = (d, t - my_x + lax.rem(my_x + m, 4))
            send(src, src, yx_s.at[n, m], yx_r.at[n, m], dev)

    def conv(i, carry):
        total = jnp.zeros((ROWS, ROWS), F32)
        for j in range(TAPS):
            total = total + tapf[i, j:j + 1, :] * gext[i, j:j + ROWS, :]
        normed = total * gain[pl.ds(i, 1), :] + shift[pl.ds(i, 1), :]
        normed_s[i] = normed
        acts[i, :, my_frames] = (normed * jax.nn.sigmoid(normed)).T.astype(BF)
        return carry

    lax.fori_loop(0, NB, conv, 0)


    def acts_of(aa):
        return acts.at[:, :, frames_of(aa)]

    send(acts_of(a), acts_of(a), at_s.at[0], at_r.at[0], (par, t))
    send(acts_of(a), acts_of(a), at_s.at[1], at_r.at[1], (sib, t))

    for m in range(1, TENSOR):
        got(cand.at[lax.rem(t + m, TENSOR)], s1_r.at[TENSOR - m])
    r_rows = pl.ds(pl.multiple_of(r_slot * 32, 32), 32)
    for m in range(NBLK):
        x = m // Z
        zz = t if x else lax.rem(z + m, Z)
        slot = home[8 if x else zz]
        own, which = lax.shift_right_logical(slot, 1), slot & 1
        lpick[m] = cand[own, which, 0]
        rpick[m] = cand[own, which, 1]
        r_dev = zz * 4 + r_to
        l_dev = zz * 4 + a
        send(rpick.at[m], rrows.at[x, r_rows], r2_s.at[m], r2_r.at[x, r_slot], (r_dev, t), r_dev != d)
        pl.when(r_dev == d)(functools.partial(keep, rrows, (x, r_rows), rpick, m))
        send(lpick.at[m], lfull.at[x, z, a], l2_s.at[m], l2_r.at[x, z], (l_dev, t), l_dev != d)
        pl.when(l_dev == d)(functools.partial(keep, lfull, (x, z, a), lpick, m))

    off_relay, off_plain = 2 + 4 * c, 6 - 4 * c
    offs = (4, 3, 5, None, off_plain, 1, 7, 0, off_relay)

    def product(n, chip):
        block = Z if n == 3 else lax.rem(z + offs[n], Z)
        row, col = (2, 2) if n == 3 else (lax.div(block, NB), lax.rem(block, NB))
        span = pl.ds(pl.multiple_of(chip * 256, 256), 256)
        return dot(acts[row, :, span], ycols[col, span, :], ((1,), (0,)))

    y_own.wait()
    got(ycols.at[:, frames_of(a_sib)], ys_r.at[0])
    got(acts_of(a_sib), at_r.at[1])
    for n in range(NBLK):
        gacc[n] = product(n, yh)

    got(acts_of(a_par), at_r.at[0])
    send(acts_of(a_par), acts_of(a_par), at_s.at[2], at_r.at[2], (sib, t))
    for n, aa in enumerate((a_par, a_far)):
        for m in range(1, 4):
            got(piece_of(aa, lax.rem(my_x + 4 - m, 4)), yx_r.at[n, m])
    got(acts_of(a_far), at_r.at[2])

    e_off = lax.rem(z - t + Z, Z)
    e_far = (e_off > 1) & (e_off < 7)
    e_low = (e_off < 4) | ((e_off == 4) & (c == 0))
    e_via = at_z(jnp.where(e_low, t + 1, t - 1))

    def e_merge(sources, odd):
        for n in sources:
            got(erecv.at[n], ez_r.at[n])

        @pl.when(c == odd)
        def _():
            got(erecv.at[4], ez_r.at[4])

        @pl.when(c != odd)
        def _():
            erecv[4] = jnp.zeros((ROWS, QUART), BF)

        total = gacc[3] + erecv[4].astype(F32)
        for n in sources:
            total = total + erecv[n].astype(F32)
        zsend[3] = total.astype(BF)

    my_cols = pl.ds(pl.multiple_of(t * ROWS, ROWS), ROWS)

    def roots_in(x):
        for n in range(Z):
            source = 8 * quad + n
            rows = pl.ds(32 * n, 32)
            pl.when(source != d)(functools.partial(got, rrows.at[x, rows], r2_r.at[x, n]))
            pl.when(z != n)(functools.partial(got, lfull.at[x, n, a], l2_r.at[x, n]))
        rfull[x, :, my_cols] = rrows[x]

    def roots_out(x, when):
        for m in range(1, TENSOR):
            dev = diagonal(m) if x else (d, lax.rem(t + m, TENSOR))
            send(rrows.at[x], rfull.at[x, :, my_cols], r3_s.at[x, m], r3_r.at[x, m], dev, when)
        mine = lfull.at[x, :, a]
        send(mine, mine, l3_s.at[x, 0], l3_r.at[x, 0], (par, t), when)
        send(mine, mine, l3_s.at[x, 1], l3_r.at[x, 1], (sib, t), when)

    def left_on(x, when):
        his = lfull.at[x, :, a_par]
        if when is None:
            got(his, l3_r.at[x, 0])
        else:
            pl.when(when)(functools.partial(got, his, l3_r.at[x, 0]))
        send(his, his, l3_s.at[x, 2], l3_r.at[x, 2], (sib, t), when)

    for n in range(NBLK):
        if n == 3:
            roots_in(0)
            roots_out(0, None)
            pl.when(home_z)(functools.partial(roots_in, 1))
            roots_out(1, home_z)
        total = gacc[n] + product(n, 1 - yh)
        if n == 3:
            gacc[n] = total
            zsend[n] = total.astype(BF)
            send(zsend.at[n], erecv.at[e_off], ez_s.at[0], ez_r.at[e_off], (e_via, t), e_far)
        elif n == 0:
            zsend[n] = total.astype(BF)
            send(zsend.at[n], relay, z_s.at[n], z_r.at[4], (at_z(z + off_relay), t))
        elif n == 7:
            gacc[n] = total
        else:
            if n == 8:
                got(relay, z_r.at[4])
                total = total + relay[...].astype(F32)
            zsend[n] = total.astype(BF)
            send(
                zsend.at[n], zrecv.at[offs[n]], z_s.at[n], z_r.at[offs[n]],
                (at_z(z + offs[n]), t),
            )

    pl.when(e_off == 1)(functools.partial(e_merge, (2, 3), 0))
    pl.when(e_off == 7)(functools.partial(e_merge, (5, 6), 1))
    near = (e_off == 1) | (e_off == 7)
    send(zsend.at[3], erecv.at[e_off], ez_s.at[0], ez_r.at[e_off], (at_z(t), t), near)

    cot_copy.wait()
    w_copy.wait()
    for i in range(NB):
        grad = jnp.zeros((ROWS, ROWS), F32)
        for j in range(NB):
            grad = grad + dot(cot[j], weight[i, j], ((1,), (1,)))
        normed = normed_s[i]
        sg = jax.nn.sigmoid(normed)
        cg = (grad * sg * (1.0 + normed * (1.0 - sg)) * gain[i:i + 1, :]).astype(BF)
        cg_b[i] = cg
        cgext[i, HALF:HALF + ROWS, :] = cg.astype(F32)
    send(cg_b.at[:, 0:HALF], cg_halo.at[1], ch_s.at[0], ch_r.at[1], dn, left_ok)
    send(cg_b.at[:, ROWS - HALF:ROWS], cg_halo.at[0], ch_s.at[1], ch_r.at[0], up, right_ok)

    left_on(0, None)
    left_on(1, home_z)

    def tap_grad(i, carry):
        cg = cgext[i, HALF:HALF + ROWS, :]
        for j in range(TAPS):
            terms = (cg * gext[i, j:j + ROWS, :]).reshape(ROWS // 8, 8, ROWS)
            row = jnp.sum(jnp.sum(terms, axis=0), axis=0, keepdims=True)
            kpart[j // HALF, i, j % HALF:j % HALF + 1, :] = row
        return carry

    lax.fori_loop(0, NB, tap_grad, 0)
    send(kpart.at[1 - c], kin1, k_s.at[0], k_r.at[0], (sib, t))

    def roots_all(x):
        for m in range(1, TENSOR):
            tt = lax.rem(t + m, TENSOR)
            cols = pl.ds(pl.multiple_of(tt * ROWS, ROWS), ROWS)
            got(rfull.at[x, :, cols], r3_r.at[x, TENSOR - m])
        got(lfull.at[x, :, a_sib], l3_r.at[x, 1])
        got(lfull.at[x, :, a_far], l3_r.at[x, 2])
        for zz in range(Z):
            part = lfull[x, zz].reshape(ROWS, ROWS).astype(F32)
            lturn[x, :, ROWS * zz:ROWS * zz + ROWS] = part.T.astype(BF)

    def join(x):
        total = gacc[3 if x else 7]
        for n in range(Z):
            if x == 0 and n not in (0, 4):
                got(zrecv.at[n], z_r.at[n])
                total = total + zrecv[n].astype(F32)
            elif x == 1 and n in (1, 7):
                got(erecv.at[n], ez_r.at[n])
                total = total + erecv[n].astype(F32)
        gfull[x, quad] = total.astype(BF)

    par_quad = 2 * c + 1 - yh

    def quarters_out(x, when):
        mine = gfull.at[x, quad]
        send(mine, mine, c_s.at[x, 0], c_r.at[x, 0], (par, t), when)
        send(mine, mine, c_s.at[x, 1], c_r.at[x, 1], (sib, t), when)

    def quarters_on(x, when):
        his = gfull.at[x, par_quad]
        send(his, his, c_s.at[x, 2], c_r.at[x, 2], (sib, t), when)

    def quarters_in(x):
        got(gfull.at[x, 2 * (1 - c) + yh], c_r.at[x, 1])
        got(gfull.at[x, 2 * (1 - c) + 1 - yh], c_r.at[x, 2])

    join(0)
    quarters_out(0, None)
    pl.when(home_z)(functools.partial(join, 1))
    quarters_out(1, home_z)

    got(kin1, k_r.at[0])
    ksend2[...] = kpart[c] + kin1[...]
    send(ksend2, kin2, k_s.at[1], k_r.at[1], (par, t))

    roots_all(0)
    pl.when(home_z)(functools.partial(roots_all, 1))

    got(gfull.at[0, par_quad], c_r.at[0, 0])
    quarters_on(0, None)
    pl.when(home_z)(functools.partial(got, gfull.at[1, par_quad], c_r.at[1, 0]))
    quarters_on(1, home_z)
    quarters_in(0)

    def right(x):
        part = jnp.zeros((ROWS, QUART), F32)
        for q in range(QUADS):
            part = part + dot(gfull[x, q], rfull[x, :, QUART * q:QUART * q + QUART], ((1,), (1,)))
        wall[x, t] = (part * SHARE).astype(BF)

    right(0)
    for m in range(1, TENSOR):
        dev = (d, lax.rem(t + m, TENSOR))
        send(wall.at[0, t], wall.at[0, t], wt_s.at[0, m], wt_r.at[0, m], dev)

    @pl.when(home_z)
    def _():
        quarters_in(1)
        right(1)

    for m in range(1, TENSOR):
        send(wall.at[1, t], wall.at[1, t], wt_s.at[1, m], wt_r.at[1, m], diagonal(m), home_z)

    got(kin2, k_r.at[1])
    ksum[...] = ksend2[...] + kin2[...]
    for m in range(1, Z):
        send(ksum, kz.at[z], k_s.at[1 + m], k_r.at[1 + m], (at_z(z + m), t))
    kz[z] = ksum[...]

    rim(0, left_ok, ch_r, cg_halo, cgext, low)
    rim(1, right_ok, ch_r, cg_halo, cgext, high)

    for i in range(NB):
        total = jnp.zeros((ROWS, ROWS), F32)
        for j in range(TAPS):
            total = total + tapf[i, j:j + 1, :] * cgext[i, TAPS - j:TAPS - j + ROWS, :]
        lin, gate = halves(i)
        sg = jax.nn.sigmoid(gate)
        total = total * sg
        ggrad[:, i, 0, :] = total.astype(BF)
        ggrad[:, i, 1, :] = (total * lin * (1.0 - sg)).astype(BF)

    def quarter(block, q):
        cols = pl.ds(pl.multiple_of(q * QUART, QUART), QUART)
        return upd.at[lax.div(block, NB), lax.rem(block, NB), :, cols]

    def left_mult(x, block):
        for m in range(1, TENSOR):
            got(wall.at[x, lax.rem(t + m, TENSOR)], wt_r.at[x, TENSOR - m])
        part = dot(lturn[x], wall[x].reshape(BLOCK, QUART), ((1,), (0,)))
        quarter(block, quad)[...] = part.astype(BF)

    second = jnp.int32(Z)
    sib_quads = (2 * (1 - c) + yh, 2 * (1 - c) + 1 - yh)

    def piece(n, q):
        return quarter(second if n == Z else lax.rem(z + n, Z), q)

    def on(n, h, when=None):
        src = piece(n, par_quad if h else quad)
        if h == 0 and n not in (1, 7):
            send(src, src, uy_s.at[n], uy_r.at[n], (par, t), when)
        send(src, src, us_s.at[n, h], us_r.at[n, h], (sib, t), when)

    left_mult(0, z)
    for off in (3, 5, 2, 6, 1, 7):
        src = piece(0, quad)
        send(src, src, uz_s.at[off], uz_r.at[off], (at_z(z + off), t))
    on(0, 0)

    @pl.when(home_z)
    def _():
        left_mult(1, second)

    for off in (3, 5, 2, 6, 1, 7):
        src = piece(Z, quad)
        send(src, src, uz_s.at[Z + off], uz_r.at[Z], (at_z(z + off), t), home_z)

    for m in range(1, Z):
        got(kz.at[lax.rem(z + m, Z)], k_r.at[1 + Z - m])
    total = kz[0]
    for zz in range(1, Z):
        total = total + kz[zz]
    khalf[c] = total * SHARE
    send(khalf.at[c], khalf.at[c], k_s.at[9], k_r.at[9], (sib, t))

    got(piece(0, par_quad), uy_r.at[0])
    for off in (1, 7):
        src = piece(0, par_quad)
        send(src, src, uy_s.at[off], uy_r.at[Z - off], (at_z(z + off), t))
    on(0, 1)

    def pass_on(n, land, when):
        src = piece(n, quad)
        send(src, src, uz_s.at[4 + land], uz_r.at[land], (at_z(z - 1 + 2 * c), t), when)

    for off in (3, 5, 2, 6, 1, 7):
        got(piece(off, quad), uz_r.at[Z - off])
        if off == 3:
            pass_on(3, 4, c == 0)
        if off == 5:
            pass_on(5, 4, c == 1)
        on(off, 0)
    pl.when(jnp.logical_not(home_z))(functools.partial(got, piece(Z, quad), uz_r.at[Z]))
    pass_on(Z, Z, lax.rem(t - z + Z, Z) == 3 + 2 * c)
    on(Z, 0)
    got(piece(4, quad), uz_r.at[4])
    on(4, 0)
    for n in (1, 7, 3, 5, 2, 6, Z, 4):
        got(piece(n, par_quad), uy_r.at[n])
        on(n, 1)

    got(khalf.at[1 - c], k_r.at[9])
    for half in range(2):
        for i in range(NB):
            kgrad[i, HALF * half:HALF * half + HALF, :] = khalf[half, i]

    for n in range(Z + 1):
        for h in range(2):
            got(piece(n, sib_quads[h]), us_r.at[n, h])

    for copy, when in sends:
        if when is None:
            copy.wait_send()
        else:
            pl.when(when)(copy.wait_send)


def hand_over(upd, kgrad, ggrad, upd_out, kgrad_out, ggrad_out, upd_v, kgrad_v, ggrad_v, ins, outs):
    legs = [(kgrad, kgrad_v, kgrad_out), (ggrad, ggrad_v, ggrad_out)]
    for b in range(NBLK):
        at = (b // NB, b % NB)
        legs.append((upd.at[at], upd_v.at[at], upd_out.at[at]))
    arrive = [pltpu.make_async_copy(x, y, ins.at[n]) for n, (x, y, _) in enumerate(legs)]
    leave = [pltpu.make_async_copy(y, w, outs.at[n]) for n, (_, y, w) in enumerate(legs)]
    for copy in arrive:
        copy.start()
    for copy, then in zip(arrive, leave):
        copy.wait()
        then.start()
    for copy in leave:
        copy.wait()


def per_device(
    glu_input, conv_kernel, norm_gain, norm_shift, out_weight, out_cotangent, root_stack, home
):
    vmem = pl.BlockSpec(memory_space=pltpu.VMEM)
    hbm = pl.BlockSpec(memory_space=pltpu.HBM)
    dma = pltpu.SemaphoreType.DMA
    sq = (NB, ROWS, ROWS)
    out = pl.pallas_call(
        kernel,
        out_shape=(
            jax.ShapeDtypeStruct((NB, NB, ROWS, BLOCK), BF),
            jax.ShapeDtypeStruct((NB, TAPS, ROWS), F32),
            jax.ShapeDtypeStruct((ROWS, NB, 2, ROWS), BF),
        ),
        in_specs=[
            pl.BlockSpec(memory_space=pltpu.SMEM), hbm, hbm, hbm, hbm, vmem, vmem, vmem,
        ],
        out_specs=(vmem, vmem, vmem),
        scratch_shapes=[
            pltpu.VMEM((ROWS, NB, 2, ROWS), BF),
            pltpu.VMEM(sq, BF),
            pltpu.VMEM((NB, ROWS, BLOCK), BF),
            pltpu.VMEM((2, 2, 32, BLOCK), BF),
            pltpu.VMEM((NB, TAPS, ROWS), F32),
            pltpu.VMEM((TENSOR, 2, 2, 32, ROWS), BF),
            pltpu.VMEM((NBLK, 32, ROWS), BF),
            pltpu.VMEM((NBLK, 32, ROWS), BF),
            pltpu.VMEM((2, QUART, ROWS), BF),
            pltpu.VMEM((2, QUART, BLOCK), BF),
            pltpu.VMEM((2, Z, QUADS, 32, ROWS), BF),
            pltpu.VMEM((2, ROWS, BLOCK), BF),
            pltpu.VMEM((2, NB, HALF, ROWS), BF),
            pltpu.VMEM((2, NB, HALF, ROWS), BF),
            pltpu.VMEM((NB, ROWS + TAPS, ROWS), F32),
            pltpu.VMEM(sq, F32),
            pltpu.VMEM(sq, BF),
            pltpu.VMEM((NB, ROWS + TAPS, ROWS), F32),
            pltpu.VMEM((NB, NB, ROWS, BLOCK), BF),
            pltpu.VMEM((NB, ROWS, QUADS * ROWS), BF),
            pltpu.VMEM((NB, QUADS * ROWS, QUART), BF),
            pltpu.VMEM((NBLK, ROWS, QUART), F32),
            pltpu.VMEM((ROWS, QUART), BF),
            pltpu.VMEM((NBLK, ROWS, QUART), BF),
            pltpu.VMEM((Z, ROWS, QUART), BF),
            pltpu.VMEM((Z, ROWS, QUART), BF),
            pltpu.VMEM((2, QUADS, ROWS, QUART), BF),
            pltpu.VMEM((2, TENSOR, ROWS, QUART), BF),
            pltpu.VMEM((2, NB, HALF, ROWS), F32),
            pltpu.VMEM((NB, HALF, ROWS), F32),
            pltpu.VMEM((NB, HALF, ROWS), F32),
            pltpu.VMEM((NB, HALF, ROWS), F32),
            pltpu.VMEM((NB, HALF, ROWS), F32),
            pltpu.VMEM((Z, NB, HALF, ROWS), F32),
            pltpu.VMEM((2, NB, HALF, ROWS), F32),
            dma, dma, dma, dma,
            dma((2,)), dma((2,)),
            dma((8,)), dma((8,)),
            dma((9,)), dma((2, 8)),
            dma((9,)), dma((2, 8)),
            dma((2, 8)), dma((2, 8)),
            dma((2, 4)), dma((2, 4)),
            dma((2,)), dma((2,)),
            dma((1,)), dma((1,)),
            dma((2, 4)), dma((2, 4)),
            dma((3,)), dma((3,)),
            dma,
            dma((9,)), dma((8,)),
            dma((1,)), dma((8,)),
            dma((2, 3)), dma((2, 3)),
            dma((2, 8)), dma((2, 8)),
            dma((16,)), dma((9,)),
            dma((9,)), dma((9,)),
            dma((9, 2)), dma((9, 2)),
            dma((2,)), dma((2,)),
            dma((10,)), dma((10,)),
        ],
        compiler_params=pltpu.CompilerParams(
            collective_id=0, has_side_effects=True, vmem_limit_bytes=60 * 2**20
        ),
    )(
        home, glu_input.transpose(0, 2, 1, 3), out_weight.transpose(0, 2, 1, 3), out_cotangent.transpose(1, 0, 2),
        root_stack, conv_kernel.transpose(1, 0, 2), norm_gain, norm_shift,
    )
    update, kernel_grad, glu_grad = pl.pallas_call(
        hand_over,
        out_shape=[jax.ShapeDtypeStruct(x.shape, x.dtype) for x in out],
        in_specs=[hbm] * 3,
        out_specs=[hbm] * 3,
        scratch_shapes=[pltpu.VMEM(x.shape, x.dtype) for x in out]
        + [dma((NBLK + 2,)), dma((NBLK + 2,))],
        compiler_params=pltpu.CompilerParams(vmem_limit_bytes=60 * 2**20),
    )(*out)
    return glu_grad.transpose(0, 2, 1, 3), kernel_grad.transpose(1, 0, 2), update.transpose(0, 2, 1, 3)


def solution(mesh):
    placed = (
        P("dp", None, None, "tensor"),
        P(None, None, "tensor"),
        P(None, "tensor"),
        P(None, "tensor"),
        P(None, "tensor", None, None),
        P("dp", None, None),
        P("tensor", None, "dp", None),
        P(),
    )
    return jax.shard_map(
        per_device,
        mesh=mesh,
        in_specs=placed,
        out_specs=(
            P("dp", None, None, "tensor"),
            P(None, None, "tensor"),
            P(None, "tensor", None, None),
        ),
        check_vma=False,
    )
```

```python
import functools

import jax
import jax.numpy as jnp
from jax import lax
from jax.experimental import pallas as pl
from jax.experimental.pallas import tpu as pltpu
from jax.sharding import PartitionSpec as P

LEN = 2048
MESH = pl.DeviceIdType.MESH
BF = jnp.bfloat16
F32 = jnp.float32

Z = 8
QUADS = 4
TENSOR = 8
TAPS = 32
HALF = TAPS // 2
ROWS = 128
BLOCK = 1024
NB = 3
NBLK = 9
QUART = BLOCK // 4
SHARE = LEN / (ROWS * Z * QUADS)

ORDER = (4, 3, 5, 2, 6, 1, 7, 0)
SPOT = {off: k for k, off in enumerate(ORDER)}
HOPS = ((4, 3), (3, 4))


def dot(a, b, dims):
    return lax.dot_general(a, b, (dims, ((), ())), preferred_element_type=F32)


def keep(dst, at, src, m):
    dst[at] = src[m]


def kernel(
    home, glu_hbm, weight_hbm, cot_hbm, roots_hbm, taps, gain, shift,
    upd, kgrad, ggrad,
    raw, glu, cot, roots, tapf, cand, rpick, lpick, rrows, rfull, lfull, lturn,
    halo, cg_halo, gext, normed_s, cg_b, cgext, weight,
    acts, ycols, gacc, relay, zsend, zrecv, erecv, gfull, wall,
    kpart, kin1, ksend2, kin2, ksum, kz, khalf,
    raw_sem, w_sem, cot_sem, roots_sem, halo_s, halo_r, s1_s, s1_r, r2_s, r2_r, l2_s, l2_r,
    r3_s, r3_r, l3_s, l3_r, yc_s, yc_r, ys_s, ys_r, yx_s, yx_r, at_s, at_r, yc_own, z_s, z_r, ez_s, ez_r,
    c_s, c_r, wt_s, wt_r, uz_s, uz_r, uy_s, uy_r, us_s, us_r, ch_s, ch_r, k_s, k_r,
):
    d = lax.axis_index("dp")
    t = lax.axis_index("tensor")
    z = lax.div(d, 4)
    a = lax.rem(d, 4)
    yh = lax.div(a, 2)
    c = lax.rem(a, 2)
    sib = d + 1 - 2 * c
    par = d + 2 - 4 * yh

    def at_z(zz):
        return lax.rem(zz + 2 * Z, Z) * 4 + a

    quad = 2 * c + yh
    home_z = z == t

    def diagonal(m):
        tt = lax.rem(t + m, TENSOR)
        return (tt * 4 + a, tt)

    sends = []

    def send(src, dst, ss, rs, dev, when=None):
        copy = pltpu.make_async_remote_copy(
            src_ref=src, dst_ref=dst, send_sem=ss, recv_sem=rs,
            device_id=dev, device_id_type=MESH,
        )
        if when is None:
            copy.start()
        else:
            pl.when(when)(copy.start)
        sends.append((copy, when))

    def got(dst, rs):
        pltpu.make_async_remote_copy(
            src_ref=dst, dst_ref=dst, send_sem=s1_s.at[0], recv_sem=rs,
            device_id=(sib, t), device_id_type=MESH,
        ).wait_recv()

    barrier = pltpu.get_barrier_semaphore()

    def hello(dev):
        pl.semaphore_signal(barrier, inc=1, device_id=dev, device_id_type=MESH)

    hello((lax.rem(d + 31, 32), t))
    hello((lax.rem(d + 1, 32), t))
    for m in range(1, 4):
        hello((z * 4 + lax.rem(a + m, 4), t))
    for m in range(1, Z):
        hello((at_z(z + m), t))
    for m in range(1, TENSOR):
        hello((d, lax.rem(t + m, TENSOR)))

    r_quad = lax.div(z, 2)
    r_to = lax.rem(r_quad, 2) * 2 + lax.div(r_quad, 2)
    r_slot = lax.rem(z, 2) * 4 + a

    for n in range(Z):
        pl.when(8 * quad + n != d)(functools.partial(hello, (8 * quad + n, t)))
    for m in range(1, TENSOR):
        pl.when(home_z)(functools.partial(hello, diagonal(m)))

    raw_copy = pltpu.make_async_copy(glu_hbm, raw, raw_sem)
    raw_copy.start()
    roots_copy = pltpu.make_async_copy(roots_hbm, roots, roots_sem)
    roots_copy.start()
    cot_copy = pltpu.make_async_copy(cot_hbm, cot, cot_sem)
    cot_copy.start()
    w_copy = pltpu.make_async_copy(weight_hbm, weight, w_sem)
    w_copy.start()

    left_ok = (d != 0) & (lax.rem(d * ROWS + LEN // 2, LEN) != 0)
    right_ok = (d != 31) & (lax.rem((d + 1) * ROWS + LEN // 2, LEN) != 0)
    raw_copy.wait()

    def halves(i):
        both = raw[:, i].astype(F32)
        return both[:, 0, :], both[:, 1, :]

    for i in range(NB):
        lin, gate = halves(i)
        glu[i] = (lin * jax.nn.sigmoid(gate)).astype(BF)
        gext[i, HALF:HALF + ROWS, :] = glu[i].astype(F32)
        tapf[i] = taps[i].astype(F32)

    more = jnp.where(home_z, TENSOR - 1, 0) - jnp.where(r_to == a, 1, 0)
    pl.semaphore_wait(barrier, 2 + 3 + Z - 1 + TENSOR - 1 + Z + more)

    dn, up = (lax.rem(d + 31, 32), t), (lax.rem(d + 1, 32), t)
    send(glu.at[:, 0:HALF], halo.at[1], halo_s.at[0], halo_r.at[1], dn, left_ok)
    send(glu.at[:, ROWS - HALF:ROWS], halo.at[0], halo_s.at[1], halo_r.at[0], up, right_ok)
    roots_copy.wait()
    def quad_of(aa):
        return 2 * lax.rem(aa, 2) + lax.div(aa, 2)

    def quad_cols(aa):
        return pl.ds(pl.multiple_of(quad_of(aa) * QUART, QUART), QUART)

    def frames_of(aa):
        return pl.ds(pl.multiple_of(aa * ROWS, ROWS), ROWS)

    my_frames = frames_of(a)
    y_own = pltpu.make_async_copy(cot_hbm.at[:, :, quad_cols(a)], ycols.at[:, my_frames], yc_own)
    y_own.start()
    a_par, a_sib, a_far = a + 2 - 4 * yh, a + 1 - 2 * c, 3 - a
    my_x = lax.rem(t, 4)

    def piece_of(aa, xx):
        rows = pl.ds(pl.multiple_of(aa * ROWS + xx * 32, 32), 32)
        return ycols.at[:, rows]

    x_rows = pl.ds(pl.multiple_of(my_x * 32, 32), 32)
    for n, aa in enumerate((a_par, a_far)):
        src = cot_hbm.at[:, x_rows, quad_cols(aa)]
        send(src, piece_of(a, my_x), yc_s.at[n], yc_r.at[n], (z * 4 + aa, t))
    src = cot_hbm.at[:, :, quad_cols(a_sib)]
    send(src, ycols.at[:, my_frames], ys_s.at[0], ys_r.at[0], (sib, t))

    for m in range(1, TENSOR):
        tt = lax.rem(t + m, TENSOR)
        share_cols = pl.ds(pl.multiple_of(tt * ROWS, ROWS), ROWS)
        send(roots.at[:, :, :, share_cols], cand.at[t], s1_s.at[m], s1_r.at[m], (d, tt))
    cand[t] = roots[:, :, :, pl.ds(pl.multiple_of(t * ROWS, ROWS), ROWS)]

    def rim(side, ok, sem, src, dst, rows):
        @pl.when(ok)
        def _():
            got(src.at[side], sem.at[side])
            for i in range(NB):
                dst[i, rows, :] = src[side, i].astype(F32)

        @pl.when(jnp.logical_not(ok))
        def _():
            for i in range(NB):
                dst[i, rows, :] = jnp.zeros((HALF, ROWS), F32)

    low, high = pl.ds(0, HALF), pl.ds(HALF + ROWS, HALF)
    rim(0, left_ok, halo_r, halo, gext, low)
    rim(1, right_ok, halo_r, halo, gext, high)

    for n, aa in enumerate((a_par, a_far)):
        src = piece_of(aa, my_x)
        got(src, yc_r.at[n])
        for m in range(1, 4):
            dev = (d, t - my_x + lax.rem(my_x + m, 4))
            send(src, src, yx_s.at[n, m], yx_r.at[n, m], dev)

    def conv(i, carry):
        total = jnp.zeros((ROWS, ROWS), F32)
        for j in range(TAPS):
            total = total + tapf[i, j:j + 1, :] * gext[i, j:j + ROWS, :]
        normed = total * gain[pl.ds(i, 1), :] + shift[pl.ds(i, 1), :]
        normed_s[i] = normed
        acts[i, :, my_frames] = (normed * jax.nn.sigmoid(normed)).T.astype(BF)
        return carry


    def acts_of(aa):
        return acts.at[:, :, frames_of(aa)]

    for i in range(NB):
        conv(i, 0)
        mine = acts.at[i, :, my_frames]
        send(mine, mine, at_s.at[i], at_r.at[i], (par, t))
    send(acts_of(a), acts_of(a), at_s.at[3], at_r.at[3], (sib, t))

    for m in range(1, TENSOR):
        got(cand.at[lax.rem(t + m, TENSOR)], s1_r.at[TENSOR - m])
    r_rows = pl.ds(pl.multiple_of(r_slot * 32, 32), 32)
    for m in range(NBLK):
        x = m // Z
        zz = t if x else lax.rem(z + m, Z)
        slot = home[8 if x else zz]
        own, which = lax.shift_right_logical(slot, 1), slot & 1
        lpick[m] = cand[own, which, 0]
        rpick[m] = cand[own, which, 1]
        r_dev = zz * 4 + r_to
        l_dev = zz * 4 + a
        send(rpick.at[m], rrows.at[x, r_rows], r2_s.at[m], r2_r.at[x, r_slot], (r_dev, t), r_dev != d)
        pl.when(r_dev == d)(functools.partial(keep, rrows, (x, r_rows), rpick, m))
        send(lpick.at[m], lfull.at[x, z, a], l2_s.at[m], l2_r.at[x, z], (l_dev, t), l_dev != d)
        pl.when(l_dev == d)(functools.partial(keep, lfull, (x, z, a), lpick, m))

    off_relay, off_plain = 2 + 4 * c, 6 - 4 * c
    offs = (4, 3, 5, None, off_plain, 1, 7, 0, off_relay)

    def product(n, chip):
        block = Z if n == 3 else lax.rem(z + offs[n], Z)
        row, col = (2, 2) if n == 3 else (lax.div(block, NB), lax.rem(block, NB))
        span = pl.ds(pl.multiple_of(chip * 256, 256), 256)
        return dot(acts[row, :, span], ycols[col, span, :], ((1,), (0,)))

    y_own.wait()
    got(ycols.at[:, frames_of(a_sib)], ys_r.at[0])
    got(acts_of(a_sib), at_r.at[3])
    for n in range(NBLK):
        gacc[n] = product(n, yh)

    for i in range(NB):
        his = acts.at[i, :, frames_of(a_par)]
        got(his, at_r.at[i])
        send(his, his, at_s.at[4 + i], at_r.at[4 + i], (sib, t))
    for n, aa in enumerate((a_par, a_far)):
        for m in range(1, 4):
            got(piece_of(aa, lax.rem(my_x + 4 - m, 4)), yx_r.at[n, m])
    for i in range(NB):
        got(acts.at[i, :, frames_of(a_far)], at_r.at[4 + i])

    e_off = lax.rem(z - t + Z, Z)
    e_far = (e_off > 1) & (e_off < 7)
    e_low = (e_off < 4) | ((e_off == 4) & (c == 0))
    e_via = at_z(jnp.where(e_low, t + 1, t - 1))

    def e_merge(sources, odd):
        for n in sources:
            got(erecv.at[n], ez_r.at[n])

        @pl.when(c == odd)
        def _():
            got(erecv.at[4], ez_r.at[4])

        @pl.when(c != odd)
        def _():
            erecv[4] = jnp.zeros((ROWS, QUART), BF)

        total = gacc[3] + erecv[4].astype(F32)
        for n in sources:
            total = total + erecv[n].astype(F32)
        zsend[3] = total.astype(BF)

    my_cols = pl.ds(pl.multiple_of(t * ROWS, ROWS), ROWS)

    def roots_in(x):
        for n in range(Z):
            source = 8 * quad + n
            rows = pl.ds(32 * n, 32)
            pl.when(source != d)(functools.partial(got, rrows.at[x, rows], r2_r.at[x, n]))
            pl.when(z != n)(functools.partial(got, lfull.at[x, n, a], l2_r.at[x, n]))
        rfull[x, :, my_cols] = rrows[x]

    def roots_out(x, when):
        for m in range(1, TENSOR):
            dev = diagonal(m) if x else (d, lax.rem(t + m, TENSOR))
            send(rrows.at[x], rfull.at[x, :, my_cols], r3_s.at[x, m], r3_r.at[x, m], dev, when)
        mine = lfull.at[x, :, a]
        send(mine, mine, l3_s.at[x, 0], l3_r.at[x, 0], (par, t), when)
        send(mine, mine, l3_s.at[x, 1], l3_r.at[x, 1], (sib, t), when)

    def left_on(x, when):
        his = lfull.at[x, :, a_par]
        if when is None:
            got(his, l3_r.at[x, 0])
        else:
            pl.when(when)(functools.partial(got, his, l3_r.at[x, 0]))
        send(his, his, l3_s.at[x, 2], l3_r.at[x, 2], (sib, t), when)

    for n in range(NBLK):
        if n == 8:
            roots_in(0)
            roots_out(0, None)
            pl.when(home_z)(functools.partial(roots_in, 1))
            roots_out(1, home_z)
        total = gacc[n] + product(n, 1 - yh)
        if n == 3:
            gacc[n] = total
            zsend[n] = total.astype(BF)
            send(zsend.at[n], erecv.at[e_off], ez_s.at[0], ez_r.at[e_off], (e_via, t), e_far)
        elif n == 0:
            zsend[n] = total.astype(BF)
            send(zsend.at[n], relay, z_s.at[n], z_r.at[4], (at_z(z + off_relay), t))
        elif n == 7:
            gacc[n] = total
        else:
            if n == 8:
                got(relay, z_r.at[4])
                total = total + relay[...].astype(F32)
            zsend[n] = total.astype(BF)
            send(
                zsend.at[n], zrecv.at[offs[n]], z_s.at[n], z_r.at[offs[n]],
                (at_z(z + offs[n]), t),
            )

    pl.when(e_off == 1)(functools.partial(e_merge, (2, 3), 0))
    pl.when(e_off == 7)(functools.partial(e_merge, (5, 6), 1))
    near = (e_off == 1) | (e_off == 7)
    send(zsend.at[3], erecv.at[e_off], ez_s.at[0], ez_r.at[e_off], (at_z(t), t), near)

    cot_copy.wait()
    w_copy.wait()
    for i in range(NB):
        grad = jnp.zeros((ROWS, ROWS), F32)
        for j in range(NB):
            grad = grad + dot(cot[j], weight[i, j], ((1,), (1,)))
        normed = normed_s[i]
        sg = jax.nn.sigmoid(normed)
        cg = (grad * sg * (1.0 + normed * (1.0 - sg)) * gain[i:i + 1, :]).astype(BF)
        cg_b[i] = cg
        cgext[i, HALF:HALF + ROWS, :] = cg.astype(F32)
    send(cg_b.at[:, 0:HALF], cg_halo.at[1], ch_s.at[0], ch_r.at[1], dn, left_ok)
    send(cg_b.at[:, ROWS - HALF:ROWS], cg_halo.at[0], ch_s.at[1], ch_r.at[0], up, right_ok)

    left_on(0, None)
    left_on(1, home_z)

    def tap_grad(i, carry):
        cg = cgext[i, HALF:HALF + ROWS, :]
        for j in range(TAPS):
            terms = (cg * gext[i, j:j + ROWS, :]).reshape(ROWS // 8, 8, ROWS)
            row = jnp.sum(jnp.sum(terms, axis=0), axis=0, keepdims=True)
            kpart[j // HALF, i, j % HALF:j % HALF + 1, :] = row
        return carry

    lax.fori_loop(0, NB, tap_grad, 0)
    send(kpart.at[1 - c], kin1, k_s.at[0], k_r.at[0], (sib, t))

    def roots_all(x):
        for m in range(1, TENSOR):
            tt = lax.rem(t + m, TENSOR)
            cols = pl.ds(pl.multiple_of(tt * ROWS, ROWS), ROWS)
            got(rfull.at[x, :, cols], r3_r.at[x, TENSOR - m])
        got(lfull.at[x, :, a_sib], l3_r.at[x, 1])
        got(lfull.at[x, :, a_far], l3_r.at[x, 2])
        for zz in range(Z):
            part = lfull[x, zz].reshape(ROWS, ROWS).astype(F32)
            lturn[x, :, ROWS * zz:ROWS * zz + ROWS] = part.T.astype(BF)

    def join(x):
        total = gacc[3 if x else 7]
        for n in range(Z):
            if x == 0 and n not in (0, 4):
                got(zrecv.at[n], z_r.at[n])
                total = total + zrecv[n].astype(F32)
            elif x == 1 and n in (1, 7):
                got(erecv.at[n], ez_r.at[n])
                total = total + erecv[n].astype(F32)
        gfull[x, quad] = total.astype(BF)

    par_quad = 2 * c + 1 - yh

    def quarters_out(x, when):
        mine = gfull.at[x, quad]
        send(mine, mine, c_s.at[x, 0], c_r.at[x, 0], (par, t), when)
        send(mine, mine, c_s.at[x, 1], c_r.at[x, 1], (sib, t), when)

    def quarters_on(x, when):
        his = gfull.at[x, par_quad]
        send(his, his, c_s.at[x, 2], c_r.at[x, 2], (sib, t), when)

    def quarters_in(x):
        got(gfull.at[x, 2 * (1 - c) + yh], c_r.at[x, 1])
        got(gfull.at[x, 2 * (1 - c) + 1 - yh], c_r.at[x, 2])

    join(0)
    quarters_out(0, None)
    pl.when(home_z)(functools.partial(join, 1))
    quarters_out(1, home_z)

    got(kin1, k_r.at[0])
    ksend2[...] = kpart[c] + kin1[...]
    send(ksend2, kin2, k_s.at[1], k_r.at[1], (par, t))

    roots_all(0)
    pl.when(home_z)(functools.partial(roots_all, 1))

    got(gfull.at[0, par_quad], c_r.at[0, 0])
    quarters_on(0, None)
    pl.when(home_z)(functools.partial(got, gfull.at[1, par_quad], c_r.at[1, 0]))
    quarters_on(1, home_z)
    quarters_in(0)

    def right(x):
        part = jnp.zeros((ROWS, QUART), F32)
        for q in range(QUADS):
            part = part + dot(gfull[x, q], rfull[x, :, QUART * q:QUART * q + QUART], ((1,), (1,)))
        wall[x, t] = (part * SHARE).astype(BF)

    right(0)
    for m in range(1, TENSOR):
        dev = (d, lax.rem(t + m, TENSOR))
        send(wall.at[0, t], wall.at[0, t], wt_s.at[0, m], wt_r.at[0, m], dev)

    @pl.when(home_z)
    def _():
        quarters_in(1)
        right(1)

    for m in range(1, TENSOR):
        send(wall.at[1, t], wall.at[1, t], wt_s.at[1, m], wt_r.at[1, m], diagonal(m), home_z)

    got(kin2, k_r.at[1])
    ksum[...] = ksend2[...] + kin2[...]
    for m in range(1, Z):
        send(ksum, kz.at[z], k_s.at[1 + m], k_r.at[1 + m], (at_z(z + m), t))
    kz[z] = ksum[...]

    rim(0, left_ok, ch_r, cg_halo, cgext, low)
    rim(1, right_ok, ch_r, cg_halo, cgext, high)

    for i in range(NB):
        total = jnp.zeros((ROWS, ROWS), F32)
        for j in range(TAPS):
            total = total + tapf[i, j:j + 1, :] * cgext[i, TAPS - j:TAPS - j + ROWS, :]
        lin, gate = halves(i)
        sg = jax.nn.sigmoid(gate)
        total = total * sg
        ggrad[:, i, 0, :] = total.astype(BF)
        ggrad[:, i, 1, :] = (total * lin * (1.0 - sg)).astype(BF)

    def quarter(block, q):
        cols = pl.ds(pl.multiple_of(q * QUART, QUART), QUART)
        return upd.at[lax.div(block, NB), lax.rem(block, NB), :, cols]

    def left_mult(x, block):
        for m in range(1, TENSOR):
            got(wall.at[x, lax.rem(t + m, TENSOR)], wt_r.at[x, TENSOR - m])
        part = dot(lturn[x], wall[x].reshape(BLOCK, QUART), ((1,), (0,)))
        quarter(block, quad)[...] = part.astype(BF)

    second = jnp.int32(Z)
    sib_quads = (2 * (1 - c) + yh, 2 * (1 - c) + 1 - yh)

    def piece(n, q):
        return quarter(second if n == Z else lax.rem(z + n, Z), q)

    def on(n, h, when=None):
        src = piece(n, par_quad if h else quad)
        if h == 0 and n not in (1, 7):
            send(src, src, uy_s.at[n], uy_r.at[n], (par, t), when)
        send(src, src, us_s.at[n, h], us_r.at[n, h], (sib, t), when)

    left_mult(0, z)
    for off in (3, 5, 2, 6, 1, 7):
        src = piece(0, quad)
        send(src, src, uz_s.at[off], uz_r.at[off], (at_z(z + off), t))
    on(0, 0)

    @pl.when(home_z)
    def _():
        left_mult(1, second)

    for off in (3, 5, 2, 6, 1, 7):
        src = piece(Z, quad)
        send(src, src, uz_s.at[Z + off], uz_r.at[Z], (at_z(z + off), t), home_z)

    for m in range(1, Z):
        got(kz.at[lax.rem(z + m, Z)], k_r.at[1 + Z - m])
    total = kz[0]
    for zz in range(1, Z):
        total = total + kz[zz]
    khalf[c] = total * SHARE
    send(khalf.at[c], khalf.at[c], k_s.at[9], k_r.at[9], (sib, t))

    got(piece(0, par_quad), uy_r.at[0])
    for off in (1, 7):
        src = piece(0, par_quad)
        send(src, src, uy_s.at[off], uy_r.at[Z - off], (at_z(z + off), t))
    on(0, 1)

    def pass_on(n, land, when):
        src = piece(n, quad)
        send(src, src, uz_s.at[4 + land], uz_r.at[land], (at_z(z - 1 + 2 * c), t), when)

    for off in (3, 5, 2, 6, 1, 7):
        got(piece(off, quad), uz_r.at[Z - off])
        if off == 3:
            pass_on(3, 4, c == 0)
        if off == 5:
            pass_on(5, 4, c == 1)
        on(off, 0)
    pl.when(jnp.logical_not(home_z))(functools.partial(got, piece(Z, quad), uz_r.at[Z]))
    pass_on(Z, Z, lax.rem(t - z + Z, Z) == 3 + 2 * c)
    on(Z, 0)
    got(piece(4, quad), uz_r.at[4])
    on(4, 0)
    for n in (1, 7, 3, 5, 2, 6, Z, 4):
        got(piece(n, par_quad), uy_r.at[n])
        on(n, 1)

    got(khalf.at[1 - c], k_r.at[9])
    for half in range(2):
        for i in range(NB):
            kgrad[i, HALF * half:HALF * half + HALF, :] = khalf[half, i]

    for n in range(Z + 1):
        for h in range(2):
            got(piece(n, sib_quads[h]), us_r.at[n, h])

    for copy, when in sends:
        if when is None:
            copy.wait_send()
        else:
            pl.when(when)(copy.wait_send)


def hand_over(upd, kgrad, ggrad, upd_out, kgrad_out, ggrad_out, upd_v, kgrad_v, ggrad_v, ins, outs):
    legs = [(kgrad, kgrad_v, kgrad_out), (ggrad, ggrad_v, ggrad_out)]
    for b in range(NBLK):
        at = (b // NB, b % NB)
        legs.append((upd.at[at], upd_v.at[at], upd_out.at[at]))
    arrive = [pltpu.make_async_copy(x, y, ins.at[n]) for n, (x, y, _) in enumerate(legs)]
    leave = [pltpu.make_async_copy(y, w, outs.at[n]) for n, (_, y, w) in enumerate(legs)]
    for copy in arrive:
        copy.start()
    for copy, then in zip(arrive, leave):
        copy.wait()
        then.start()
    for copy in leave:
        copy.wait()


def per_device(
    glu_input, conv_kernel, norm_gain, norm_shift, out_weight, out_cotangent, root_stack, home
):
    vmem = pl.BlockSpec(memory_space=pltpu.VMEM)
    hbm = pl.BlockSpec(memory_space=pltpu.HBM)
    dma = pltpu.SemaphoreType.DMA
    sq = (NB, ROWS, ROWS)
    out = pl.pallas_call(
        kernel,
        out_shape=(
            jax.ShapeDtypeStruct((NB, NB, ROWS, BLOCK), BF),
            jax.ShapeDtypeStruct((NB, TAPS, ROWS), F32),
            jax.ShapeDtypeStruct((ROWS, NB, 2, ROWS), BF),
        ),
        in_specs=[
            pl.BlockSpec(memory_space=pltpu.SMEM), hbm, hbm, hbm, hbm, vmem, vmem, vmem,
        ],
        out_specs=(vmem, vmem, vmem),
        scratch_shapes=[
            pltpu.VMEM((ROWS, NB, 2, ROWS), BF),
            pltpu.VMEM(sq, BF),
            pltpu.VMEM((NB, ROWS, BLOCK), BF),
            pltpu.VMEM((2, 2, 32, BLOCK), BF),
            pltpu.VMEM((NB, TAPS, ROWS), F32),
            pltpu.VMEM((TENSOR, 2, 2, 32, ROWS), BF),
            pltpu.VMEM((NBLK, 32, ROWS), BF),
            pltpu.VMEM((NBLK, 32, ROWS), BF),
            pltpu.VMEM((2, QUART, ROWS), BF),
            pltpu.VMEM((2, QUART, BLOCK), BF),
            pltpu.VMEM((2, Z, QUADS, 32, ROWS), BF),
            pltpu.VMEM((2, ROWS, BLOCK), BF),
            pltpu.VMEM((2, NB, HALF, ROWS), BF),
            pltpu.VMEM((2, NB, HALF, ROWS), BF),
            pltpu.VMEM((NB, ROWS + TAPS, ROWS), F32),
            pltpu.VMEM(sq, F32),
            pltpu.VMEM(sq, BF),
            pltpu.VMEM((NB, ROWS + TAPS, ROWS), F32),
            pltpu.VMEM((NB, NB, ROWS, BLOCK), BF),
            pltpu.VMEM((NB, ROWS, QUADS * ROWS), BF),
            pltpu.VMEM((NB, QUADS * ROWS, QUART), BF),
            pltpu.VMEM((NBLK, ROWS, QUART), F32),
            pltpu.VMEM((ROWS, QUART), BF),
            pltpu.VMEM((NBLK, ROWS, QUART), BF),
            pltpu.VMEM((Z, ROWS, QUART), BF),
            pltpu.VMEM((Z, ROWS, QUART), BF),
            pltpu.VMEM((2, QUADS, ROWS, QUART), BF),
            pltpu.VMEM((2, TENSOR, ROWS, QUART), BF),
            pltpu.VMEM((2, NB, HALF, ROWS), F32),
            pltpu.VMEM((NB, HALF, ROWS), F32),
            pltpu.VMEM((NB, HALF, ROWS), F32),
            pltpu.VMEM((NB, HALF, ROWS), F32),
            pltpu.VMEM((NB, HALF, ROWS), F32),
            pltpu.VMEM((Z, NB, HALF, ROWS), F32),
            pltpu.VMEM((2, NB, HALF, ROWS), F32),
            dma, dma, dma, dma,
            dma((2,)), dma((2,)),
            dma((8,)), dma((8,)),
            dma((9,)), dma((2, 8)),
            dma((9,)), dma((2, 8)),
            dma((2, 8)), dma((2, 8)),
            dma((2, 4)), dma((2, 4)),
            dma((2,)), dma((2,)),
            dma((1,)), dma((1,)),
            dma((2, 4)), dma((2, 4)),
            dma((7,)), dma((7,)),
            dma,
            dma((9,)), dma((8,)),
            dma((1,)), dma((8,)),
            dma((2, 3)), dma((2, 3)),
            dma((2, 8)), dma((2, 8)),
            dma((16,)), dma((9,)),
            dma((9,)), dma((9,)),
            dma((9, 2)), dma((9, 2)),
            dma((2,)), dma((2,)),
            dma((10,)), dma((10,)),
        ],
        compiler_params=pltpu.CompilerParams(
            collective_id=0, has_side_effects=True, vmem_limit_bytes=60 * 2**20
        ),
    )(
        home, glu_input.transpose(0, 2, 1, 3), out_weight.transpose(0, 2, 1, 3), out_cotangent.transpose(1, 0, 2),
        root_stack, conv_kernel.transpose(1, 0, 2), norm_gain, norm_shift,
    )
    update, kernel_grad, glu_grad = pl.pallas_call(
        hand_over,
        out_shape=[jax.ShapeDtypeStruct(x.shape, x.dtype) for x in out],
        in_specs=[hbm] * 3,
        out_specs=[hbm] * 3,
        scratch_shapes=[pltpu.VMEM(x.shape, x.dtype) for x in out]
        + [dma((NBLK + 2,)), dma((NBLK + 2,))],
        compiler_params=pltpu.CompilerParams(vmem_limit_bytes=60 * 2**20),
    )(*out)
    return glu_grad.transpose(0, 2, 1, 3), kernel_grad.transpose(1, 0, 2), update.transpose(0, 2, 1, 3)


def solution(mesh):
    placed = (
        P("dp", None, None, "tensor"),
        P(None, None, "tensor"),
        P(None, "tensor"),
        P(None, "tensor"),
        P(None, "tensor", None, None),
        P("dp", None, None),
        P("tensor", None, "dp", None),
        P(),
    )
    return jax.shard_map(
        per_device,
        mesh=mesh,
        in_specs=placed,
        out_specs=(
            P("dp", None, None, "tensor"),
            P(None, None, "tensor"),
            P(None, "tensor", None, None),
        ),
        check_vma=False,
    )
```
